32 devices in a mesh: seq: 8 (over z, x), chan: 4 (over y, core).
Axes of the slice: x: 2, y: 2, z: 4, core: 2. Of those that a mesh axis runs over, the one named last changes fastest.
Arguments:
- tokens: bfloat16 [12288, 1024], P('seq', 'chan'), may hold values from -8 to 8
- doc_starts: int32 [12288], P('seq'), may hold values from 0 to 1, as said below
- cotangent: bfloat16 [12288, 1024], P('seq', 'chan'), may hold values from -8 to 8
- gains: float32 [2, 1024], P(None, 'chan'), may hold values from 0.4 to 3
- conv_kernel: float32 [3, 1024], P(None, 'chan'), may hold values from -3.5 to 3.5
- in_proj: float32 [1024, 3, 1024], P('seq', None, 'chan'), may hold values from -0.1875 to 0.1875
- gate_up: float32 [1024, 2, 4608], P('seq', None, 'chan'), may hold values from -0.1875 to 0.1875
- out_proj: float32 [1024, 1024], P('chan', 'seq'), may hold values from -0.1875 to 0.1875
- down_proj: float32 [4608, 1024], P('chan', 'seq'), may hold values from -0.09375 to 0.09375
- in_left: float32 [8, 3, 8, 128, 128], P('seq', None, 'chan'), as said below
- in_right: float32 [8, 3, 8, 128, 128], P('seq', None, 'chan'), as said below
- in_left_root: float32 [8, 3, 8, 128, 128], P('seq', None, 'chan'), as said below
- in_right_root: float32 [8, 3, 8, 128, 128], P('seq', None, 'chan'), as said below
- gate_left: float32 [8, 2, 36, 128, 128], P('seq', None, 'chan'), as said below
- gate_right: float32 [8, 2, 36, 128, 128], P('seq', None, 'chan'), as said below
- gate_left_root: float32 [8, 2, 36, 128, 128], P('seq', None, 'chan'), as said below
- gate_right_root: float32 [8, 2, 36, 128, 128], P('seq', None, 'chan'), as said below
- out_left: float32 [8, 8, 128, 128], P('chan', 'seq'), as said below
- out_right: float32 [8, 8, 128, 128], P('chan', 'seq'), as said below
- out_left_root: float32 [8, 8, 128, 128], P('chan', 'seq'), as said below
- out_right_root: float32 [8, 8, 128, 128], P('chan', 'seq'), as said below
- down_left: float32 [36, 8, 128, 128], P('chan', 'seq'), as said below
- down_right: float32 [36, 8, 128, 128], P('chan', 'seq'), as said below
- down_left_root: float32 [36, 8, 128, 128], P('chan', 'seq'), as said below
- down_right_root: float32 [36, 8, 128, 128], P('chan', 'seq'), as said below
- gain_first: float32 [2, 1024], P(None, 'chan'), may hold values from -112 to 112
- gain_second: float32 [2, 1024], P(None, 'chan'), may hold values from 1474.56 to 6144
- kernel_first: float32 [3, 1024], P(None, 'chan'), may hold values from -112 to 112
- kernel_second: float32 [3, 1024], P(None, 'chan'), may hold values from 1474.56 to 6144
Outputs:
- mixed: bfloat16 [12288, 1024], P('seq', 'chan')
- input_grad: float32 [12288, 1024], P('seq', 'chan')
- in_proj_grad: float32 [1024, 3, 1024], P('seq', None, 'chan')
- gate_up_grad: float32 [1024, 2, 4608], P('seq', None, 'chan')
- out_proj_grad: float32 [1024, 1024], P('chan', 'seq')
- down_proj_grad: float32 [4608, 1024], P('chan', 'seq')
- in_proj_new: float32 [1024, 3, 1024], P('seq', None, 'chan')
- gate_up_new: float32 [1024, 2, 4608], P('seq', None, 'chan')
- out_proj_new: float32 [1024, 1024], P('chan', 'seq')
- down_proj_new: float32 [4608, 1024], P('chan', 'seq')
- in_left_new: float32 [8, 3, 8, 128, 128], P('seq', None, 'chan')
- in_right_new: float32 [8, 3, 8, 128, 128], P('seq', None, 'chan')
- gate_left_new: float32 [8, 2, 36, 128, 128], P('seq', None, 'chan')
- gate_right_new: float32 [8, 2, 36, 128, 128], P('seq', None, 'chan')
- out_left_new: float32 [8, 8, 128, 128], P('chan', 'seq')
- out_right_new: float32 [8, 8, 128, 128], P('chan', 'seq')
- down_left_new: float32 [36, 8, 128, 128], P('chan', 'seq')
- down_right_new: float32 [36, 8, 128, 128], P('chan', 'seq')
- gain_first_new: float32 [2, 1024], P(None, 'chan')
- gain_second_new: float32 [2, 1024], P(None, 'chan')
- gains_new: float32 [2, 1024], P(None, 'chan')
- kernel_first_new: float32 [3, 1024], P(None, 'chan')
- kernel_second_new: float32 [3, 1024], P(None, 'chan')
- kernel_new: float32 [3, 1024], P(None, 'chan')
The draws below stay inside these ranges and needn't reach their ends.
Inputs may be any that keep to these rules, and one draw needn't show every extreme that they name: `doc_starts`: 1 marks the first token of a document; the first token is 1; a document begins at token 1535 and ends among the last 1536 tokens. `in_left`: each tile's matrix is symmetric. `in_right`: each tile's matrix is symmetric. `in_left_root`: each tile's matrix is symmetric. `in_right_root`: each tile's matrix is symmetric. `gate_left`: each tile's matrix is symmetric. `gate_right`: each tile's matrix is symmetric. `gate_left_root`: each tile's matrix is symmetric. `gate_right_root`: each tile's matrix is symmetric. `out_left`: each tile's matrix is symmetric. `out_right`: each tile's matrix is symmetric. `out_left_root`: each tile's matrix is symmetric. `out_right_root`: each tile's matrix is symmetric. `down_left`: each tile's matrix is symmetric. `down_right`: each tile's matrix is symmetric. `down_left_root`: each tile's matrix is symmetric. `down_right_root`: each tile's matrix is symmetric.
All inputs are finite; a program needn't handle non-finite values.
Results may differ from the reference program's by a relative error of at most 0.012.
The reference program's roundings to bfloat16 on the way count: a program that leaves them out, or rounds other values in their place, can miss the bound.
Values may be sent and summed in bfloat16 or wider, within the bound.
No kernel may reach another device: no remote copies, remote signals or barrier semaphores. Data moves between devices by JAX's collectives and lax.ppermute only.
A program may use at most 192 MiB of HBM per device.

```python
import math
import jax
import jax.numpy as jnp
from jax import lax

D = 1024
FF = 4608
TOK_DEV = 1536
TILE = 128
STEP = 10
TOKENS = 12288
ROWS_OWN = 128
D_TILES = 8
F_TILES = 36
N_SEQ = 8


def square_field(key, leading, extent, magnitude, spread, lowest, highest):
    key_diag, key_rest = jax.random.split(key)
    diagonal = jax.random.uniform(key_diag, leading + (extent,), jnp.float32, lowest, highest) * magnitude
    jitter = jax.random.normal(key_rest, leading + (extent, extent), jnp.float32) * (magnitude * spread / math.sqrt(extent))
    mirror = (jitter + jnp.swapaxes(jitter, -1, -2)) * 0.5
    ident = jnp.eye(extent, dtype=jnp.float32)
    return mirror * (1.0 - ident) + ident * diagonal[..., None]


def draw_doc_starts(key, part):
    key = jax.random.fold_in(key, 11)
    key_close, key_rand = jax.random.split(key, 2)
    opening = TOK_DEV - 1
    closing = TOKENS - jax.random.randint(key_close, (), 1, TOK_DEV // 2 + 1)
    places = jnp.arange(TOKENS, dtype=jnp.int32)
    sparse = jax.random.randint(key_rand, (TOKENS,), 0, 16) == 0
    outside = (places < opening) | (places >= closing)
    start_marks = sparse & outside | (places == 0) | (places == opening) | (places == closing)
    return start_marks.astype(jnp.int32)


def draw_gains(key, part):
    key = jax.random.fold_in(key, 3)
    lowest, highest = (0.6, 1.8)
    rising = lowest + (highest - lowest) * jnp.arange(D, dtype=jnp.float32) / (D - 1)
    jitter = jax.random.uniform(key, (2, D), jnp.float32, 0.85, 1.15)
    return rising[None, :] * jitter


def draw_in_left(key, part):
    key = jax.random.fold_in(key, 21)
    return square_field(key, (N_SEQ, 3, D_TILES), ROWS_OWN, float(TILE * TOKENS), 0.7, 1.0, 4.0)


def draw_in_right(key, part):
    key = jax.random.fold_in(key, 22)
    return square_field(key, (N_SEQ, 3, D_TILES), TILE, float(ROWS_OWN * TOKENS), 0.7, 1.0, 4.0)


def draw_in_left_root(key, part):
    key = jax.random.fold_in(key, 23)
    return square_field(key, (N_SEQ, 3, D_TILES), ROWS_OWN, float(D * TOKENS) ** (-0.25), 0.7, 1.0, 2.0)


def draw_in_right_root(key, part):
    key = jax.random.fold_in(key, 24)
    return square_field(key, (N_SEQ, 3, D_TILES), TILE, float(D * TOKENS) ** (-0.25), 0.7, 1.0, 2.0)


def draw_gate_left(key, part):
    key = jax.random.fold_in(key, 31)
    return square_field(key, (N_SEQ, 2, F_TILES), ROWS_OWN, float(TILE * TOKENS), 0.7, 1.0, 4.0)


def draw_gate_right(key, part):
    key = jax.random.fold_in(key, 32)
    return square_field(key, (N_SEQ, 2, F_TILES), TILE, float(ROWS_OWN * TOKENS), 0.7, 1.0, 4.0)


def draw_gate_left_root(key, part):
    key = jax.random.fold_in(key, 33)
    return square_field(key, (N_SEQ, 2, F_TILES), ROWS_OWN, float(D * TOKENS) ** (-0.25), 0.7, 1.0, 2.0)


def draw_gate_right_root(key, part):
    key = jax.random.fold_in(key, 34)
    return square_field(key, (N_SEQ, 2, F_TILES), TILE, float(D * TOKENS) ** (-0.25), 0.7, 1.0, 2.0)


def draw_out_left(key, part):
    key = jax.random.fold_in(key, 41)
    return square_field(key, (D_TILES, N_SEQ), TILE, float(ROWS_OWN * TOKENS), 0.7, 1.0, 4.0)


def draw_out_right(key, part):
    key = jax.random.fold_in(key, 42)
    return square_field(key, (D_TILES, N_SEQ), ROWS_OWN, float(TILE * TOKENS), 0.7, 1.0, 4.0)


def draw_out_left_root(key, part):
    key = jax.random.fold_in(key, 43)
    return square_field(key, (D_TILES, N_SEQ), TILE, float(D * TOKENS) ** (-0.25), 0.7, 1.0, 2.0)


def draw_out_right_root(key, part):
    key = jax.random.fold_in(key, 44)
    return square_field(key, (D_TILES, N_SEQ), ROWS_OWN, float(D * TOKENS) ** (-0.25), 0.7, 1.0, 2.0)


def draw_down_left(key, part):
    key = jax.random.fold_in(key, 51)
    return square_field(key, (F_TILES, N_SEQ), TILE, float(ROWS_OWN * TOKENS), 0.7, 1.0, 4.0)


def draw_down_right(key, part):
    key = jax.random.fold_in(key, 52)
    return square_field(key, (F_TILES, N_SEQ), ROWS_OWN, float(TILE * TOKENS), 0.7, 1.0, 4.0)


def draw_down_left_root(key, part):
    key = jax.random.fold_in(key, 53)
    return square_field(key, (F_TILES, N_SEQ), TILE, float(FF * TOKENS) ** (-0.25), 0.7, 1.0, 2.0)


def draw_down_right_root(key, part):
    key = jax.random.fold_in(key, 54)
    return square_field(key, (F_TILES, N_SEQ), ROWS_OWN, float(FF * TOKENS) ** (-0.25), 0.7, 1.0, 2.0)


def raised(result, rng, source, target, blocks, factor):
    def block_of(dim):
        return (jnp.arange(result.shape[dim]) // (result.shape[dim] // blocks)).reshape((-1,) + (1,) * (result.ndim - 1 - dim))

    first = jax.random.permutation(rng, blocks)[block_of(target)]
    other_side = (block_of(target) + blocks // 2) % blocks
    return jnp.where((block_of(source) == first) | (block_of(source) == other_side), factor * result, result)


def steps_of(own_key, dims, pieces, least, high):
    def one(position, parts):
        heights = jax.random.uniform(jax.random.fold_in(jax.random.fold_in(own_key, 6), position), (parts,), jnp.float32, least / len(pieces), high / len(pieces))
        return jnp.repeat(jnp.exp(heights), dims[position] // parts).reshape((-1,) + (1,) * (len(dims) - position - 1))

    level = one(*pieces[0])
    for cut in pieces[1:]:
        level = level * one(*cut)
    return level


def centred(key, shape, deviation, most, cuts=(), kind=jnp.bfloat16):
    values = jax.random.normal(key, shape, jnp.float32) * deviation
    if len(cuts) > 0:
        values = steps_of(key, shape, cuts, -0.22, 0.18) * values
    return jnp.clip(values, min=-most, max=most).astype(kind)


def bell_draw_with(stream_key, dims, width, reach, shards, heavy, kind=jnp.bfloat16):
    result = width * jax.random.normal(stream_key, dims, jnp.float32)
    if shards:
        result = result * steps_of(stream_key, dims, shards, -0.22, 0.18)
    return jnp.clip(raised(result, jax.random.fold_in(stream_key, 3), *heavy), -reach, reach).astype(kind)


def setup_inputs(seed: int = 0) -> dict:
    key_of = jax.random.split(jax.random.key(seed), 30)
    return {
        "tokens": bell_draw_with(key_of[0], (TOKENS, D), 1.0, 8.0, ((0, 8), (1, 4)), (0, 1, 8, 2.0)),
        "doc_starts": draw_doc_starts(jax.random.fold_in(key_of[29], 71), 0),
        "cotangent": bell_draw_with(key_of[2], (TOKENS, D), 1.0, 8.0, ((0, 8), (1, 4)), (0, 1, 8, 2.0)),
        "gains": draw_gains(jax.random.fold_in(key_of[29], 71), 0),
        "conv_kernel": centred(key_of[4], (3, D), 0.6, 3.5, ((1, 4),), jnp.float32),
        "in_proj": centred(key_of[5], (D, 3, D), D ** -0.5, 0.1875, ((0, 8), (2, 4)), jnp.float32),
        "gate_up": centred(key_of[6], (D, 2, FF), D ** -0.5, 0.1875, ((0, 8), (2, 4)), jnp.float32),
        "out_proj": centred(key_of[7], (D, D), D ** -0.5, 0.1875, ((0, 4), (1, 8)), jnp.float32),
        "down_proj": centred(key_of[8], (FF, D), FF ** -0.5, 0.09375, ((0, 4), (1, 8)), jnp.float32),
        "in_left": draw_in_left(jax.random.fold_in(key_of[29], 71), 0),
        "in_right": draw_in_right(jax.random.fold_in(key_of[29], 71), 0),
        "in_left_root": draw_in_left_root(jax.random.fold_in(key_of[29], 71), 0),
        "in_right_root": draw_in_right_root(jax.random.fold_in(key_of[29], 71), 0),
        "gate_left": draw_gate_left(jax.random.fold_in(key_of[29], 71), 0),
        "gate_right": draw_gate_right(jax.random.fold_in(key_of[29], 71), 0),
        "gate_left_root": draw_gate_left_root(jax.random.fold_in(key_of[29], 71), 0),
        "gate_right_root": draw_gate_right_root(jax.random.fold_in(key_of[29], 71), 0),
        "out_left": draw_out_left(jax.random.fold_in(key_of[29], 71), 0),
        "out_right": draw_out_right(jax.random.fold_in(key_of[29], 71), 0),
        "out_left_root": draw_out_left_root(jax.random.fold_in(key_of[29], 71), 0),
        "out_right_root": draw_out_right_root(jax.random.fold_in(key_of[29], 71), 0),
        "down_left": draw_down_left(jax.random.fold_in(key_of[29], 71), 0),
        "down_right": draw_down_right(jax.random.fold_in(key_of[29], 71), 0),
        "down_left_root": draw_down_left_root(jax.random.fold_in(key_of[29], 71), 0),
        "down_right_root": draw_down_right_root(jax.random.fold_in(key_of[29], 71), 0),
        "gain_first": centred(key_of[25], (2, D), (0.17 * TOKENS ** 0.5), 112.0, ((1, 4),), jnp.float32),
        "gain_second": jnp.clip(jnp.exp(math.log(6144.0) - 1.4271163 * jax.random.uniform(key_of[26], (2, D), jnp.float32) ** steps_of(key_of[26], (2, D), ((1, 4),), -0.2, 0.2)), 1474.56, 6144.0),
        "kernel_first": centred(key_of[27], (3, D), (0.17 * TOKENS ** 0.5), 112.0, ((1, 4),), jnp.float32),
        "kernel_second": jnp.clip(jnp.exp(math.log(6144.0) - 1.4271163 * jax.random.uniform(key_of[28], (3, D), jnp.float32) ** steps_of(key_of[28], (3, D), ((1, 4),), -0.2, 0.2)), 1474.56, 6144.0),
    }


@jax.custom_vjp
def low(v):
    return lax.optimization_barrier(v.astype(jnp.bfloat16)).astype(jnp.float32)

@jax.custom_vjp
def low_back(v):
    return v

def low_keep(v):
    return (low(v), None)

def low_pass(kept, grad):
    return (grad,)

def back_keep(v):
    return (v, None)

def back_low(kept, grad):
    return (low(grad),)
low.defvjp(low_keep, low_pass)
low_back.defvjp(back_keep, back_low)
EPS = 1e-05
DECAY = 0.5
MATRIX_RATE = 0.5
VECTOR_RATE = 1.0
BETA_ONE = 0.9
BETA_TWO = 0.95
ADAM_EPS = 1e-08
WEIGHT_DECAY = 0.01
HIGH = lax.Precision.HIGHEST

def rms_gain(values, gain_row):
    inverse = lax.rsqrt(lax.optimization_barrier(jnp.mean(values * values, axis=-1, keepdims=True)) + EPS)
    return values * inverse * gain_row

def keep_masks(starts):
    keep_one = 1.0 - starts
    before = jnp.concatenate([jnp.zeros((1,), jnp.float32), starts[:-1]])
    return (keep_one, keep_one * (1.0 - before))

def conv_taps(padded, kernel, keep_one, keep_two):
    return kernel[2] * padded[2:] + kernel[1] * keep_one[:, None] * padded[1:-1] + kernel[0] * keep_two[:, None] * padded[:-2]

def forward(starts, tokens, gains, kernel, in_proj, gate_up, out_proj, down_proj):
    normed_one = low(rms_gain(tokens, gains[0]))
    projected = low_back(jnp.einsum('td,dkc->tkc', normed_one, low(in_proj), precision=HIGH))
    product_bx = low_back(low(projected[:, 0] * projected[:, 2]))
    padded = jnp.concatenate([jnp.zeros((2, product_bx.shape[1]), jnp.float32), product_bx], axis=0)
    keep_one, keep_two = keep_masks(starts)
    filtered = conv_taps(padded, kernel, keep_one, keep_two)
    gated = low(projected[:, 1] * filtered)
    residual = tokens + low_back(jnp.dot(gated, low(out_proj), precision=HIGH))
    normed_two = low(rms_gain(residual, gains[1]))
    hidden = low_back(jnp.einsum('td,dkf->tkf', normed_two, low(gate_up), precision=HIGH))
    activated = low(jax.nn.silu(hidden[:, 0]) * hidden[:, 1])
    return residual + jnp.dot(activated, low(down_proj), precision=HIGH)

def column_update(weight, gradient, left_stat, right_stat, left_root, right_root):
    blocks = gradient.reshape(left_stat.shape[0], left_stat.shape[3], left_stat.shape[1], left_stat.shape[2], right_stat.shape[3])
    new_left = DECAY * left_stat + (1.0 - DECAY) * jnp.einsum('nrabc,nsabc->nabrs', blocks, blocks, precision=HIGH)
    new_right = DECAY * right_stat + (1.0 - DECAY) * jnp.einsum('nrabc,nrabe->nabce', blocks, blocks, precision=HIGH)
    half_step = jnp.einsum('nabrs,nsabc->nrabc', left_root, blocks, precision=HIGH)
    update = jnp.einsum('nrabc,nabce->nrabe', half_step, right_root, precision=HIGH)
    return (weight - MATRIX_RATE * update.reshape(weight.shape), new_left, new_right)

def row_update(weight, gradient, left_stat, right_stat, left_root, right_root):
    blocks = gradient.reshape(left_stat.shape[0], left_stat.shape[2], left_stat.shape[1], right_stat.shape[3])
    new_left = DECAY * left_stat + (1.0 - DECAY) * jnp.einsum('bcnr,benr->bnce', blocks, blocks, precision=HIGH)
    new_right = DECAY * right_stat + (1.0 - DECAY) * jnp.einsum('bcnr,bcns->bnrs', blocks, blocks, precision=HIGH)
    half_step = jnp.einsum('bnce,benr->bcnr', left_root, blocks, precision=HIGH)
    update = jnp.einsum('bcnr,bnrs->bcns', half_step, right_root, precision=HIGH)
    return (weight - MATRIX_RATE * update.reshape(weight.shape), new_left, new_right)

def adam_step(values, gradient, moment_one, second):
    moment_one = BETA_ONE * moment_one + (1.0 - BETA_ONE) * gradient
    second = BETA_TWO * second + (1.0 - BETA_TWO) * gradient * gradient
    first_hat = moment_one / (1.0 - BETA_ONE ** STEP)
    second_hat = second / (1.0 - BETA_TWO ** STEP)
    new_values = values - VECTOR_RATE * (first_hat / (jnp.sqrt(second_hat) + ADAM_EPS) + WEIGHT_DECAY * values)
    return (moment_one, second, new_values)

def reference(tokens, doc_starts, cotangent, gains, conv_kernel, in_proj, gate_up, out_proj, down_proj, in_left, in_right, in_left_root, in_right_root, gate_left, gate_right, gate_left_root, gate_right_root, out_left, out_right, out_left_root, out_right_root, down_left, down_right, down_left_root, down_right_root, gain_first, gain_second, kernel_first, kernel_second):
    starts = doc_starts.astype(jnp.float32)

    def closed(inputs, gain_rows, kernel, first_mat, second_mat, third_mat, fourth_mat):
        return forward(starts, inputs, gain_rows, kernel, first_mat, second_mat, third_mat, fourth_mat)
    output, pullback = jax.vjp(closed, tokens.astype(jnp.float32), gains, conv_kernel, in_proj, gate_up, out_proj, down_proj)
    grads = pullback(cotangent.astype(jnp.float32))
    input_grad, gain_grad, kernel_grad, in_grad, gate_grad, out_grad, down_grad = grads
    in_new, in_left_new, in_right_new = column_update(in_proj, in_grad, in_left, in_right, in_left_root, in_right_root)
    gate_new, gate_left_new, gate_right_new = column_update(gate_up, gate_grad, gate_left, gate_right, gate_left_root, gate_right_root)
    out_new, out_left_new, out_right_new = row_update(out_proj, out_grad, out_left, out_right, out_left_root, out_right_root)
    down_new, down_left_new, down_right_new = row_update(down_proj, down_grad, down_left, down_right, down_left_root, down_right_root)
    gain_one, gain_two, gains_new = adam_step(gains, gain_grad, gain_first, gain_second)
    kernel_one, kernel_two, kernel_new = adam_step(conv_kernel, kernel_grad, kernel_first, kernel_second)
    return (output.astype(jnp.bfloat16), input_grad, in_grad, gate_grad, out_grad, down_grad, in_new, gate_new, out_new, down_new, in_left_new, in_right_new, gate_left_new, gate_right_new, out_left_new, out_right_new, down_left_new, down_right_new, gain_one, gain_two, gains_new, kernel_one, kernel_two, kernel_new)
```

```python
import jax
import jax.numpy as jnp
from jax import lax
from jax.experimental import pallas as pl
from jax.experimental.pallas import tpu as pltpu
from jax.sharding import PartitionSpec as P

D = 1024
STEP = 10


EPS = 1e-05
DECAY = 0.5
MATRIX_RATE = 0.5
VECTOR_RATE = 1.0
BETA_ONE = 0.9
BETA_TWO = 0.95
ADAM_EPS = 1e-08
WEIGHT_DECAY = 0.01
LOW = jnp.bfloat16
WIDE = jnp.float32
VMEM_BYTES = 56 * 1024 * 1024


def after(value, *earlier):
    return lax.optimization_barrier((value,) + earlier)[0]


def after_all(values, *earlier):
    return lax.optimization_barrier(tuple(values) + earlier)[: len(values)]


def from_behind(block, axis, distance):
    devices = range(lax.axis_size(axis))
    route = [(i - distance, i) for i in devices if i - distance in devices]
    return lax.ppermute(block, axis, route)


def swap(block, axis, bit):
    devices = range(lax.axis_size(axis))
    return lax.ppermute(block, axis, [(i, i ^ bit) for i in devices])


def all_sum(block, axis):
    bit = 1
    while bit < lax.axis_size(axis):
        block = block + swap(block, axis, bit)
        bit *= 2
    return block


def ring_order(count):
    return [2 * p if 2 * p < count else 2 * (count - p) - 1 for p in range(count)]


def ring_index(place, count):
    place = lax.rem(place + 2 * count, count)
    return jnp.where(2 * place < count, 2 * place, 2 * (count - place) - 1)


def ring_place(index, count):
    return jnp.where(lax.rem(index, 2) == 0, index // 2, count - 1 - index // 2)


def ring_send(block, step):
    order = ring_order(lax.axis_size("seq"))
    count = len(order)
    route = [(order[p], order[(p + step) % count]) for p in range(count)]
    return lax.ppermute(block, "seq", route)


def row_start(index, rows):
    quarter_rows = D // 4
    first = index * rows
    relative = (first // quarter_rows) ^ lax.axis_index("chan")
    place = (relative >> 1) | ((relative & 1) << 1)
    return place * quarter_rows + lax.rem(first, quarter_rows)


def copy_pieces(starts, pieces, whole, sems):
    copies = []
    for i, piece in enumerate(pieces):
        rows = pl.ds(pl.multiple_of(starts[i], 16), piece.shape[0])
        copies.append(pltpu.make_async_copy(piece, whole.at[rows], sems.at[i]))
    for copy in copies:
        copy.start()
    for copy in copies:
        copy.wait()


def place_kernel(starts, *refs):
    copy_pieces(starts, refs[:-2], refs[-2], refs[-1])


def placed_rows(pieces, starts):
    width = pieces[0].shape[1]
    count = len(pieces)
    total = sum(p.shape[0] for p in pieces)
    return pl.pallas_call(
        place_kernel,
        grid_spec=pltpu.PrefetchScalarGridSpec(
            num_scalar_prefetch=1,
            grid=(1,),
            in_specs=[pl.BlockSpec(memory_space=pl.ANY)] * count,
            out_specs=pl.BlockSpec((total, width), lambda i, starts: (0, 0)),
            scratch_shapes=[pltpu.SemaphoreType.DMA((count,))],
        ),
        out_shape=jax.ShapeDtypeStruct((total, width), pieces[0].dtype),
        compiler_params=pltpu.CompilerParams(vmem_limit_bytes=VMEM_BYTES),
        cost_estimate=pl.CostEstimate(
            flops=0, bytes_accessed=4 * total * width, transcendentals=0
        ),
    )(starts, *pieces)


def ring_gather(shard, *during):
    count = lax.axis_size("seq")
    place = ring_place(lax.axis_index("seq"), count)
    rows = shard.shape[0]
    pieces, starts = [], []

    def put(block, source, offset=0):
        pieces.append(block)
        starts.append(row_start(ring_index(source, count), rows) + offset)

    put(shard, place)
    ahead = behind = shard
    for step in range(1, count // 2):
        if step == 2:
            ahead, behind = after(ahead, *during), after(behind, *during)
        ahead = ring_send(ahead, 1)
        behind = ring_send(behind, -1)
        put(ahead, place - step)
        put(behind, place + step)
    half = rows // 2
    ahead = ring_send(ahead[:half], 1)
    behind = ring_send(behind[half:], -1)
    put(ahead, place - count // 2)
    put(behind, place - count // 2, half)
    return pieces, jnp.stack(starts).astype(jnp.int32)


def ring_total(partial, *later):
    count = lax.axis_size("seq")
    place = ring_place(lax.axis_index("seq"), count)
    rows = partial.shape[0] // count
    half = rows // 2
    far = count // 2

    def own(target, offset=0, extent=rows):
        start = row_start(ring_index(target, count), rows) + offset
        return lax.dynamic_slice(partial, (start, 0), (extent, partial.shape[1]))

    ahead = ring_send(own(place + far, 0, half), 1)
    behind = ring_send(own(place - far, half, half), -1)
    for step in range(far - 1, 0, -1):
        earlier = later if step == 1 else ()
        ahead, behind = lax.optimization_barrier((ahead, behind) + earlier)[:2]
        up, down = own(place + step).astype(WIDE), own(place - step).astype(WIDE)
        if step == far - 1:
            up = up + jnp.pad(ahead.astype(WIDE), ((0, rows - half), (0, 0)))
            down = down + jnp.pad(behind.astype(WIDE), ((half, 0), (0, 0)))
        else:
            up = up + ahead.astype(WIDE)
            down = down + behind.astype(WIDE)
        arrived = ahead, behind
        ahead = ring_send(up.astype(LOW), 1)
        behind = ring_send(down.astype(LOW), -1)
    return (own(place), ahead, behind), arrived


def spread(quarter, *earlier):
    across = swap(quarter, "chan", 2)
    pair = jnp.concatenate([quarter, after(across, *earlier)], axis=-1)
    return jnp.concatenate([pair, swap(pair, "chan", 1)], axis=-1), across


def far_sum(other, far):
    return (far + other[:, D // 4 :].astype(WIDE)).astype(LOW)


def near_sum(other, near, across):
    return near + other[:, : D // 4].astype(WIDE) + across.astype(WIDE)


def branch_parts(rows, matrix, *earlier):
    def product(low, high):
        return lax.dot_general(
            rows, matrix[low:high], (((1,), (1,)), ((), ())), preferred_element_type=WIDE
        )

    other = after(swap(product(D // 2, D).astype(LOW), "chan", 1), *earlier)
    sent = far_sum(other, product(D // 4, D // 2))
    return other, sent, product(0, D // 4)


def pair_kernel(rows, matrix, send_out, far_out, near_out):
    def back(low, high):
        return lax.dot_general(
            rows[...], matrix[low:high, :], (((1,), (1,)), ((), ())), preferred_element_type=WIDE
        )

    send_out[...] = back(D // 2, D).astype(LOW)
    keep = back(0, D // 2)
    near_out[...] = keep[:, : D // 4]
    far_out[...] = keep[:, D // 4 :]


def pair_parts(rows, matrix):
    tokens, depth = rows.shape
    block = 256

    def cut(extent):
        return pl.BlockSpec((block, extent), lambda i: (i, 0))

    return pl.pallas_call(
        pair_kernel,
        grid=(tokens // block,),
        in_specs=[cut(depth), pl.BlockSpec(matrix.shape, lambda i: (0, 0))],
        out_specs=[cut(D // 2), cut(D // 4), cut(D // 4)],
        out_shape=[
            jax.ShapeDtypeStruct((tokens, D // 2), LOW),
            jax.ShapeDtypeStruct((tokens, D // 4), WIDE),
            jax.ShapeDtypeStruct((tokens, D // 4), WIDE),
        ],
        compiler_params=pltpu.CompilerParams(vmem_limit_bytes=VMEM_BYTES),
        cost_estimate=pl.CostEstimate(
            flops=2 * tokens * D * depth,
            bytes_accessed=2 * matrix.size + 2 * rows.size + 6 * tokens * D // 2,
            transcendentals=0,
        ),
    )(rows, matrix)


def norm_back(grad_rows, hat_rows, inverse, gain_row, inner):
    scaled = grad_rows * gain_row[None, :]
    return (
        inverse[:, None] * (scaled - hat_rows * (inner / D)[:, None]),
        jnp.sum(grad_rows * hat_rows, axis=0),
    )


def keep_masks(starts):
    keep_one = 1.0 - starts
    before = jnp.concatenate([jnp.zeros((1,), jnp.float32), starts[:-1]])
    return (keep_one, keep_one * (1.0 - before))


def conv_taps(padded, kernel, keep_one, keep_two):
    return (
        kernel[2] * padded[2:]
        + kernel[1] * keep_one[:, None] * padded[1:-1]
        + kernel[0] * keep_two[:, None] * padded[:-2]
    )


def product(one, two, dims):
    return lax.dot_general(
        one.astype(LOW), two.astype(LOW), ((dims[:1], dims[1:]), ((), ())),
        preferred_element_type=WIDE,
    )


def summed(terms, *at):
    return terms[0][at].astype(WIDE) + terms[1][at].astype(WIDE) + terms[2][at].astype(WIDE)


def tile_update(g, left_stat, right_stat, left_root, right_root):
    low = g.astype(LOW)
    new_left = DECAY * left_stat + (1.0 - DECAY) * product(low, low, (1, 1))
    new_right = DECAY * right_stat + (1.0 - DECAY) * product(low, low, (0, 0))
    update = product(product(left_root, low, (1, 0)), right_root, (1, 0))
    return update, new_left, new_right


def column_kernel(kinds, tiles, by_kind, *refs):
    parts, rest = refs[: 3 * kinds], refs[3 * kinds :]
    weight, left, right, left_root, right_root = rest[:5]
    grad_out, weight_out, left_out, right_out = rest[5:]
    extent = right.shape[-1]
    for k in range(kinds):
        for i in range(tiles):
            columns = slice(i * extent, (i + 1) * extent)
            at = (k, slice(None), columns) if by_kind else (slice(None), k, columns)
            g = summed(parts[3 * k : 3 * k + 3], slice(None), columns)
            update, new_left, new_right = tile_update(
                g, left[0, k, i], right[0, k, i], left_root[0, k, i], right_root[0, k, i]
            )
            grad_out[at] = g
            weight_out[at] = weight[at] - MATRIX_RATE * update
            left_out[0, k, i] = new_left
            right_out[0, k, i] = new_right


def column_update(weight, terms, first_column, step_tiles, by_kind, *stats):
    kinds, width = stats[0].shape[1], weight.shape[2]
    rows, extent = terms[0].shape[0], stats[1].shape[-1]
    steps = width // extent // step_tiles
    step = step_tiles * extent
    begin = first_column // step

    def part(k):
        return [pl.BlockSpec((rows, step), lambda i: (0, begin + k * steps + i))] * 3

    shape = (kinds, rows, step) if by_kind else (rows, kinds, step)
    cut = pl.BlockSpec(shape, lambda i: (0, 0, i))
    stat_cuts = [
        pl.BlockSpec((1, kinds, step_tiles) + s.shape[-2:], lambda i: (0, 0, i, 0, 0))
        for s in stats
    ]
    return pl.pallas_call(
        lambda *refs: column_kernel(kinds, step_tiles, by_kind, *refs),
        grid=(steps,),
        in_specs=[spec for k in range(kinds) for spec in part(k)] + [cut] + stat_cuts,
        out_specs=[cut, cut] + stat_cuts[:2],
        out_shape=[jax.ShapeDtypeStruct(weight.shape, WIDE)] * 2
        + [jax.ShapeDtypeStruct(s.shape, WIDE) for s in stats[:2]],
        compiler_params=pltpu.CompilerParams(vmem_limit_bytes=VMEM_BYTES),
        cost_estimate=pl.CostEstimate(
            flops=8 * extent * weight.size, bytes_accessed=38 * weight.size, transcendentals=0
        ),
    )(*list(terms) * kinds, weight, *stats)


def row_kernel(tiles, *refs):
    terms, weight, left, right, left_root, right_root = refs[:3], *refs[3:8]
    grad_out, weight_out, left_out, right_out = refs[8:]
    extent = left.shape[-1]
    for i in range(tiles):
        rows = slice(i * extent, (i + 1) * extent)
        g = summed(terms, slice(None), rows).T
        update, new_left, new_right = tile_update(
            g, left[i, 0], right[i, 0], left_root[i, 0], right_root[i, 0]
        )
        grad_out[rows, :] = g
        weight_out[rows, :] = weight[rows, :] - MATRIX_RATE * update
        left_out[i, 0] = new_left
        right_out[i, 0] = new_right


def row_update(weight, terms, first_column, step_tiles, *stats):
    extent = stats[0].shape[-1]
    columns = weight.shape[1]
    step = step_tiles * extent
    begin = first_column // step
    cut = pl.BlockSpec((step, columns), lambda i: (i, 0))
    stat_cuts = [
        pl.BlockSpec((step_tiles, 1) + s.shape[-2:], lambda i: (i, 0, 0, 0)) for s in stats
    ]
    return pl.pallas_call(
        lambda *refs: row_kernel(step_tiles, *refs),
        grid=(weight.shape[0] // step,),
        in_specs=[pl.BlockSpec((columns, step), lambda i: (0, begin + i))] * 3
        + [cut]
        + stat_cuts,
        out_specs=[cut, cut] + stat_cuts[:2],
        out_shape=[jax.ShapeDtypeStruct(weight.shape, WIDE)] * 2
        + [jax.ShapeDtypeStruct(s.shape, WIDE) for s in stats[:2]],
        compiler_params=pltpu.CompilerParams(vmem_limit_bytes=VMEM_BYTES),
        cost_estimate=pl.CostEstimate(
            flops=8 * extent * weight.size, bytes_accessed=38 * weight.size, transcendentals=0
        ),
    )(*terms, weight, *stats)


def shard_kernel(by_kind, column, row, out):
    kinds, width = column.shape[0 if by_kind else 1], column.shape[2]
    for k in range(kinds):
        block = column[k] if by_kind else column[:, k, :]
        out[:, k * width : (k + 1) * width] = block.astype(LOW)
    out[:, kinds * width :] = row[...].T.astype(LOW)


def low_shard(column, row, by_kind):
    rows, size = row.shape[1], column.size + row.size
    return pl.pallas_call(
        lambda *refs: shard_kernel(by_kind, *refs),
        out_shape=jax.ShapeDtypeStruct((rows, size // rows), LOW),
        compiler_params=pltpu.CompilerParams(vmem_limit_bytes=VMEM_BYTES),
        cost_estimate=pl.CostEstimate(flops=0, bytes_accessed=6 * size, transcendentals=0),
    )(column, row)


def ffn_kernel(units, starts, features, cotangents, *refs):
    act_out, grad_out, send_out, far_out, near_out, inner_out, down_out = refs[-10:-3]
    matrix, sems, sem = refs[-3:]

    def down_copy():
        return pltpu.make_async_copy(matrix.at[:, pl.ds(2 * units, units)], down_out, sem)

    @pl.when(pl.program_id(0) == 0)
    def _():
        copy_pieces(starts, refs[:-10], matrix, sems)
        down_copy().start()

    normed, cot = features[...], cotangents[...]
    inner = jnp.zeros((normed.shape[0], 1), WIDE)
    for low in range(0, units, 256):
        high = min(low + 256, units)
        gate = jnp.dot(normed, matrix[:, low:high], preferred_element_type=WIDE)
        up = jnp.dot(normed, matrix[:, units + low : units + high], preferred_element_type=WIDE)
        grad = jnp.dot(
            cot, matrix[:, 2 * units + low : 2 * units + high], preferred_element_type=WIDE
        )
        sigmoid = jax.nn.sigmoid(gate)
        silu = gate * sigmoid
        act_out[:, low:high] = (silu * up).astype(LOW)
        grad_gate = (grad * up * sigmoid * (1.0 + gate * (1.0 - sigmoid))).astype(LOW)
        grad_up = (grad * silu).astype(LOW)
        grad_out[:, low:high] = grad_gate
        grad_out[:, units + low : units + high] = grad_up
        terms = grad_gate.astype(WIDE) * gate + grad_up.astype(WIDE) * up
        inner += jnp.sum(terms, axis=1, keepdims=True)
    inner_out[...] = jnp.broadcast_to(inner, (inner.shape[0], 128)).T[:8]
    grads = grad_out[...]

    def back(low, high):
        return lax.dot_general(
            grads, matrix[low:high, : 2 * units], (((1,), (1,)), ((), ())),
            preferred_element_type=WIDE,
        )

    send_out[...] = back(D // 2, D).astype(LOW)
    keep = back(0, D // 2)
    near_out[...] = keep[:, : D // 4]
    far_out[...] = keep[:, D // 4 :]

    @pl.when(pl.program_id(0) == pl.num_programs(0) - 1)
    def _():
        down_copy().wait()


def ffn(features, cotangents, pieces, starts):
    tokens, units, count = features.shape[0], pieces[0].shape[1] // 3, len(pieces)
    block = 256

    def cut(extent):
        return pl.BlockSpec((block, extent), lambda i, starts: (i, 0))

    whole = pl.BlockSpec(memory_space=pl.ANY)
    return pl.pallas_call(
        lambda *refs: ffn_kernel(units, *refs),
        grid_spec=pltpu.PrefetchScalarGridSpec(
            num_scalar_prefetch=1,
            grid=(tokens // block,),
            in_specs=[cut(D), cut(D)] + [whole] * count,
            out_specs=[cut(units), cut(2 * units), cut(D // 2), cut(D // 4), cut(D // 4),
                pl.BlockSpec((8, block), lambda i, starts: (0, i)), whole],
            scratch_shapes=[
                pltpu.VMEM((D, 3 * units), LOW),
                pltpu.SemaphoreType.DMA((count,)),
                pltpu.SemaphoreType.DMA,
            ],
        ),
        out_shape=[
            jax.ShapeDtypeStruct((tokens, units), LOW),
            jax.ShapeDtypeStruct((tokens, 2 * units), LOW),
            jax.ShapeDtypeStruct((tokens, D // 2), LOW),
            jax.ShapeDtypeStruct((tokens, D // 4), WIDE),
            jax.ShapeDtypeStruct((tokens, D // 4), WIDE),
            jax.ShapeDtypeStruct((8, tokens), WIDE),
            jax.ShapeDtypeStruct((D, units), LOW),
        ],
        compiler_params=pltpu.CompilerParams(vmem_limit_bytes=VMEM_BYTES),
        cost_estimate=pl.CostEstimate(
            flops=10 * tokens * D * units,
            bytes_accessed=6 * D * units + 16 * tokens * D,
            transcendentals=tokens * units,
        ),
    )(starts, features, cotangents, *pieces)


def parts_kernel(split, features, cotangents, grads, activated, out):
    def product(left, right):
        out[...] = lax.dot_general(
            left[...], right[...], (((0,), (0,)), ((), ())), preferred_element_type=WIDE
        ).astype(LOW)

    @pl.when(pl.program_id(0) < split)
    def _():
        product(features, grads)

    @pl.when(pl.program_id(0) == split)
    def _():
        product(cotangents, activated)


def gradient_parts(features, cotangents, grads, activated):
    tokens, units = activated.shape
    split = grads.shape[1] // units
    block, steps = 512, D // 512
    last = steps - 1
    return pl.pallas_call(
        lambda *refs: parts_kernel(split, *refs),
        grid=(split + 1, steps),
        in_specs=[
            pl.BlockSpec((tokens, block), lambda j, i: (0, jnp.where(j < split, i, last))),
            pl.BlockSpec((tokens, block), lambda j, i: (0, jnp.where(j < split, 0, i))),
            pl.BlockSpec((tokens, units), lambda j, i: (0, jnp.minimum(j, split - 1))),
            pl.BlockSpec((tokens, units), lambda j, i: (0, 0)),
        ],
        out_specs=pl.BlockSpec((block, units), lambda j, i: (i, j)),
        out_shape=jax.ShapeDtypeStruct((D, (split + 1) * units), LOW),
        compiler_params=pltpu.CompilerParams(vmem_limit_bytes=VMEM_BYTES),
        cost_estimate=pl.CostEstimate(
            flops=2 * tokens * D * (split + 1) * units,
            bytes_accessed=4 * tokens * D,
            transcendentals=0,
        ),
    )(features, cotangents, grads, activated)


def adam_step(values, gradient, moment_one, second):
    moment_one = BETA_ONE * moment_one + (1.0 - BETA_ONE) * gradient
    second = BETA_TWO * second + (1.0 - BETA_TWO) * gradient * gradient
    first_hat = moment_one / (1.0 - BETA_ONE**STEP)
    second_hat = second / (1.0 - BETA_TWO**STEP)
    new_values = values - VECTOR_RATE * (
        first_hat / (jnp.sqrt(second_hat) + ADAM_EPS) + WEIGHT_DECAY * values
    )
    return (moment_one, second, new_values)


def dot(one, two, dims):
    return lax.dot_general(
        one, two, ((dims[:1], dims[1:]), ((), ())), preferred_element_type=WIDE
    )


def body(
    tokens,
    doc_starts,
    cotangent,
    gains,
    conv_kernel,
    in_proj,
    gate_up,
    out_proj,
    down_proj,
    in_left,
    in_right,
    in_left_root,
    in_right_root,
    gate_left,
    gate_right,
    gate_left_root,
    gate_right_root,
    out_left,
    out_right,
    out_left_root,
    out_right_root,
    down_left,
    down_right,
    down_left_root,
    down_right_root,
    gain_first,
    gain_second,
    kernel_first,
    kernel_second,
):
    chan_in = in_proj.shape[2]
    units = gate_up.shape[2]

    in_kinds = in_proj.transpose(1, 0, 2)
    second_shard = low_shard(gate_up, down_proj, False)
    first_pieces, first_starts = ring_gather(low_shard(in_kinds, out_proj, True), second_shard)
    tokens_full, tokens_across = spread(tokens, *first_pieces[3:5])
    gain_full, _ = spread(gains[:1])
    cot_full, cot_across = spread(after(cotangent, tokens_across), *first_pieces[-2:])
    pieces, starts_two = ring_gather(after(second_shard, *first_pieces[-4:-2]))
    first_full = placed_rows(first_pieces, first_starts)
    in_full, out_full = first_full[:, : 3 * chan_in], first_full[:, 3 * chan_in :]

    wide_full = tokens_full.astype(WIDE)
    inv_one = lax.rsqrt(jnp.sum(wide_full * wide_full, axis=1) / D + EPS)
    spread_one = (wide_full * inv_one[:, None] * gain_full).astype(LOW)
    resid_in = tokens.astype(WIDE)
    hat_one = resid_in * inv_one[:, None]
    projected = dot(spread_one, in_full, (1, 0))
    in_gate = projected[:, :chan_in]
    out_gate = projected[:, chan_in : 2 * chan_in]
    conv_input = projected[:, 2 * chan_in :]
    bx_low = (in_gate * conv_input).astype(LOW)
    starts = doc_starts.astype(WIDE)
    tail_keep = 1.0 - starts[-1]
    edge_rows = jnp.concatenate([bx_low[-2:-1] * tail_keep.astype(LOW), bx_low[-1:]], axis=0)
    carried = after(from_behind(edge_rows, "seq", 1), cot_across, *pieces[1:3])
    padded = jnp.concatenate([carried, bx_low], axis=0).astype(WIDE)
    keep_one, keep_two = keep_masks(starts)
    filtered = conv_taps(padded, conv_kernel, keep_one, keep_two)
    gated_low = (out_gate * filtered).astype(LOW)
    other, sent, near = branch_parts(gated_low, out_full)
    across = after(swap(sent, "chan", 2), *pieces[3:5])
    residual = resid_in + near_sum(other, near, across)

    squares = all_sum(jnp.sum(residual * residual, axis=1), "chan")
    inv_two = lax.rsqrt(squares / D + EPS)
    hat_two = residual * inv_two[:, None]
    normed_two = (hat_two * gains[1][None, :]).astype(LOW)
    spread_two, _ = spread(normed_two, *pieces[5:7])
    activated, grad_hidden, two_send, two_far, two_near, inner_two, down_full = ffn(
        spread_two, cot_full, pieces, starts_two
    )
    other = swap(two_send, "chan", 1)
    sent_two = sent = far_sum(other, two_far)
    inner_two = all_sum(inner_two[0], "chan")
    second_part = gradient_parts(spread_two, cot_full, after(grad_hidden, sent), activated)
    across = after(swap(sent, "chan", 2), second_part, inner_two)
    grad_norm_two = near_sum(other, two_near, across)
    resid_norm, gain_two = norm_back(grad_norm_two, hat_two, inv_two, gains[1], inner_two)
    grad_resid = cotangent.astype(WIDE) + resid_norm
    mixed_send, mixed_far, mixed_near = pair_parts(after(activated, grad_resid), down_full)
    resid_full, resid_across = spread(grad_resid.astype(LOW), mixed_send)
    grad_gated = dot(resid_full, out_full, (1, 0))
    grad_conv = grad_gated * out_gate
    grad_cpart = grad_gated * filtered
    tap_one = keep_one[:, None] * grad_conv
    tap_two = keep_two[:, None] * grad_conv
    grad_padded = (
        jnp.pad(conv_kernel[2][None, :] * grad_conv, ((2, 0), (0, 0)))
        + jnp.pad(conv_kernel[1][None, :] * tap_one, ((1, 1), (0, 0)))
        + jnp.pad(conv_kernel[0][None, :] * tap_two, ((0, 2), (0, 0)))
    )
    out_part = dot(resid_full, gated_low, (0, 0)).astype(LOW)
    returned = after(from_behind(grad_padded[:2], "seq", -1), out_part)
    edge_back = jnp.concatenate([returned[0:1] * tail_keep, returned[1:2]], axis=0)
    grad_bx = grad_padded[2:] + jnp.pad(edge_back, ((grad_conv.shape[0] - 2, 0), (0, 0)))
    grad_bx = lax.optimization_barrier(grad_bx.astype(LOW)).astype(WIDE)
    kernel_part = jnp.stack(
        [
            jnp.sum(tap_two * padded[:-2], axis=0),
            jnp.sum(tap_one * padded[1:-1], axis=0),
            jnp.sum(grad_conv * padded[2:], axis=0),
        ]
    )
    grad_proj = jnp.concatenate(
        [
            (grad_bx * conv_input).astype(LOW),
            grad_cpart.astype(LOW),
            (grad_bx * in_gate).astype(LOW),
        ],
        axis=1,
    )
    second_terms, arrived = ring_total(second_part, kernel_part)
    other, last_sent, near = branch_parts(grad_proj, in_full, *arrived)
    grad_norm_one = near_sum(other, near, swap(last_sent, "chan", 2))
    other = swap(after(mixed_send, last_sent), "chan", 1)
    sent = after(far_sum(other, mixed_far), grad_norm_one)
    mixed = (residual + near_sum(other, mixed_near, swap(sent, "chan", 2))).astype(LOW)
    inner_one = all_sum(jnp.sum(grad_proj.astype(WIDE) * projected, axis=1), "chan")
    input_norm, gain_one = norm_back(grad_norm_one, hat_one, inv_one, gains[0], inner_one)
    input_grad = grad_resid + input_norm

    in_part = dot(spread_one, grad_proj, (0, 0)).astype(LOW)
    first_part = after(jnp.concatenate([in_part, out_part], axis=1), last_sent)
    first_terms, _ = ring_total(first_part)
    second_terms = after_all(second_terms, last_sent)
    vector_grad = all_sum(
        jnp.concatenate([gain_one[None], gain_two[None], kernel_part], axis=0), "seq"
    )
    gain_grad, kernel_grad = vector_grad[:2], vector_grad[2:]

    in_grad, in_new, in_left_new, in_right_new = column_update(
        in_kinds, first_terms, 0, 2, True, in_left, in_right, in_left_root, in_right_root
    )
    in_grad, in_new = in_grad.transpose(1, 0, 2), in_new.transpose(1, 0, 2)
    gate_grad, gate_new, gate_left_new, gate_right_new = column_update(
        gate_up, second_terms, 0, 3, False, gate_left, gate_right, gate_left_root, gate_right_root
    )
    out_grad, out_new, out_left_new, out_right_new = row_update(
        out_proj, first_terms, 3 * chan_in, 2, out_left, out_right, out_left_root, out_right_root
    )
    down_grad, down_new, down_left_new, down_right_new = row_update(
        down_proj, second_terms, 2 * units, 3, down_left, down_right, down_left_root,
        down_right_root,
    )
    gain_one_new, gain_two_new, gains_new = adam_step(gains, gain_grad, gain_first, gain_second)
    kernel_one_new, kernel_two_new, kernel_new = adam_step(
        conv_kernel, kernel_grad, kernel_first, kernel_second
    )
    return (
        mixed,
        input_grad,
        in_grad,
        gate_grad,
        out_grad,
        down_grad,
        in_new,
        gate_new,
        out_new,
        down_new,
        in_left_new,
        in_right_new,
        gate_left_new,
        gate_right_new,
        out_left_new,
        out_right_new,
        down_left_new,
        down_right_new,
        gain_one_new,
        gain_two_new,
        gains_new,
        kernel_one_new,
        kernel_two_new,
        kernel_new,
    )


def solution(mesh):
    placed = (
        P("seq", "chan"),
        P("seq"),
        P("seq", "chan"),
        P(None, "chan"),
        P(None, "chan"),
        P("seq", None, "chan"),
        P("seq", None, "chan"),
        P("chan", "seq"),
        P("chan", "seq"),
        P("seq", None, "chan", None, None),
        P("seq", None, "chan", None, None),
        P("seq", None, "chan", None, None),
        P("seq", None, "chan", None, None),
        P("seq", None, "chan", None, None),
        P("seq", None, "chan", None, None),
        P("seq", None, "chan", None, None),
        P("seq", None, "chan", None, None),
        P("chan", "seq", None, None),
        P("chan", "seq", None, None),
        P("chan", "seq", None, None),
        P("chan", "seq", None, None),
        P("chan", "seq", None, None),
        P("chan", "seq", None, None),
        P("chan", "seq", None, None),
        P("chan", "seq", None, None),
        P(None, "chan"),
        P(None, "chan"),
        P(None, "chan"),
        P(None, "chan"),
    )
    return jax.shard_map(
        body,
        mesh=mesh,
        in_specs=placed,
        out_specs=(
            P("seq", "chan"),
            P("seq", "chan"),
            P("seq", None, "chan"),
            P("seq", None, "chan"),
            P("chan", "seq"),
            P("chan", "seq"),
            P("seq", None, "chan"),
            P("seq", None, "chan"),
            P("chan", "seq"),
            P("chan", "seq"),
            P("seq", None, "chan", None, None),
            P("seq", None, "chan", None, None),
            P("seq", None, "chan", None, None),
            P("seq", None, "chan", None, None),
            P("chan", "seq", None, None),
            P("chan", "seq", None, None),
            P("chan", "seq", None, None),
            P("chan", "seq", None, None),
            P(None, "chan"),
            P(None, "chan"),
            P(None, "chan"),
            P(None, "chan"),
            P(None, "chan"),
            P(None, "chan"),
        ),
        check_vma=False,
    )
```

```python
import jax
import jax.numpy as jnp
from jax import lax
from jax.experimental import pallas as pl
from jax.experimental.pallas import tpu as pltpu
from jax.sharding import PartitionSpec as P

D = 1024
STEP = 10


EPS = 1e-05
DECAY = 0.5
MATRIX_RATE = 0.5
VECTOR_RATE = 1.0
BETA_ONE = 0.9
BETA_TWO = 0.95
ADAM_EPS = 1e-08
WEIGHT_DECAY = 0.01
LOW = jnp.bfloat16
WIDE = jnp.float32
VMEM_BYTES = 56 * 1024 * 1024


def after(value, *earlier):
    return lax.optimization_barrier((value,) + earlier)[0]


def after_all(values, *earlier):
    return lax.optimization_barrier(tuple(values) + earlier)[: len(values)]


def from_behind(block, axis, distance):
    devices = range(lax.axis_size(axis))
    route = [(i - distance, i) for i in devices if i - distance in devices]
    return lax.ppermute(block, axis, route)


def swap(block, axis, bit):
    devices = range(lax.axis_size(axis))
    return lax.ppermute(block, axis, [(i, i ^ bit) for i in devices])


def all_sum(block, axis):
    bit = 1
    while bit < lax.axis_size(axis):
        block = block + swap(block, axis, bit)
        bit *= 2
    return block


def ring_order(count):
    return [2 * p if 2 * p < count else 2 * (count - p) - 1 for p in range(count)]


def ring_index(place, count):
    place = lax.rem(place + 2 * count, count)
    return jnp.where(2 * place < count, 2 * place, 2 * (count - place) - 1)


def ring_place(index, count):
    return jnp.where(lax.rem(index, 2) == 0, index // 2, count - 1 - index // 2)


def ring_send(block, step):
    order = ring_order(lax.axis_size("seq"))
    count = len(order)
    route = [(order[p], order[(p + step) % count]) for p in range(count)]
    return lax.ppermute(block, "seq", route)


def row_start(index, rows):
    quarter_rows = D // 4
    first = index * rows
    relative = (first // quarter_rows) ^ lax.axis_index("chan")
    place = (relative >> 1) | ((relative & 1) << 1)
    return place * quarter_rows + lax.rem(first, quarter_rows)


def copy_pieces(starts, pieces, whole, sems):
    copies = []
    for i, piece in enumerate(pieces):
        rows = pl.ds(pl.multiple_of(starts[i], 16), piece.shape[0])
        copies.append(pltpu.make_async_copy(piece, whole.at[rows], sems.at[i]))
    for copy in copies:
        copy.start()
    for copy in copies:
        copy.wait()


def place_kernel(starts, *refs):
    copy_pieces(starts, refs[:-2], refs[-2], refs[-1])


def placed_rows(pieces, starts):
    width = pieces[0].shape[1]
    count = len(pieces)
    total = sum(p.shape[0] for p in pieces)
    return pl.pallas_call(
        place_kernel,
        grid_spec=pltpu.PrefetchScalarGridSpec(
            num_scalar_prefetch=1,
            grid=(1,),
            in_specs=[pl.BlockSpec(memory_space=pl.ANY)] * count,
            out_specs=pl.BlockSpec((total, width), lambda i, starts: (0, 0)),
            scratch_shapes=[pltpu.SemaphoreType.DMA((count,))],
        ),
        out_shape=jax.ShapeDtypeStruct((total, width), pieces[0].dtype),
        compiler_params=pltpu.CompilerParams(vmem_limit_bytes=VMEM_BYTES),
        cost_estimate=pl.CostEstimate(
            flops=0, bytes_accessed=4 * total * width, transcendentals=0
        ),
    )(starts, *pieces)


def ring_gather(shard, *during):
    count = lax.axis_size("seq")
    place = ring_place(lax.axis_index("seq"), count)
    rows = shard.shape[0]
    pieces, starts = [], []

    def put(block, source, offset=0):
        pieces.append(block)
        starts.append(row_start(ring_index(source, count), rows) + offset)

    put(shard, place)
    ahead = behind = shard
    for step in range(1, count // 2):
        if step == 2:
            ahead, behind = after(ahead, *during), after(behind, *during)
        ahead = ring_send(ahead, 1)
        behind = ring_send(behind, -1)
        put(ahead, place - step)
        put(behind, place + step)
    half = rows // 2
    ahead = ring_send(ahead[:half], 1)
    behind = ring_send(behind[half:], -1)
    put(ahead, place - count // 2)
    put(behind, place - count // 2, half)
    return pieces, jnp.stack(starts).astype(jnp.int32)


def ring_total(partial, *later):
    count = lax.axis_size("seq")
    place = ring_place(lax.axis_index("seq"), count)
    rows = partial.shape[0] // count
    half = rows // 2
    far = count // 2

    def own(target, offset=0, extent=rows):
        start = row_start(ring_index(target, count), rows) + offset
        return lax.dynamic_slice(partial, (start, 0), (extent, partial.shape[1]))

    ahead = ring_send(own(place + far, 0, half), 1)
    behind = ring_send(own(place - far, half, half), -1)
    for step in range(far - 1, 0, -1):
        earlier = later if step == 1 else ()
        ahead, behind = lax.optimization_barrier((ahead, behind) + earlier)[:2]
        up, down = own(place + step).astype(WIDE), own(place - step).astype(WIDE)
        if step == far - 1:
            up = up + jnp.pad(ahead.astype(WIDE), ((0, rows - half), (0, 0)))
            down = down + jnp.pad(behind.astype(WIDE), ((half, 0), (0, 0)))
        else:
            up = up + ahead.astype(WIDE)
            down = down + behind.astype(WIDE)
        arrived = ahead, behind
        if step == 2:
            early = ahead, behind
        ahead = ring_send(up.astype(LOW), 1)
        behind = ring_send(down.astype(LOW), -1)
    return (own(place), ahead, behind), arrived, early


def spread(quarter, *earlier):
    across = swap(quarter, "chan", 2)
    pair = jnp.concatenate([quarter, after(across, *earlier)], axis=-1)
    return (pair, swap(pair, "chan", 1)), across


def far_sum(other, far):
    return (far + other[:, D // 4 :].astype(WIDE)).astype(LOW)


def near_sum(other, near, across):
    return near + other[:, : D // 4].astype(WIDE) + across.astype(WIDE)


def branch_parts(rows, matrix, *earlier):
    def product(low, high):
        return lax.dot_general(
            rows, matrix[low:high], (((1,), (1,)), ((), ())), preferred_element_type=WIDE
        )

    other = after(swap(product(D // 2, D).astype(LOW), "chan", 1), *earlier)
    sent = far_sum(other, product(D // 4, D // 2))
    return other, sent, product(0, D // 4)


def pair_kernel(rows, matrix, send_out, far_out, near_out):
    def back(low, high):
        return lax.dot_general(
            rows[...], matrix[low:high, :], (((1,), (1,)), ((), ())), preferred_element_type=WIDE
        )

    send_out[...] = back(D // 2, D).astype(LOW)
    keep = back(0, D // 2)
    near_out[...] = keep[:, : D // 4]
    far_out[...] = keep[:, D // 4 :]


def pair_parts(rows, matrix):
    tokens, depth = rows.shape
    block = 512

    def cut(extent):
        return pl.BlockSpec((block, extent), lambda i: (i, 0))

    return pl.pallas_call(
        pair_kernel,
        grid=(tokens // block,),
        in_specs=[cut(depth), pl.BlockSpec(matrix.shape, lambda i: (0, 0))],
        out_specs=[cut(D // 2), cut(D // 4), cut(D // 4)],
        out_shape=[
            jax.ShapeDtypeStruct((tokens, D // 2), LOW),
            jax.ShapeDtypeStruct((tokens, D // 4), WIDE),
            jax.ShapeDtypeStruct((tokens, D // 4), WIDE),
        ],
        compiler_params=pltpu.CompilerParams(vmem_limit_bytes=VMEM_BYTES),
        cost_estimate=pl.CostEstimate(
            flops=2 * tokens * D * depth,
            bytes_accessed=2 * matrix.size + 2 * rows.size + 6 * tokens * D // 2,
            transcendentals=0,
        ),
    )(rows, matrix)


def norm_back(grad_rows, hat_rows, inverse, gain_row, inner):
    scaled = grad_rows * gain_row[None, :]
    return (
        inverse[:, None] * (scaled - hat_rows * (inner / D)[:, None]),
        jnp.sum(grad_rows * hat_rows, axis=0),
    )


def keep_masks(starts):
    keep_one = 1.0 - starts
    before = jnp.concatenate([jnp.zeros((1,), jnp.float32), starts[:-1]])
    return (keep_one, keep_one * (1.0 - before))


def conv_taps(padded, kernel, keep_one, keep_two):
    return (
        kernel[2] * padded[2:]
        + kernel[1] * keep_one[:, None] * padded[1:-1]
        + kernel[0] * keep_two[:, None] * padded[:-2]
    )


def product(one, two, dims):
    return lax.dot_general(
        one.astype(LOW), two.astype(LOW), ((dims[:1], dims[1:]), ((), ())),
        preferred_element_type=WIDE,
    )


def summed(terms, *at):
    return terms[0][at].astype(WIDE) + terms[1][at].astype(WIDE) + terms[2][at].astype(WIDE)


def tile_update(g, left_stat, right_stat, left_root, right_root):
    low = g.astype(LOW)
    new_left = DECAY * left_stat + (1.0 - DECAY) * product(low, low, (1, 1))
    new_right = DECAY * right_stat + (1.0 - DECAY) * product(low, low, (0, 0))
    update = product(product(left_root, low, (1, 0)), right_root, (1, 0))
    return update, new_left, new_right


def column_kernel(kinds, tiles, by_kind, *refs):
    parts, rest = refs[: 3 * kinds], refs[3 * kinds :]
    weight, left, right, left_root, right_root = rest[:5]
    grad_out, weight_out, left_out, right_out = rest[5:]
    extent = right.shape[-1]
    for k in range(kinds):
        for i in range(tiles):
            columns = slice(i * extent, (i + 1) * extent)
            at = (k, slice(None), columns) if by_kind else (slice(None), k, columns)
            g = summed(parts[3 * k : 3 * k + 3], slice(None), columns)
            update, new_left, new_right = tile_update(
                g, left[0, k, i], right[0, k, i], left_root[0, k, i], right_root[0, k, i]
            )
            grad_out[at] = g
            weight_out[at] = weight[at] - MATRIX_RATE * update
            left_out[0, k, i] = new_left
            right_out[0, k, i] = new_right


def column_update(weight, terms, first_column, step_tiles, by_kind, *stats):
    kinds, width = stats[0].shape[1], weight.shape[2]
    rows, extent = terms[0].shape[0], stats[1].shape[-1]
    steps = width // extent // step_tiles
    step = step_tiles * extent
    begin = first_column // step

    def part(k):
        return [pl.BlockSpec((rows, step), lambda i: (0, begin + k * steps + i))] * 3

    shape = (kinds, rows, step) if by_kind else (rows, kinds, step)
    cut = pl.BlockSpec(shape, lambda i: (0, 0, i))
    stat_cuts = [
        pl.BlockSpec((1, kinds, step_tiles) + s.shape[-2:], lambda i: (0, 0, i, 0, 0))
        for s in stats
    ]
    return pl.pallas_call(
        lambda *refs: column_kernel(kinds, step_tiles, by_kind, *refs),
        grid=(steps,),
        in_specs=[spec for k in range(kinds) for spec in part(k)] + [cut] + stat_cuts,
        out_specs=[cut, cut] + stat_cuts[:2],
        out_shape=[jax.ShapeDtypeStruct(weight.shape, WIDE)] * 2
        + [jax.ShapeDtypeStruct(s.shape, WIDE) for s in stats[:2]],
        compiler_params=pltpu.CompilerParams(vmem_limit_bytes=VMEM_BYTES),
        cost_estimate=pl.CostEstimate(
            flops=8 * extent * weight.size, bytes_accessed=38 * weight.size, transcendentals=0
        ),
    )(*list(terms) * kinds, weight, *stats)


def row_kernel(tiles, *refs):
    terms, weight, left, right, left_root, right_root = refs[:3], *refs[3:8]
    grad_out, weight_out, left_out, right_out = refs[8:]
    extent = left.shape[-1]
    for i in range(tiles):
        rows = slice(i * extent, (i + 1) * extent)
        g = summed(terms, slice(None), rows).T
        update, new_left, new_right = tile_update(
            g, left[i, 0], right[i, 0], left_root[i, 0], right_root[i, 0]
        )
        grad_out[rows, :] = g
        weight_out[rows, :] = weight[rows, :] - MATRIX_RATE * update
        left_out[i, 0] = new_left
        right_out[i, 0] = new_right


def row_update(weight, terms, first_column, step_tiles, *stats):
    extent = stats[0].shape[-1]
    columns = weight.shape[1]
    step = step_tiles * extent
    begin = first_column // step
    cut = pl.BlockSpec((step, columns), lambda i: (i, 0))
    stat_cuts = [
        pl.BlockSpec((step_tiles, 1) + s.shape[-2:], lambda i: (i, 0, 0, 0)) for s in stats
    ]
    return pl.pallas_call(
        lambda *refs: row_kernel(step_tiles, *refs),
        grid=(weight.shape[0] // step,),
        in_specs=[pl.BlockSpec((columns, step), lambda i: (0, begin + i))] * 3
        + [cut]
        + stat_cuts,
        out_specs=[cut, cut] + stat_cuts[:2],
        out_shape=[jax.ShapeDtypeStruct(weight.shape, WIDE)] * 2
        + [jax.ShapeDtypeStruct(s.shape, WIDE) for s in stats[:2]],
        compiler_params=pltpu.CompilerParams(vmem_limit_bytes=VMEM_BYTES),
        cost_estimate=pl.CostEstimate(
            flops=8 * extent * weight.size, bytes_accessed=38 * weight.size, transcendentals=0
        ),
    )(*terms, weight, *stats)


def shard_kernel(by_kind, column, row, out):
    kinds, width = column.shape[0 if by_kind else 1], column.shape[2]
    for k in range(kinds):
        block = column[k] if by_kind else column[:, k, :]
        out[:, k * width : (k + 1) * width] = block.astype(LOW)
    out[:, kinds * width :] = row[...].T.astype(LOW)


def low_shard(column, row, by_kind):
    rows, size = row.shape[1], column.size + row.size
    return pl.pallas_call(
        lambda *refs: shard_kernel(by_kind, *refs),
        out_shape=jax.ShapeDtypeStruct((rows, size // rows), LOW),
        compiler_params=pltpu.CompilerParams(vmem_limit_bytes=VMEM_BYTES),
        cost_estimate=pl.CostEstimate(flops=0, bytes_accessed=6 * size, transcendentals=0),
    )(column, row)


def ffn_kernel(units, starts, mine, theirs, cot_mine, cot_theirs, *refs):
    act_out, grad_out, send_out, far_out, near_out, inner_out, down_out = refs[-10:-3]
    matrix, sems, sem = refs[-3:]

    def down_copy():
        return pltpu.make_async_copy(matrix.at[:, pl.ds(2 * units, units)], down_out, sem)

    @pl.when(pl.program_id(0) == 0)
    def _():
        copy_pieces(starts, refs[:-10], matrix, sems)
        down_copy().start()

    normed = jnp.concatenate([mine[...], theirs[...]], axis=1)
    cot = jnp.concatenate([cot_mine[...], cot_theirs[...]], axis=1)
    inner = jnp.zeros((normed.shape[0], 1), WIDE)
    for low in range(0, units, 256):
        high = min(low + 256, units)
        gate = jnp.dot(normed, matrix[:, low:high], preferred_element_type=WIDE)
        up = jnp.dot(normed, matrix[:, units + low : units + high], preferred_element_type=WIDE)
        grad = jnp.dot(
            cot, matrix[:, 2 * units + low : 2 * units + high], preferred_element_type=WIDE
        )
        sigmoid = 0.5 * jnp.tanh(0.5 * gate) + 0.5
        silu = gate * sigmoid
        grad_gate = grad * up * (sigmoid + silu * (1.0 - sigmoid))
        grad_up = grad * silu
        act_out[:, low:high] = (silu * up).astype(LOW)
        grad_out[:, low:high] = grad_gate.astype(LOW)
        grad_out[:, units + low : units + high] = grad_up.astype(LOW)
        inner += jnp.sum(grad_gate * gate + grad_up * up, axis=1, keepdims=True)
    inner_out[...] = jnp.broadcast_to(inner, (inner.shape[0], 128)).T[:8]
    grads = grad_out[...]

    def back(low, high):
        return lax.dot_general(
            grads, matrix[low:high, : 2 * units], (((1,), (1,)), ((), ())),
            preferred_element_type=WIDE,
        )

    send_out[...] = back(D // 2, D).astype(LOW)
    keep = back(0, D // 2)
    near_out[...] = keep[:, : D // 4]
    far_out[...] = keep[:, D // 4 :]

    @pl.when(pl.program_id(0) == pl.num_programs(0) - 1)
    def _():
        down_copy().wait()


def ffn(features, cotangents, pieces, starts):
    tokens, units, count = features[0].shape[0], pieces[0].shape[1] // 3, len(pieces)
    block = 256

    def cut(extent):
        return pl.BlockSpec((block, extent), lambda i, starts: (i, 0))

    whole = pl.BlockSpec(memory_space=pl.ANY)
    return pl.pallas_call(
        lambda *refs: ffn_kernel(units, *refs),
        grid_spec=pltpu.PrefetchScalarGridSpec(
            num_scalar_prefetch=1,
            grid=(tokens // block,),
            in_specs=[cut(D // 2)] * 4 + [whole] * count,
            out_specs=[cut(units), cut(2 * units), cut(D // 2), cut(D // 4), cut(D // 4),
                pl.BlockSpec((8, block), lambda i, starts: (0, i)), whole],
            scratch_shapes=[
                pltpu.VMEM((D, 3 * units), LOW),
                pltpu.SemaphoreType.DMA((count,)),
                pltpu.SemaphoreType.DMA,
            ],
        ),
        out_shape=[
            jax.ShapeDtypeStruct((tokens, units), LOW),
            jax.ShapeDtypeStruct((tokens, 2 * units), LOW),
            jax.ShapeDtypeStruct((tokens, D // 2), LOW),
            jax.ShapeDtypeStruct((tokens, D // 4), WIDE),
            jax.ShapeDtypeStruct((tokens, D // 4), WIDE),
            jax.ShapeDtypeStruct((8, tokens), WIDE),
            jax.ShapeDtypeStruct((D, units), LOW),
        ],
        compiler_params=pltpu.CompilerParams(vmem_limit_bytes=VMEM_BYTES),
        cost_estimate=pl.CostEstimate(
            flops=10 * tokens * D * units,
            bytes_accessed=6 * D * units + 16 * tokens * D,
            transcendentals=tokens * units,
        ),
    )(starts, *features, *cotangents, *pieces)


def parts_kernel(split, mine, theirs, cot_mine, cot_theirs, grads, activated, out):
    j, i = pl.program_id(0), pl.program_id(1)

    def product(left, right):
        out[...] = lax.dot_general(
            left[...], right[...], (((0,), (0,)), ((), ())), preferred_element_type=WIDE
        ).astype(LOW)

    for half, left, right in ((0, mine, grads), (1, theirs, grads)):

        @pl.when((j < split) & (i == half))
        def _():
            product(left, right)

    for half, left, right in ((0, cot_mine, activated), (1, cot_theirs, activated)):

        @pl.when((j == split) & (i == half))
        def _():
            product(left, right)


def gradient_parts(features, cotangents, grads, activated):
    tokens, units = activated.shape
    split = grads.shape[1] // units
    half = pl.BlockSpec((tokens, D // 2), lambda j, i: (0, 0))
    return pl.pallas_call(
        lambda *refs: parts_kernel(split, *refs),
        grid=(split + 1, 2),
        in_specs=[half] * 4
        + [
            pl.BlockSpec((tokens, units), lambda j, i: (0, jnp.minimum(j, split - 1))),
            pl.BlockSpec((tokens, units), lambda j, i: (0, 0)),
        ],
        out_specs=pl.BlockSpec((D // 2, units), lambda j, i: (i, j)),
        out_shape=jax.ShapeDtypeStruct((D, (split + 1) * units), LOW),
        compiler_params=pltpu.CompilerParams(vmem_limit_bytes=VMEM_BYTES),
        cost_estimate=pl.CostEstimate(
            flops=2 * tokens * D * (split + 1) * units,
            bytes_accessed=4 * tokens * D,
            transcendentals=0,
        ),
    )(*features, *cotangents, grads, activated)


def adam_step(values, gradient, moment_one, second):
    moment_one = BETA_ONE * moment_one + (1.0 - BETA_ONE) * gradient
    second = BETA_TWO * second + (1.0 - BETA_TWO) * gradient * gradient
    first_hat = moment_one / (1.0 - BETA_ONE**STEP)
    second_hat = second / (1.0 - BETA_TWO**STEP)
    new_values = values - VECTOR_RATE * (
        first_hat / (jnp.sqrt(second_hat) + ADAM_EPS) + WEIGHT_DECAY * values
    )
    return (moment_one, second, new_values)


def dot(one, two, dims):
    return lax.dot_general(
        one, two, ((dims[:1], dims[1:]), ((), ())), preferred_element_type=WIDE
    )


def body(
    tokens,
    doc_starts,
    cotangent,
    gains,
    conv_kernel,
    in_proj,
    gate_up,
    out_proj,
    down_proj,
    in_left,
    in_right,
    in_left_root,
    in_right_root,
    gate_left,
    gate_right,
    gate_left_root,
    gate_right_root,
    out_left,
    out_right,
    out_left_root,
    out_right_root,
    down_left,
    down_right,
    down_left_root,
    down_right_root,
    gain_first,
    gain_second,
    kernel_first,
    kernel_second,
):
    chan_in = in_proj.shape[2]
    units = gate_up.shape[2]

    in_kinds = in_proj.transpose(1, 0, 2)
    second_shard = low_shard(gate_up, down_proj, False)
    first_pieces, first_starts = ring_gather(low_shard(in_kinds, out_proj, True), second_shard)
    tokens_halves, tokens_across = spread(tokens, *first_pieces[3:5])
    tokens_full = jnp.concatenate(tokens_halves, axis=1)
    gain_full = jnp.concatenate(spread(gains[:1])[0], axis=1)
    pieces, starts_two = ring_gather(after(second_shard, *first_pieces[-4:-2]))

    cot_halves, cot_across = spread(after(cotangent, tokens_across), pieces[1])
    wide_full = tokens_full.astype(WIDE)
    inv_one = lax.rsqrt(jnp.sum(wide_full * wide_full, axis=1) / D + EPS)
    spread_one = (wide_full * inv_one[:, None] * gain_full).astype(LOW)
    resid_in = tokens.astype(WIDE)
    hat_one = resid_in * inv_one[:, None]
    first_full = placed_rows(first_pieces, first_starts)
    in_full, out_full = first_full[:, : 3 * chan_in], first_full[:, 3 * chan_in :]
    projected = dot(spread_one, in_full, (1, 0))
    in_gate = projected[:, :chan_in]
    out_gate = projected[:, chan_in : 2 * chan_in]
    conv_input = projected[:, 2 * chan_in :]
    bx_low = (in_gate * conv_input).astype(LOW)
    starts = doc_starts.astype(WIDE)
    tail_keep = 1.0 - starts[-1]
    edge_rows = jnp.concatenate([bx_low[-2:-1] * tail_keep.astype(LOW), bx_low[-1:]], axis=0)
    carried = after(from_behind(edge_rows, "seq", 1), cot_across, *pieces[1:3])
    padded = jnp.concatenate([carried, bx_low], axis=0).astype(WIDE)
    keep_one, keep_two = keep_masks(starts)
    filtered = conv_taps(padded, conv_kernel, keep_one, keep_two)
    gated_low = (out_gate * filtered).astype(LOW)
    other, sent, near = branch_parts(gated_low, out_full)
    across = after(swap(sent, "chan", 2), *pieces[3:5])
    residual = resid_in + near_sum(other, near, across)

    squares = all_sum(jnp.sum(residual * residual, axis=1), "chan")
    inv_two = lax.rsqrt(squares / D + EPS)
    hat_two = residual * inv_two[:, None]
    normed_two = (hat_two * gains[1][None, :]).astype(LOW)
    two_halves, _ = spread(normed_two, *pieces[5:7])
    activated, grad_hidden, two_send, two_far, two_near, inner_two, down_full = ffn(
        two_halves, cot_halves, pieces, starts_two
    )
    other = swap(two_send, "chan", 1)
    sent_two = sent = far_sum(other, two_far)
    inner_two = all_sum(inner_two[0], "chan")
    second_part = gradient_parts(two_halves, cot_halves, after(grad_hidden, sent, inner_two), activated)
    across = after(swap(sent, "chan", 2), second_part, inner_two)
    grad_norm_two = near_sum(other, two_near, across)
    resid_norm, gain_two = norm_back(grad_norm_two, hat_two, inv_two, gains[1], inner_two)
    grad_resid = cotangent.astype(WIDE) + resid_norm
    mixed_send, mixed_far, mixed_near = pair_parts(after(activated, grad_resid), down_full)
    resid_halves, resid_across = spread(grad_resid.astype(LOW), mixed_send)
    resid_full = jnp.concatenate(resid_halves, axis=1)
    grad_gated = dot(resid_full, out_full, (1, 0))
    grad_conv = grad_gated * out_gate
    grad_cpart = grad_gated * filtered
    tap_one = keep_one[:, None] * grad_conv
    tap_two = keep_two[:, None] * grad_conv
    grad_padded = (
        jnp.pad(conv_kernel[2][None, :] * grad_conv, ((2, 0), (0, 0)))
        + jnp.pad(conv_kernel[1][None, :] * tap_one, ((1, 1), (0, 0)))
        + jnp.pad(conv_kernel[0][None, :] * tap_two, ((0, 2), (0, 0)))
    )
    out_part = dot(resid_full, gated_low, (0, 0)).astype(LOW)
    returned = after(from_behind(grad_padded[:2], "seq", -1), out_part)
    edge_back = jnp.concatenate([returned[0:1] * tail_keep, returned[1:2]], axis=0)
    grad_bx = grad_padded[2:] + jnp.pad(edge_back, ((grad_conv.shape[0] - 2, 0), (0, 0)))
    grad_bx = lax.optimization_barrier(grad_bx.astype(LOW)).astype(WIDE)
    kernel_part = jnp.stack(
        [
            jnp.sum(tap_two * padded[:-2], axis=0),
            jnp.sum(tap_one * padded[1:-1], axis=0),
            jnp.sum(grad_conv * padded[2:], axis=0),
        ]
    )
    grad_proj = jnp.concatenate(
        [
            (grad_bx * conv_input).astype(LOW),
            grad_cpart.astype(LOW),
            (grad_bx * in_gate).astype(LOW),
        ],
        axis=1,
    )
    second_terms, arrived, early2 = ring_total(after(second_part, grad_norm_two))
    other, last_sent, near = branch_parts(grad_proj, in_full, *arrived)
    grad_norm_one = near_sum(other, near, swap(last_sent, "chan", 2))
    other = swap(after(mixed_send, last_sent), "chan", 1)
    sent = after(far_sum(other, mixed_far), grad_norm_one)
    mixed = (residual + near_sum(other, mixed_near, swap(sent, "chan", 2))).astype(LOW)
    inner_one = all_sum(jnp.sum(grad_proj.astype(WIDE) * projected, axis=1), "chan")
    input_norm, gain_one = norm_back(grad_norm_one, hat_one, inv_one, gains[0], inner_one)
    input_grad = grad_resid + input_norm

    in_part = dot(spread_one, grad_proj, (0, 0)).astype(LOW)
    first_part = after(jnp.concatenate([in_part, out_part], axis=1), last_sent)
    first_terms, _, early = ring_total(first_part)
    down_terms = after_all(second_terms, grad_norm_one)
    second_terms = after_all(second_terms, *early)
    vector_grad = all_sum(
        jnp.concatenate([gain_one[None], gain_two[None], kernel_part], axis=0), "seq"
    )
    gain_grad, kernel_grad = vector_grad[:2], vector_grad[2:]

    in_grad, in_new, in_left_new, in_right_new = column_update(
        in_kinds, first_terms, 0, 2, True, in_left, in_right, in_left_root, in_right_root
    )
    in_grad, in_new = in_grad.transpose(1, 0, 2), in_new.transpose(1, 0, 2)
    gate_grad, gate_new, gate_left_new, gate_right_new = column_update(
        gate_up, second_terms, 0, 3, False, gate_left, gate_right, gate_left_root, gate_right_root
    )
    out_grad, out_new, out_left_new, out_right_new = row_update(
        out_proj, first_terms, 3 * chan_in, 2, out_left, out_right, out_left_root, out_right_root
    )
    down_grad, down_new, down_left_new, down_right_new = row_update(
        down_proj, down_terms, 2 * units, 3, down_left, down_right, down_left_root,
        down_right_root,
    )
    gain_one_new, gain_two_new, gains_new = adam_step(gains, gain_grad, gain_first, gain_second)
    kernel_one_new, kernel_two_new, kernel_new = adam_step(
        conv_kernel, kernel_grad, kernel_first, kernel_second
    )
    return (
        mixed,
        input_grad,
        in_grad,
        gate_grad,
        out_grad,
        down_grad,
        in_new,
        gate_new,
        out_new,
        down_new,
        in_left_new,
        in_right_new,
        gate_left_new,
        gate_right_new,
        out_left_new,
        out_right_new,
        down_left_new,
        down_right_new,
        gain_one_new,
        gain_two_new,
        gains_new,
        kernel_one_new,
        kernel_two_new,
        kernel_new,
    )


def solution(mesh):
    placed = (
        P("seq", "chan"),
        P("seq"),
        P("seq", "chan"),
        P(None, "chan"),
        P(None, "chan"),
        P("seq", None, "chan"),
        P("seq", None, "chan"),
        P("chan", "seq"),
        P("chan", "seq"),
        P("seq", None, "chan", None, None),
        P("seq", None, "chan", None, None),
        P("seq", None, "chan", None, None),
        P("seq", None, "chan", None, None),
        P("seq", None, "chan", None, None),
        P("seq", None, "chan", None, None),
        P("seq", None, "chan", None, None),
        P("seq", None, "chan", None, None),
        P("chan", "seq", None, None),
        P("chan", "seq", None, None),
        P("chan", "seq", None, None),
        P("chan", "seq", None, None),
        P("chan", "seq", None, None),
        P("chan", "seq", None, None),
        P("chan", "seq", None, None),
        P("chan", "seq", None, None),
        P(None, "chan"),
        P(None, "chan"),
        P(None, "chan"),
        P(None, "chan"),
    )
    return jax.shard_map(
        body,
        mesh=mesh,
        in_specs=placed,
        out_specs=(
            P("seq", "chan"),
            P("seq", "chan"),
            P("seq", None, "chan"),
            P("seq", None, "chan"),
            P("chan", "seq"),
            P("chan", "seq"),
            P("seq", None, "chan"),
            P("seq", None, "chan"),
            P("chan", "seq"),
            P("chan", "seq"),
            P("seq", None, "chan", None, None),
            P("seq", None, "chan", None, None),
            P("seq", None, "chan", None, None),
            P("seq", None, "chan", None, None),
            P("chan", "seq", None, None),
            P("chan", "seq", None, None),
            P("chan", "seq", None, None),
            P("chan", "seq", None, None),
            P(None, "chan"),
            P(None, "chan"),
            P(None, "chan"),
            P(None, "chan"),
            P(None, "chan"),
            P(None, "chan"),
        ),
        check_vma=False,
    )
```

```python
import collections
import math

import jax
import jax.numpy as jnp
from jax import lax
from jax.experimental import pallas as pl
from jax.experimental.pallas import tpu as pltpu
from jax.sharding import PartitionSpec as P

D = 1024
STEP = 10


EPS = 1e-05
DECAY = 0.5
MATRIX_RATE = 0.5
VECTOR_RATE = 1.0
BETA_ONE = 0.9
BETA_TWO = 0.95
ADAM_EPS = 1e-08
WEIGHT_DECAY = 0.01
LOW = jnp.bfloat16
WIDE = jnp.float32
VMEM_BYTES = 56 * 1024 * 1024


def after(value, *earlier):
    return lax.optimization_barrier((value,) + earlier)[0]


def after_all(values, *earlier):
    return lax.optimization_barrier(tuple(values) + earlier)[: len(values)]


def from_behind(block, axis, distance):
    devices = range(lax.axis_size(axis))
    route = [(i - distance, i) for i in devices if i - distance in devices]
    return lax.ppermute(block, axis, route)


def swap(block, axis, bit):
    devices = range(lax.axis_size(axis))
    return lax.ppermute(block, axis, [(i, i ^ bit) for i in devices])


def all_sum(block, axis):
    bit = 1
    while bit < lax.axis_size(axis):
        block = block + swap(block, axis, bit)
        bit *= 2
    return block


def ring_order(count):
    return [2 * p if 2 * p < count else 2 * (count - p) - 1 for p in range(count)]


def ring_index(place, count):
    place = lax.rem(place + 2 * count, count)
    return jnp.where(2 * place < count, 2 * place, 2 * (count - place) - 1)


def ring_place(index, count):
    return jnp.where(lax.rem(index, 2) == 0, index // 2, count - 1 - index // 2)


def ring_send(block, step):
    order = ring_order(lax.axis_size("seq"))
    count = len(order)
    route = [(order[p], order[(p + step) % count]) for p in range(count)]
    return lax.ppermute(block, "seq", route)


def row_start(index, rows):
    quarter_rows = D // 4
    first = index * rows
    relative = (first // quarter_rows) ^ lax.axis_index("chan")
    place = (relative >> 1) | ((relative & 1) << 1)
    return place * quarter_rows + lax.rem(first, quarter_rows)


def copy_pieces(starts, pieces, whole, sems):
    copies = []
    for i, piece in enumerate(pieces):
        rows = pl.ds(pl.multiple_of(starts[i], 16), piece.shape[0])
        copies.append(pltpu.make_async_copy(piece, whole.at[rows], sems.at[i]))
    for copy in copies:
        copy.start()
    for copy in copies:
        copy.wait()


def place_kernel(starts, *refs):
    copy_pieces(starts, refs[:-2], refs[-2], refs[-1])


def placed_rows(pieces, starts):
    width = pieces[0].shape[1]
    count = len(pieces)
    total = sum(p.shape[0] for p in pieces)
    return pl.pallas_call(
        place_kernel,
        grid_spec=pltpu.PrefetchScalarGridSpec(
            num_scalar_prefetch=1,
            grid=(1,),
            in_specs=[pl.BlockSpec(memory_space=pl.ANY)] * count,
            out_specs=pl.BlockSpec((total, width), lambda i, starts: (0, 0)),
            scratch_shapes=[pltpu.SemaphoreType.DMA((count,))],
        ),
        out_shape=jax.ShapeDtypeStruct((total, width), pieces[0].dtype),
        compiler_params=pltpu.CompilerParams(vmem_limit_bytes=VMEM_BYTES),
        cost_estimate=pl.CostEstimate(
            flops=0, bytes_accessed=4 * total * width, transcendentals=0
        ),
    )(starts, *pieces)


def ring_gather(shard, *during):
    count = lax.axis_size("seq")
    place = ring_place(lax.axis_index("seq"), count)
    rows = shard.shape[0]
    pieces, starts = [], []

    def put(block, source, offset=0):
        pieces.append(block)
        starts.append(row_start(ring_index(source, count), rows) + offset)

    put(shard, place)
    ahead = behind = shard
    for step in range(1, count // 2):
        if step == 2:
            ahead, behind = after(ahead, *during), after(behind, *during)
        ahead = ring_send(ahead, 1)
        behind = ring_send(behind, -1)
        put(ahead, place - step)
        put(behind, place + step)
    half = rows // 2
    ahead = ring_send(ahead[:half], 1)
    behind = ring_send(behind[half:], -1)
    put(ahead, place - count // 2)
    put(behind, place - count // 2, half)
    return pieces, jnp.stack(starts).astype(jnp.int32)


def far_rows(halves, right, *earlier):
    count = lax.axis_size("seq")
    rows = D // count
    far = ring_place(lax.axis_index("seq"), count) + count // 2
    start = row_start(ring_index(far, count), rows)
    inner = lax.rem(start, D // 2)
    mine, theirs = [
        lax.dynamic_slice(half, (0, inner), (half.shape[0], rows)) for half in halves
    ]
    left = jnp.where(start < D // 2, mine, theirs)
    return dot(left, after(right, *earlier), (0, 0)).astype(LOW)


def ring_total(partial, *later, middle=(), across=None, entry=()):
    count = lax.axis_size("seq")
    place = ring_place(lax.axis_index("seq"), count)
    rows = partial.shape[0] // count
    half = rows // 2
    far = count // 2

    def own(target, offset=0, extent=rows):
        start = row_start(ring_index(target, count), rows) + offset
        return lax.dynamic_slice(partial, (start, 0), (extent, partial.shape[1]))

    if across is None:
        across = own(place + far)
    ahead = ring_send(across[:half], 1)
    behind = ring_send(across[half:], -1)
    for step in range(far - 1, 0, -1):
        earlier = {1: later, 2: middle, far - 1: entry}.get(step, ())
        ahead, behind = lax.optimization_barrier((ahead, behind) + earlier)[:2]
        up, down = own(place + step).astype(WIDE), own(place - step).astype(WIDE)
        if step == far - 1:
            up = up + jnp.pad(ahead.astype(WIDE), ((0, rows - half), (0, 0)))
            down = down + jnp.pad(behind.astype(WIDE), ((half, 0), (0, 0)))
        else:
            up = up + ahead.astype(WIDE)
            down = down + behind.astype(WIDE)
        arrived = ahead, behind
        if step == 2:
            early = ahead, behind
        ahead = ring_send(up.astype(LOW), 1)
        behind = ring_send(down.astype(LOW), -1)
    return (own(place), ahead, behind), arrived, early, (up.astype(LOW), down.astype(LOW))


def spread(quarter, *earlier):
    across = swap(quarter, "chan", 2)
    pair = jnp.concatenate([quarter, after(across, *earlier)], axis=-1)
    return (pair, swap(pair, "chan", 1)), across


def far_sum(other, far):
    return (far + other[:, D // 4 :].astype(WIDE)).astype(LOW)


def near_sum(other, near, across):
    return near + other[:, : D // 4].astype(WIDE) + across.astype(WIDE)


def branch_parts(rows, matrix, *earlier):
    def product(low, high):
        return lax.dot_general(
            rows, matrix[low:high], (((1,), (1,)), ((), ())), preferred_element_type=WIDE
        )

    other = after(swap(product(D // 2, D).astype(LOW), "chan", 1), *earlier)
    sent = far_sum(other, product(D // 4, D // 2))
    return other, sent, product(0, D // 4)


def pair_kernel(rows, matrix, send_out, far_out, near_out):
    def back(low, high):
        return lax.dot_general(
            rows[...], matrix[low:high, :], (((1,), (1,)), ((), ())), preferred_element_type=WIDE
        )

    send_out[...] = back(D // 2, D).astype(LOW)
    keep = back(0, D // 2)
    near_out[...] = keep[:, : D // 4]
    far_out[...] = keep[:, D // 4 :]


def pair_parts(rows, matrix):
    tokens, depth = rows.shape
    block = 512

    def cut(extent):
        return pl.BlockSpec((block, extent), lambda i: (i, 0))

    return pl.pallas_call(
        pair_kernel,
        grid=(tokens // block,),
        in_specs=[cut(depth), pl.BlockSpec(matrix.shape, lambda i: (0, 0))],
        out_specs=[cut(D // 2), cut(D // 4), cut(D // 4)],
        out_shape=[
            jax.ShapeDtypeStruct((tokens, D // 2), LOW),
            jax.ShapeDtypeStruct((tokens, D // 4), WIDE),
            jax.ShapeDtypeStruct((tokens, D // 4), WIDE),
        ],
        compiler_params=pltpu.CompilerParams(vmem_limit_bytes=VMEM_BYTES),
        cost_estimate=pl.CostEstimate(
            flops=2 * tokens * D * depth,
            bytes_accessed=2 * matrix.size + 2 * rows.size + 6 * tokens * D // 2,
            transcendentals=0,
        ),
    )(rows, matrix)


def norm_back(grad_rows, hat_rows, inverse, gain_row, inner):
    scaled = grad_rows * gain_row[None, :]
    return (
        inverse[:, None] * (scaled - hat_rows * (inner / D)[:, None]),
        jnp.sum(grad_rows * hat_rows, axis=0),
    )


def keep_masks(starts):
    keep_one = 1.0 - starts
    before = jnp.concatenate([jnp.zeros((1,), jnp.float32), starts[:-1]])
    return (keep_one, keep_one * (1.0 - before))


def conv_taps(padded, kernel, keep_one, keep_two):
    return (
        kernel[2] * padded[2:]
        + kernel[1] * keep_one[:, None] * padded[1:-1]
        + kernel[0] * keep_two[:, None] * padded[:-2]
    )


def product(one, two, dims):
    return lax.dot_general(
        one.astype(LOW), two.astype(LOW), ((dims[:1], dims[1:]), ((), ())),
        preferred_element_type=WIDE,
    )


def summed(terms, *at):
    return terms[0][at].astype(WIDE) + terms[1][at].astype(WIDE) + terms[2][at].astype(WIDE)


Tiles = collections.namedtuple(
    "Tiles", ("kernel", "steps", "in_specs", "out_specs", "operands", "shapes")
)


def tile_update(g, left_stat, right_stat, left_root, right_root):
    low = g.astype(LOW)
    new_left = DECAY * left_stat + (1.0 - DECAY) * product(low, low, (1, 1))
    new_right = DECAY * right_stat + (1.0 - DECAY) * product(low, low, (0, 0))
    update = product(product(left_root, low, (1, 0)), right_root, (1, 0))
    return update, new_left, new_right


def column_kernel(kinds, tiles, by_kind, *refs):
    parts, rest = refs[: 3 * kinds], refs[3 * kinds :]
    weight, left, right, left_root, right_root = rest[:5]
    grad_out, weight_out, left_out, right_out = rest[5:]
    extent = right.shape[-1]
    for k in range(kinds):
        for i in range(tiles):
            columns = slice(i * extent, (i + 1) * extent)
            at = (k, slice(None), columns) if by_kind else (slice(None), k, columns)
            g = summed(parts[3 * k : 3 * k + 3], slice(None), columns)
            update, new_left, new_right = tile_update(
                g, left[0, k, i], right[0, k, i], left_root[0, k, i], right_root[0, k, i]
            )
            grad_out[at] = g
            weight_out[at] = weight[at] - MATRIX_RATE * update
            left_out[0, k, i] = new_left
            right_out[0, k, i] = new_right


def column_tiles(weight, terms, first_column, step_tiles, by_kind, *stats):
    kinds, width = stats[0].shape[1], weight.shape[2]
    rows, extent = terms[0].shape[0], stats[1].shape[-1]
    steps = width // extent // step_tiles
    step = step_tiles * extent
    begin = first_column // step

    def part(k):
        return [pl.BlockSpec((rows, step), lambda i: (0, begin + k * steps + i))] * 3

    shape = (kinds, rows, step) if by_kind else (rows, kinds, step)
    cut = pl.BlockSpec(shape, lambda i: (0, 0, i))
    stat_cuts = [
        pl.BlockSpec((1, kinds, step_tiles) + s.shape[-2:], lambda i: (0, 0, i, 0, 0))
        for s in stats
    ]
    return Tiles(
        lambda *refs: column_kernel(kinds, step_tiles, by_kind, *refs),
        steps,
        [spec for k in range(kinds) for spec in part(k)] + [cut] + stat_cuts,
        [cut, cut] + stat_cuts[:2],
        list(terms) * kinds + [weight, *stats],
        [weight.shape] * 2 + [s.shape for s in stats[:2]],
    )


def row_kernel(tiles, *refs):
    terms, weight, left, right, left_root, right_root = refs[:3], *refs[3:8]
    grad_out, weight_out, left_out, right_out = refs[8:]
    extent = left.shape[-1]
    for i in range(tiles):
        rows = slice(i * extent, (i + 1) * extent)
        g = summed(terms, slice(None), rows).T
        update, new_left, new_right = tile_update(
            g, left[i, 0], right[i, 0], left_root[i, 0], right_root[i, 0]
        )
        grad_out[rows, :] = g
        weight_out[rows, :] = weight[rows, :] - MATRIX_RATE * update
        left_out[i, 0] = new_left
        right_out[i, 0] = new_right


def row_tiles(weight, terms, first_column, step_tiles, *stats):
    extent = stats[0].shape[-1]
    columns = weight.shape[1]
    step = step_tiles * extent
    begin = first_column // step
    cut = pl.BlockSpec((step, columns), lambda i: (i, 0))
    stat_cuts = [
        pl.BlockSpec((step_tiles, 1) + s.shape[-2:], lambda i: (i, 0, 0, 0)) for s in stats
    ]
    return Tiles(
        lambda *refs: row_kernel(step_tiles, *refs),
        weight.shape[0] // step,
        [pl.BlockSpec((columns, step), lambda i: (0, begin + i))] * len(terms) + [cut] + stat_cuts,
        [cut, cut] + stat_cuts[:2],
        [*terms, weight, *stats],
        [weight.shape] * 2 + [s.shape for s in stats[:2]],
    )


def both_updates(one, two):
    assert one.steps == two.steps
    ins = len(one.operands), len(two.operands)

    def kernel(*refs):
        outs = refs[sum(ins) :]
        one.kernel(*refs[: ins[0]], *outs[:4])
        two.kernel(*refs[ins[0] : sum(ins)], *outs[4:])

    operands = one.operands + two.operands
    shapes = one.shapes + two.shapes
    size = math.prod(one.shapes[0]) + math.prod(two.shapes[0])
    new = pl.pallas_call(
        kernel,
        grid=(one.steps,),
        in_specs=one.in_specs + two.in_specs,
        out_specs=one.out_specs + two.out_specs,
        out_shape=[jax.ShapeDtypeStruct(shape, WIDE) for shape in shapes],
        compiler_params=pltpu.CompilerParams(vmem_limit_bytes=VMEM_BYTES),
        cost_estimate=pl.CostEstimate(
            flops=1024 * size, bytes_accessed=38 * size, transcendentals=0
        ),
    )(*operands)
    return new[:4], new[4:]


def shard_kernel(by_kind, column, row, out):
    kinds, width = column.shape[0 if by_kind else 1], column.shape[2]
    for k in range(kinds):
        block = column[k] if by_kind else column[:, k, :]
        out[:, k * width : (k + 1) * width] = block.astype(LOW)
    out[:, kinds * width :] = row[...].T.astype(LOW)


def low_shard(column, row, by_kind):
    rows, size = row.shape[1], column.size + row.size
    return pl.pallas_call(
        lambda *refs: shard_kernel(by_kind, *refs),
        out_shape=jax.ShapeDtypeStruct((rows, size // rows), LOW),
        compiler_params=pltpu.CompilerParams(vmem_limit_bytes=VMEM_BYTES),
        cost_estimate=pl.CostEstimate(flops=0, bytes_accessed=6 * size, transcendentals=0),
    )(column, row)


def ffn_kernel(units, starts, mine, theirs, cot_mine, cot_theirs, *refs):
    act_out, grad_out, send_out, far_out, near_out, inner_out, down_out = refs[-10:-3]
    matrix, sems, sem = refs[-3:]

    def down_copy():
        return pltpu.make_async_copy(matrix.at[:, pl.ds(2 * units, units)], down_out, sem)

    @pl.when(pl.program_id(0) == 0)
    def _():
        copy_pieces(starts, refs[:-10], matrix, sems)
        down_copy().start()

    normed = jnp.concatenate([mine[...], theirs[...]], axis=1)
    cot = jnp.concatenate([cot_mine[...], cot_theirs[...]], axis=1)
    inner = jnp.zeros((normed.shape[0], 1), WIDE)
    for low in range(0, units, 256):
        high = min(low + 256, units)
        gate = jnp.dot(normed, matrix[:, low:high], preferred_element_type=WIDE)
        up = jnp.dot(normed, matrix[:, units + low : units + high], preferred_element_type=WIDE)
        grad = jnp.dot(
            cot, matrix[:, 2 * units + low : 2 * units + high], preferred_element_type=WIDE
        )
        sigmoid = 0.5 * jnp.tanh(0.5 * gate) + 0.5
        silu = gate * sigmoid
        grad_gate = grad * up * (sigmoid + silu * (1.0 - sigmoid))
        grad_up = grad * silu
        act_out[:, low:high] = (silu * up).astype(LOW)
        grad_out[:, low:high] = grad_gate.astype(LOW)
        grad_out[:, units + low : units + high] = grad_up.astype(LOW)
        inner += jnp.sum(grad_gate * gate + grad_up * up, axis=1, keepdims=True)
    inner_out[...] = jnp.broadcast_to(inner, (inner.shape[0], 128)).T[:8]
    grads = grad_out[...]

    def back(low, high):
        return lax.dot_general(
            grads, matrix[low:high, : 2 * units], (((1,), (1,)), ((), ())),
            preferred_element_type=WIDE,
        )

    send_out[...] = back(D // 2, D).astype(LOW)
    keep = back(0, D // 2)
    near_out[...] = keep[:, : D // 4]
    far_out[...] = keep[:, D // 4 :]

    @pl.when(pl.program_id(0) == pl.num_programs(0) - 1)
    def _():
        down_copy().wait()


def ffn(features, cotangents, pieces, starts):
    tokens, units, count = features[0].shape[0], pieces[0].shape[1] // 3, len(pieces)
    block = 256

    def cut(extent):
        return pl.BlockSpec((block, extent), lambda i, starts: (i, 0))

    whole = pl.BlockSpec(memory_space=pl.ANY)
    return pl.pallas_call(
        lambda *refs: ffn_kernel(units, *refs),
        grid_spec=pltpu.PrefetchScalarGridSpec(
            num_scalar_prefetch=1,
            grid=(tokens // block,),
            in_specs=[cut(D // 2)] * 4 + [whole] * count,
            out_specs=[cut(units), cut(2 * units), cut(D // 2), cut(D // 4), cut(D // 4),
                pl.BlockSpec((8, block), lambda i, starts: (0, i)), whole],
            scratch_shapes=[
                pltpu.VMEM((D, 3 * units), LOW),
                pltpu.SemaphoreType.DMA((count,)),
                pltpu.SemaphoreType.DMA,
            ],
        ),
        out_shape=[
            jax.ShapeDtypeStruct((tokens, units), LOW),
            jax.ShapeDtypeStruct((tokens, 2 * units), LOW),
            jax.ShapeDtypeStruct((tokens, D // 2), LOW),
            jax.ShapeDtypeStruct((tokens, D // 4), WIDE),
            jax.ShapeDtypeStruct((tokens, D // 4), WIDE),
            jax.ShapeDtypeStruct((8, tokens), WIDE),
            jax.ShapeDtypeStruct((D, units), LOW),
        ],
        compiler_params=pltpu.CompilerParams(vmem_limit_bytes=VMEM_BYTES),
        cost_estimate=pl.CostEstimate(
            flops=10 * tokens * D * units,
            bytes_accessed=6 * D * units + 16 * tokens * D,
            transcendentals=tokens * units,
        ),
    )(starts, *features, *cotangents, *pieces)


def parts_kernel(split, mine, theirs, cot_mine, cot_theirs, grads, activated, out):
    j, i = pl.program_id(0), pl.program_id(1)

    def product(left, right):
        out[...] = lax.dot_general(
            left[...], right[...], (((0,), (0,)), ((), ())), preferred_element_type=WIDE
        ).astype(LOW)

    for half, left, right in ((0, mine, grads), (1, theirs, grads)):

        @pl.when((j < split) & (i == half))
        def _():
            product(left, right)

    for half, left, right in ((0, cot_mine, activated), (1, cot_theirs, activated)):

        @pl.when((j == split) & (i == half))
        def _():
            product(left, right)


def gradient_parts(features, cotangents, grads, activated):
    tokens, units = activated.shape
    split = grads.shape[1] // units
    half = pl.BlockSpec((tokens, D // 2), lambda j, i: (0, 0))
    return pl.pallas_call(
        lambda *refs: parts_kernel(split, *refs),
        grid=(split + 1, 2),
        in_specs=[half] * 4
        + [
            pl.BlockSpec((tokens, units), lambda j, i: (0, jnp.minimum(j, split - 1))),
            pl.BlockSpec((tokens, units), lambda j, i: (0, 0)),
        ],
        out_specs=pl.BlockSpec((D // 2, units), lambda j, i: (i, j)),
        out_shape=jax.ShapeDtypeStruct((D, (split + 1) * units), LOW),
        compiler_params=pltpu.CompilerParams(vmem_limit_bytes=VMEM_BYTES),
        cost_estimate=pl.CostEstimate(
            flops=2 * tokens * D * (split + 1) * units,
            bytes_accessed=4 * tokens * D,
            transcendentals=0,
        ),
    )(*features, *cotangents, grads, activated)


def adam_step(values, gradient, moment_one, second):
    moment_one = BETA_ONE * moment_one + (1.0 - BETA_ONE) * gradient
    second = BETA_TWO * second + (1.0 - BETA_TWO) * gradient * gradient
    first_hat = moment_one / (1.0 - BETA_ONE**STEP)
    second_hat = second / (1.0 - BETA_TWO**STEP)
    new_values = values - VECTOR_RATE * (
        first_hat / (jnp.sqrt(second_hat) + ADAM_EPS) + WEIGHT_DECAY * values
    )
    return (moment_one, second, new_values)


def dot(one, two, dims):
    return lax.dot_general(
        one, two, ((dims[:1], dims[1:]), ((), ())), preferred_element_type=WIDE
    )


def body(
    tokens,
    doc_starts,
    cotangent,
    gains,
    conv_kernel,
    in_proj,
    gate_up,
    out_proj,
    down_proj,
    in_left,
    in_right,
    in_left_root,
    in_right_root,
    gate_left,
    gate_right,
    gate_left_root,
    gate_right_root,
    out_left,
    out_right,
    out_left_root,
    out_right_root,
    down_left,
    down_right,
    down_left_root,
    down_right_root,
    gain_first,
    gain_second,
    kernel_first,
    kernel_second,
):
    chan_in = in_proj.shape[2]
    units = gate_up.shape[2]

    in_kinds = in_proj.transpose(1, 0, 2)
    second_shard = low_shard(gate_up, down_proj, False)
    first_pieces, first_starts = ring_gather(low_shard(in_kinds, out_proj, True), second_shard)
    tokens_halves, tokens_across = spread(tokens, *first_pieces[3:5])
    tokens_full = jnp.concatenate(tokens_halves, axis=1)
    gain_full = jnp.concatenate(spread(gains[:1])[0], axis=1)
    pieces, starts_two = ring_gather(after(second_shard, *first_pieces[-4:-2]))

    cot_halves, cot_across = spread(after(cotangent, tokens_across), pieces[1])
    wide_full = tokens_full.astype(WIDE)
    inv_one = lax.rsqrt(jnp.sum(wide_full * wide_full, axis=1) / D + EPS)
    spread_one = (wide_full * inv_one[:, None] * gain_full).astype(LOW)
    resid_in = tokens.astype(WIDE)
    hat_one = resid_in * inv_one[:, None]
    first_full = placed_rows(first_pieces, first_starts)
    in_full, out_full = first_full[:, : 3 * chan_in], first_full[:, 3 * chan_in :]
    projected = dot(spread_one, in_full, (1, 0))
    in_gate = projected[:, :chan_in]
    out_gate = projected[:, chan_in : 2 * chan_in]
    conv_input = projected[:, 2 * chan_in :]
    bx_low = (in_gate * conv_input).astype(LOW)
    starts = doc_starts.astype(WIDE)
    tail_keep = 1.0 - starts[-1]
    edge_rows = jnp.concatenate([bx_low[-2:-1] * tail_keep.astype(LOW), bx_low[-1:]], axis=0)
    carried = after(from_behind(edge_rows, "seq", 1), cot_across, *pieces[1:3])
    padded = jnp.concatenate([carried, bx_low], axis=0).astype(WIDE)
    keep_one, keep_two = keep_masks(starts)
    filtered = conv_taps(padded, conv_kernel, keep_one, keep_two)
    gated_low = (out_gate * filtered).astype(LOW)
    other, sent, near = branch_parts(gated_low, out_full)
    across = after(swap(sent, "chan", 2), *pieces[3:5])
    residual = resid_in + near_sum(other, near, across)

    squares = all_sum(jnp.sum(residual * residual, axis=1), "chan")
    inv_two = lax.rsqrt(squares / D + EPS)
    hat_two = residual * inv_two[:, None]
    normed_two = (hat_two * gains[1][None, :]).astype(LOW)
    two_halves, _ = spread(normed_two, *pieces[5:7])
    activated, grad_hidden, two_send, two_far, two_near, inner_two, down_full = ffn(
        two_halves, cot_halves, pieces, starts_two
    )
    other = swap(two_send, "chan", 1)
    sent_two = sent = far_sum(other, two_far)
    inner_two = all_sum(inner_two[0], "chan")
    far_part = jnp.concatenate(
        [
            far_rows(two_halves, grad_hidden, sent_two),
            far_rows(cot_halves, activated, sent_two),
        ],
        axis=1,
    )
    second_part = gradient_parts(two_halves, cot_halves, after(grad_hidden, sent, inner_two), activated)
    across = after(swap(sent, "chan", 2), second_part, inner_two)
    grad_norm_two = near_sum(other, two_near, across)
    resid_norm, gain_two = norm_back(grad_norm_two, hat_two, inv_two, gains[1], inner_two)
    grad_resid = cotangent.astype(WIDE) + resid_norm
    mixed_send, mixed_far, mixed_near = pair_parts(after(activated, grad_resid), down_full)
    resid_halves, resid_across = spread(grad_resid.astype(LOW), mixed_send)
    resid_full = jnp.concatenate(resid_halves, axis=1)
    grad_gated = dot(resid_full, out_full, (1, 0))
    grad_conv = grad_gated * out_gate
    grad_cpart = grad_gated * filtered
    tap_one = keep_one[:, None] * grad_conv
    tap_two = keep_two[:, None] * grad_conv
    grad_padded = (
        jnp.pad(conv_kernel[2][None, :] * grad_conv, ((2, 0), (0, 0)))
        + jnp.pad(conv_kernel[1][None, :] * tap_one, ((1, 1), (0, 0)))
        + jnp.pad(conv_kernel[0][None, :] * tap_two, ((0, 2), (0, 0)))
    )
    out_part = dot(resid_full, gated_low, (0, 0)).astype(LOW)
    returned = after(from_behind(grad_padded[:2], "seq", -1), out_part)
    edge_back = jnp.concatenate([returned[0:1] * tail_keep, returned[1:2]], axis=0)
    grad_bx = grad_padded[2:] + jnp.pad(edge_back, ((grad_conv.shape[0] - 2, 0), (0, 0)))
    grad_bx = lax.optimization_barrier(grad_bx.astype(LOW)).astype(WIDE)
    kernel_part = jnp.stack(
        [
            jnp.sum(tap_two * padded[:-2], axis=0),
            jnp.sum(tap_one * padded[1:-1], axis=0),
            jnp.sum(grad_conv * padded[2:], axis=0),
        ]
    )
    grad_proj = jnp.concatenate(
        [
            (grad_bx * conv_input).astype(LOW),
            grad_cpart.astype(LOW),
            (grad_bx * in_gate).astype(LOW),
        ],
        axis=1,
    )
    second_terms, arrived, _, _ = ring_total(second_part, across=far_part)
    other, last_sent, near = branch_parts(grad_proj, in_full, *arrived)
    grad_norm_one = near_sum(other, near, swap(last_sent, "chan", 2))
    other = swap(after(mixed_send, last_sent), "chan", 1)
    sent = after(far_sum(other, mixed_far), grad_norm_one)
    mixed = (residual + near_sum(other, mixed_near, swap(sent, "chan", 2))).astype(LOW)
    inner_one = all_sum(jnp.sum(grad_proj.astype(WIDE) * projected, axis=1), "chan")
    input_norm, gain_one = norm_back(grad_norm_one, hat_one, inv_one, gains[0], inner_one)
    input_grad = grad_resid + input_norm

    in_part = dot(spread_one, grad_proj, (0, 0)).astype(LOW)
    first_part = after(jnp.concatenate([in_part, out_part], axis=1), last_sent)
    first_terms, _, early, _ = ring_total(first_part)
    second_terms = after_all(second_terms, *early)
    first_terms = after_all(first_terms, mixed)
    vector_grad = all_sum(
        jnp.concatenate([gain_one[None], gain_two[None], kernel_part], axis=0), "seq"
    )
    gain_grad, kernel_grad = vector_grad[:2], vector_grad[2:]

    (gate_grad, gate_new, gate_left_new, gate_right_new), down_outs = both_updates(
        column_tiles(
            gate_up, second_terms, 0, 3, False, gate_left, gate_right, gate_left_root,
            gate_right_root,
        ),
        row_tiles(
            down_proj, second_terms, 2 * units, 3, down_left, down_right, down_left_root,
            down_right_root,
        ),
    )
    down_grad, down_new, down_left_new, down_right_new = down_outs
    (in_grad, in_new, in_left_new, in_right_new), out_outs = both_updates(
        column_tiles(
            in_kinds, first_terms, 0, 1, True, in_left, in_right, in_left_root, in_right_root
        ),
        row_tiles(
            out_proj, first_terms, 3 * chan_in, 1, out_left, out_right, out_left_root,
            out_right_root,
        ),
    )
    out_grad, out_new, out_left_new, out_right_new = out_outs
    in_grad, in_new = in_grad.transpose(1, 0, 2), in_new.transpose(1, 0, 2)
    gain_one_new, gain_two_new, gains_new = adam_step(gains, gain_grad, gain_first, gain_second)
    kernel_one_new, kernel_two_new, kernel_new = adam_step(
        conv_kernel, kernel_grad, kernel_first, kernel_second
    )
    return (
        mixed,
        input_grad,
        in_grad,
        gate_grad,
        out_grad,
        down_grad,
        in_new,
        gate_new,
        out_new,
        down_new,
        in_left_new,
        in_right_new,
        gate_left_new,
        gate_right_new,
        out_left_new,
        out_right_new,
        down_left_new,
        down_right_new,
        gain_one_new,
        gain_two_new,
        gains_new,
        kernel_one_new,
        kernel_two_new,
        kernel_new,
    )


def solution(mesh):
    placed = (
        P("seq", "chan"),
        P("seq"),
        P("seq", "chan"),
        P(None, "chan"),
        P(None, "chan"),
        P("seq", None, "chan"),
        P("seq", None, "chan"),
        P("chan", "seq"),
        P("chan", "seq"),
        P("seq", None, "chan", None, None),
        P("seq", None, "chan", None, None),
        P("seq", None, "chan", None, None),
        P("seq", None, "chan", None, None),
        P("seq", None, "chan", None, None),
        P("seq", None, "chan", None, None),
        P("seq", None, "chan", None, None),
        P("seq", None, "chan", None, None),
        P("chan", "seq", None, None),
        P("chan", "seq", None, None),
        P("chan", "seq", None, None),
        P("chan", "seq", None, None),
        P("chan", "seq", None, None),
        P("chan", "seq", None, None),
        P("chan", "seq", None, None),
        P("chan", "seq", None, None),
        P(None, "chan"),
        P(None, "chan"),
        P(None, "chan"),
        P(None, "chan"),
    )
    return jax.shard_map(
        body,
        mesh=mesh,
        in_specs=placed,
        out_specs=(
            P("seq", "chan"),
            P("seq", "chan"),
            P("seq", None, "chan"),
            P("seq", None, "chan"),
            P("chan", "seq"),
            P("chan", "seq"),
            P("seq", None, "chan"),
            P("seq", None, "chan"),
            P("chan", "seq"),
            P("chan", "seq"),
            P("seq", None, "chan", None, None),
            P("seq", None, "chan", None, None),
            P("seq", None, "chan", None, None),
            P("seq", None, "chan", None, None),
            P("chan", "seq", None, None),
            P("chan", "seq", None, None),
            P("chan", "seq", None, None),
            P("chan", "seq", None, None),
            P(None, "chan"),
            P(None, "chan"),
            P(None, "chan"),
            P(None, "chan"),
            P(None, "chan"),
            P(None, "chan"),
        ),
        check_vma=False,
    )
```

```python
import collections
import math

import jax
import jax.numpy as jnp
from jax import lax
from jax.experimental import pallas as pl
from jax.experimental.pallas import tpu as pltpu
from jax.sharding import PartitionSpec as P

D = 1024
STEP = 10


EPS = 1e-05
DECAY = 0.5
MATRIX_RATE = 0.5
VECTOR_RATE = 1.0
BETA_ONE = 0.9
BETA_TWO = 0.95
ADAM_EPS = 1e-08
WEIGHT_DECAY = 0.01
LOW = jnp.bfloat16
WIDE = jnp.float32
VMEM_BYTES = 56 * 1024 * 1024


def after(value, *earlier):
    return lax.optimization_barrier((value,) + earlier)[0]


def after_all(values, *earlier):
    return lax.optimization_barrier(tuple(values) + earlier)[: len(values)]


def from_behind(block, axis, distance):
    devices = range(lax.axis_size(axis))
    route = [(i - distance, i) for i in devices if i - distance in devices]
    return lax.ppermute(block, axis, route)


def swap(block, axis, bit):
    devices = range(lax.axis_size(axis))
    return lax.ppermute(block, axis, [(i, i ^ bit) for i in devices])


def all_sum(block, axis):
    bit = 1
    while bit < lax.axis_size(axis):
        block = block + swap(block, axis, bit)
        bit *= 2
    return block


def ring_order(count):
    return [2 * p if 2 * p < count else 2 * (count - p) - 1 for p in range(count)]


def ring_index(place, count):
    place = lax.rem(place + 2 * count, count)
    return jnp.where(2 * place < count, 2 * place, 2 * (count - place) - 1)


def ring_place(index, count):
    return jnp.where(lax.rem(index, 2) == 0, index // 2, count - 1 - index // 2)


def ring_send(block, step):
    order = ring_order(lax.axis_size("seq"))
    count = len(order)
    route = [(order[p], order[(p + step) % count]) for p in range(count)]
    return lax.ppermute(block, "seq", route)


def row_start(index, rows):
    quarter_rows = D // 4
    first = index * rows
    relative = (first // quarter_rows) ^ lax.axis_index("chan")
    place = (relative >> 1) | ((relative & 1) << 1)
    return place * quarter_rows + lax.rem(first, quarter_rows)


def copy_pieces(starts, pieces, whole, sems):
    copies = []
    for i, piece in enumerate(pieces):
        rows = pl.ds(pl.multiple_of(starts[i], 16), piece.shape[0])
        copies.append(pltpu.make_async_copy(piece, whole.at[rows], sems.at[i]))
    for copy in copies:
        copy.start()
    for copy in copies:
        copy.wait()


def place_kernel(starts, *refs):
    copy_pieces(starts, refs[:-2], refs[-2], refs[-1])


def placed_rows(pieces, starts):
    width = pieces[0].shape[1]
    count = len(pieces)
    total = sum(p.shape[0] for p in pieces)
    return pl.pallas_call(
        place_kernel,
        grid_spec=pltpu.PrefetchScalarGridSpec(
            num_scalar_prefetch=1,
            grid=(1,),
            in_specs=[pl.BlockSpec(memory_space=pl.ANY)] * count,
            out_specs=pl.BlockSpec((total, width), lambda i, starts: (0, 0)),
            scratch_shapes=[pltpu.SemaphoreType.DMA((count,))],
        ),
        out_shape=jax.ShapeDtypeStruct((total, width), pieces[0].dtype),
        compiler_params=pltpu.CompilerParams(vmem_limit_bytes=VMEM_BYTES),
        cost_estimate=pl.CostEstimate(
            flops=0, bytes_accessed=4 * total * width, transcendentals=0
        ),
    )(starts, *pieces)


def ring_gather(shard, *during):
    count = lax.axis_size("seq")
    place = ring_place(lax.axis_index("seq"), count)
    rows = shard.shape[0]
    pieces, starts = [], []

    def put(block, source, offset=0):
        pieces.append(block)
        starts.append(row_start(ring_index(source, count), rows) + offset)

    put(shard, place)
    ahead = behind = shard
    for step in range(1, count // 2):
        if step == 2:
            ahead, behind = after(ahead, *during), after(behind, *during)
        ahead = ring_send(ahead, 1)
        behind = ring_send(behind, -1)
        put(ahead, place - step)
        put(behind, place + step)
    half = rows // 2
    ahead = ring_send(ahead[:half], 1)
    behind = ring_send(behind[half:], -1)
    put(ahead, place - count // 2)
    put(behind, place - count // 2, half)
    return pieces, jnp.stack(starts).astype(jnp.int32)


def ring_total(partial, *later, middle=()):
    count = lax.axis_size("seq")
    place = ring_place(lax.axis_index("seq"), count)
    rows = partial.shape[0] // count
    half = rows // 2
    far = count // 2

    def own(target, offset=0, extent=rows):
        start = row_start(ring_index(target, count), rows) + offset
        return lax.dynamic_slice(partial, (start, 0), (extent, partial.shape[1]))

    ahead = ring_send(own(place + far, 0, half), 1)
    behind = ring_send(own(place - far, half, half), -1)
    for step in range(far - 1, 0, -1):
        earlier = later if step == 1 else middle if step == 2 else ()
        ahead, behind = lax.optimization_barrier((ahead, behind) + earlier)[:2]
        up, down = own(place + step).astype(WIDE), own(place - step).astype(WIDE)
        if step == far - 1:
            up = up + jnp.pad(ahead.astype(WIDE), ((0, rows - half), (0, 0)))
            down = down + jnp.pad(behind.astype(WIDE), ((half, 0), (0, 0)))
        else:
            up = up + ahead.astype(WIDE)
            down = down + behind.astype(WIDE)
        arrived = ahead, behind
        if step == 2:
            early = ahead, behind
        ahead = ring_send(up.astype(LOW), 1)
        behind = ring_send(down.astype(LOW), -1)
    return (own(place), ahead, behind), arrived, early, (up.astype(LOW), down.astype(LOW))


def spread(quarter, *earlier):
    across = swap(quarter, "chan", 2)
    pair = jnp.concatenate([quarter, after(across, *earlier)], axis=-1)
    return (pair, swap(pair, "chan", 1)), across


def far_sum(other, far):
    return (far + other[:, D // 4 :].astype(WIDE)).astype(LOW)


def near_sum(other, near, across):
    return near + other[:, : D // 4].astype(WIDE) + across.astype(WIDE)


def branch_parts(rows, matrix, *earlier):
    def product(low, high):
        return lax.dot_general(
            rows, matrix[low:high], (((1,), (1,)), ((), ())), preferred_element_type=WIDE
        )

    other = after(swap(product(D // 2, D).astype(LOW), "chan", 1), *earlier)
    sent = far_sum(other, product(D // 4, D // 2))
    return other, sent, product(0, D // 4)


def pair_kernel(rows, matrix, send_out, far_out, near_out):
    def back(low, high):
        return lax.dot_general(
            rows[...], matrix[low:high, :], (((1,), (1,)), ((), ())), preferred_element_type=WIDE
        )

    send_out[...] = back(D // 2, D).astype(LOW)
    keep = back(0, D // 2)
    near_out[...] = keep[:, : D // 4]
    far_out[...] = keep[:, D // 4 :]


def pair_parts(rows, matrix):
    tokens, depth = rows.shape
    block = 512

    def cut(extent):
        return pl.BlockSpec((block, extent), lambda i: (i, 0))

    return pl.pallas_call(
        pair_kernel,
        grid=(tokens // block,),
        in_specs=[cut(depth), pl.BlockSpec(matrix.shape, lambda i: (0, 0))],
        out_specs=[cut(D // 2), cut(D // 4), cut(D // 4)],
        out_shape=[
            jax.ShapeDtypeStruct((tokens, D // 2), LOW),
            jax.ShapeDtypeStruct((tokens, D // 4), WIDE),
            jax.ShapeDtypeStruct((tokens, D // 4), WIDE),
        ],
        compiler_params=pltpu.CompilerParams(vmem_limit_bytes=VMEM_BYTES),
        cost_estimate=pl.CostEstimate(
            flops=2 * tokens * D * depth,
            bytes_accessed=2 * matrix.size + 2 * rows.size + 6 * tokens * D // 2,
            transcendentals=0,
        ),
    )(rows, matrix)


def norm_back(grad_rows, hat_rows, inverse, gain_row, inner):
    scaled = grad_rows * gain_row[None, :]
    return (
        inverse[:, None] * (scaled - hat_rows * (inner / D)[:, None]),
        jnp.sum(grad_rows * hat_rows, axis=0),
    )


def keep_masks(starts):
    keep_one = 1.0 - starts
    before = jnp.concatenate([jnp.zeros((1,), jnp.float32), starts[:-1]])
    return (keep_one, keep_one * (1.0 - before))


def conv_taps(padded, kernel, keep_one, keep_two):
    return (
        kernel[2] * padded[2:]
        + kernel[1] * keep_one[:, None] * padded[1:-1]
        + kernel[0] * keep_two[:, None] * padded[:-2]
    )


def product(one, two, dims):
    return lax.dot_general(
        one.astype(LOW), two.astype(LOW), ((dims[:1], dims[1:]), ((), ())),
        preferred_element_type=WIDE,
    )


def summed(terms, *at):
    return terms[0][at].astype(WIDE) + terms[1][at].astype(WIDE) + terms[2][at].astype(WIDE)


Tiles = collections.namedtuple(
    "Tiles", ("kernel", "steps", "in_specs", "out_specs", "operands", "shapes")
)


def tile_update(g, left_stat, right_stat, left_root, right_root):
    low = g.astype(LOW)
    new_left = DECAY * left_stat + (1.0 - DECAY) * product(low, low, (1, 1))
    new_right = DECAY * right_stat + (1.0 - DECAY) * product(low, low, (0, 0))
    update = product(product(left_root, low, (1, 0)), right_root, (1, 0))
    return update, new_left, new_right


def column_kernel(kinds, tiles, by_kind, *refs):
    parts, rest = refs[: 3 * kinds], refs[3 * kinds :]
    weight, left, right, left_root, right_root = rest[:5]
    grad_out, weight_out, left_out, right_out = rest[5:]
    extent = right.shape[-1]
    for k in range(kinds):
        for i in range(tiles):
            columns = slice(i * extent, (i + 1) * extent)
            at = (k, slice(None), columns) if by_kind else (slice(None), k, columns)
            g = summed(parts[3 * k : 3 * k + 3], slice(None), columns)
            update, new_left, new_right = tile_update(
                g, left[0, k, i], right[0, k, i], left_root[0, k, i], right_root[0, k, i]
            )
            grad_out[at] = g
            weight_out[at] = weight[at] - MATRIX_RATE * update
            left_out[0, k, i] = new_left
            right_out[0, k, i] = new_right


def column_tiles(weight, terms, first_column, step_tiles, by_kind, *stats):
    kinds, width = stats[0].shape[1], weight.shape[2]
    rows, extent = terms[0].shape[0], stats[1].shape[-1]
    steps = width // extent // step_tiles
    step = step_tiles * extent
    begin = first_column // step

    def part(k):
        return [pl.BlockSpec((rows, step), lambda i: (0, begin + k * steps + i))] * 3

    shape = (kinds, rows, step) if by_kind else (rows, kinds, step)
    cut = pl.BlockSpec(shape, lambda i: (0, 0, i))
    stat_cuts = [
        pl.BlockSpec((1, kinds, step_tiles) + s.shape[-2:], lambda i: (0, 0, i, 0, 0))
        for s in stats
    ]
    return Tiles(
        lambda *refs: column_kernel(kinds, step_tiles, by_kind, *refs),
        steps,
        [spec for k in range(kinds) for spec in part(k)] + [cut] + stat_cuts,
        [cut, cut] + stat_cuts[:2],
        list(terms) * kinds + [weight, *stats],
        [weight.shape] * 2 + [s.shape for s in stats[:2]],
    )


def row_kernel(tiles, *refs):
    terms, weight, left, right, left_root, right_root = refs[:3], *refs[3:8]
    grad_out, weight_out, left_out, right_out = refs[8:]
    extent = left.shape[-1]
    for i in range(tiles):
        rows = slice(i * extent, (i + 1) * extent)
        g = summed(terms, slice(None), rows).T
        update, new_left, new_right = tile_update(
            g, left[i, 0], right[i, 0], left_root[i, 0], right_root[i, 0]
        )
        grad_out[rows, :] = g
        weight_out[rows, :] = weight[rows, :] - MATRIX_RATE * update
        left_out[i, 0] = new_left
        right_out[i, 0] = new_right


def row_tiles(weight, terms, first_column, step_tiles, *stats):
    extent = stats[0].shape[-1]
    columns = weight.shape[1]
    step = step_tiles * extent
    begin = first_column // step
    cut = pl.BlockSpec((step, columns), lambda i: (i, 0))
    stat_cuts = [
        pl.BlockSpec((step_tiles, 1) + s.shape[-2:], lambda i: (i, 0, 0, 0)) for s in stats
    ]
    return Tiles(
        lambda *refs: row_kernel(step_tiles, *refs),
        weight.shape[0] // step,
        [pl.BlockSpec((columns, step), lambda i: (0, begin + i))] * len(terms) + [cut] + stat_cuts,
        [cut, cut] + stat_cuts[:2],
        [*terms, weight, *stats],
        [weight.shape] * 2 + [s.shape for s in stats[:2]],
    )


def both_updates(one, two):
    assert one.steps == two.steps
    ins = len(one.operands), len(two.operands)

    def kernel(*refs):
        outs = refs[sum(ins) :]
        one.kernel(*refs[: ins[0]], *outs[:4])
        two.kernel(*refs[ins[0] : sum(ins)], *outs[4:])

    operands = one.operands + two.operands
    shapes = one.shapes + two.shapes
    size = math.prod(one.shapes[0]) + math.prod(two.shapes[0])
    new = pl.pallas_call(
        kernel,
        grid=(one.steps,),
        in_specs=one.in_specs + two.in_specs,
        out_specs=one.out_specs + two.out_specs,
        out_shape=[jax.ShapeDtypeStruct(shape, WIDE) for shape in shapes],
        compiler_params=pltpu.CompilerParams(vmem_limit_bytes=VMEM_BYTES),
        cost_estimate=pl.CostEstimate(
            flops=1024 * size, bytes_accessed=38 * size, transcendentals=0
        ),
    )(*operands)
    return new[:4], new[4:]


def shard_kernel(by_kind, column, row, out):
    kinds, width = column.shape[0 if by_kind else 1], column.shape[2]
    for k in range(kinds):
        block = column[k] if by_kind else column[:, k, :]
        out[:, k * width : (k + 1) * width] = block.astype(LOW)
    out[:, kinds * width :] = row[...].T.astype(LOW)


def low_shard(column, row, by_kind):
    rows, size = row.shape[1], column.size + row.size
    return pl.pallas_call(
        lambda *refs: shard_kernel(by_kind, *refs),
        out_shape=jax.ShapeDtypeStruct((rows, size // rows), LOW),
        compiler_params=pltpu.CompilerParams(vmem_limit_bytes=VMEM_BYTES),
        cost_estimate=pl.CostEstimate(flops=0, bytes_accessed=6 * size, transcendentals=0),
    )(column, row)


def ffn_kernel(units, starts, mine, theirs, cot_mine, cot_theirs, *refs):
    act_out, grad_out, send_out, far_out, near_out, inner_out, down_out = refs[-10:-3]
    matrix, sems, sem = refs[-3:]

    def down_copy():
        return pltpu.make_async_copy(matrix.at[:, pl.ds(2 * units, units)], down_out, sem)

    @pl.when(pl.program_id(0) == 0)
    def _():
        copy_pieces(starts, refs[:-10], matrix, sems)
        down_copy().start()

    normed = jnp.concatenate([mine[...], theirs[...]], axis=1)
    cot = jnp.concatenate([cot_mine[...], cot_theirs[...]], axis=1)
    inner = jnp.zeros((normed.shape[0], 1), WIDE)
    for low in range(0, units, 256):
        high = min(low + 256, units)
        gate = jnp.dot(normed, matrix[:, low:high], preferred_element_type=WIDE)
        up = jnp.dot(normed, matrix[:, units + low : units + high], preferred_element_type=WIDE)
        grad = jnp.dot(
            cot, matrix[:, 2 * units + low : 2 * units + high], preferred_element_type=WIDE
        )
        sigmoid = 0.5 * jnp.tanh(0.5 * gate) + 0.5
        silu = gate * sigmoid
        grad_gate = grad * up * (sigmoid + silu * (1.0 - sigmoid))
        grad_up = grad * silu
        act_out[:, low:high] = (silu * up).astype(LOW)
        grad_out[:, low:high] = grad_gate.astype(LOW)
        grad_out[:, units + low : units + high] = grad_up.astype(LOW)
        inner += jnp.sum(grad_gate * gate + grad_up * up, axis=1, keepdims=True)
    inner_out[...] = jnp.broadcast_to(inner, (inner.shape[0], 128)).T[:8]
    grads = grad_out[...]

    def back(low, high):
        return lax.dot_general(
            grads, matrix[low:high, : 2 * units], (((1,), (1,)), ((), ())),
            preferred_element_type=WIDE,
        )

    send_out[...] = back(D // 2, D).astype(LOW)
    keep = back(0, D // 2)
    near_out[...] = keep[:, : D // 4]
    far_out[...] = keep[:, D // 4 :]

    @pl.when(pl.program_id(0) == pl.num_programs(0) - 1)
    def _():
        down_copy().wait()


def ffn(features, cotangents, pieces, starts):
    tokens, units, count = features[0].shape[0], pieces[0].shape[1] // 3, len(pieces)
    block = 256

    def cut(extent):
        return pl.BlockSpec((block, extent), lambda i, starts: (i, 0))

    whole = pl.BlockSpec(memory_space=pl.ANY)
    return pl.pallas_call(
        lambda *refs: ffn_kernel(units, *refs),
        grid_spec=pltpu.PrefetchScalarGridSpec(
            num_scalar_prefetch=1,
            grid=(tokens // block,),
            in_specs=[cut(D // 2)] * 4 + [whole] * count,
            out_specs=[cut(units), cut(2 * units), cut(D // 2), cut(D // 4), cut(D // 4),
                pl.BlockSpec((8, block), lambda i, starts: (0, i)), whole],
            scratch_shapes=[
                pltpu.VMEM((D, 3 * units), LOW),
                pltpu.SemaphoreType.DMA((count,)),
                pltpu.SemaphoreType.DMA,
            ],
        ),
        out_shape=[
            jax.ShapeDtypeStruct((tokens, units), LOW),
            jax.ShapeDtypeStruct((tokens, 2 * units), LOW),
            jax.ShapeDtypeStruct((tokens, D // 2), LOW),
            jax.ShapeDtypeStruct((tokens, D // 4), WIDE),
            jax.ShapeDtypeStruct((tokens, D // 4), WIDE),
            jax.ShapeDtypeStruct((8, tokens), WIDE),
            jax.ShapeDtypeStruct((D, units), LOW),
        ],
        compiler_params=pltpu.CompilerParams(vmem_limit_bytes=VMEM_BYTES),
        cost_estimate=pl.CostEstimate(
            flops=10 * tokens * D * units,
            bytes_accessed=6 * D * units + 16 * tokens * D,
            transcendentals=tokens * units,
        ),
    )(starts, *features, *cotangents, *pieces)


def parts_kernel(split, mine, theirs, cot_mine, cot_theirs, grads, activated, out):
    j, i = pl.program_id(0), pl.program_id(1)

    def product(left, right):
        out[...] = lax.dot_general(
            left[...], right[...], (((0,), (0,)), ((), ())), preferred_element_type=WIDE
        ).astype(LOW)

    for half, left, right in ((0, mine, grads), (1, theirs, grads)):

        @pl.when((j < split) & (i == half))
        def _():
            product(left, right)

    for half, left, right in ((0, cot_mine, activated), (1, cot_theirs, activated)):

        @pl.when((j == split) & (i == half))
        def _():
            product(left, right)


def gradient_parts(features, cotangents, grads, activated):
    tokens, units = activated.shape
    split = grads.shape[1] // units
    half = pl.BlockSpec((tokens, D // 2), lambda j, i: (0, 0))
    return pl.pallas_call(
        lambda *refs: parts_kernel(split, *refs),
        grid=(split + 1, 2),
        in_specs=[half] * 4
        + [
            pl.BlockSpec((tokens, units), lambda j, i: (0, jnp.minimum(j, split - 1))),
            pl.BlockSpec((tokens, units), lambda j, i: (0, 0)),
        ],
        out_specs=pl.BlockSpec((D // 2, units), lambda j, i: (i, j)),
        out_shape=jax.ShapeDtypeStruct((D, (split + 1) * units), LOW),
        compiler_params=pltpu.CompilerParams(vmem_limit_bytes=VMEM_BYTES),
        cost_estimate=pl.CostEstimate(
            flops=2 * tokens * D * (split + 1) * units,
            bytes_accessed=4 * tokens * D,
            transcendentals=0,
        ),
    )(*features, *cotangents, grads, activated)


def adam_step(values, gradient, moment_one, second):
    moment_one = BETA_ONE * moment_one + (1.0 - BETA_ONE) * gradient
    second = BETA_TWO * second + (1.0 - BETA_TWO) * gradient * gradient
    first_hat = moment_one / (1.0 - BETA_ONE**STEP)
    second_hat = second / (1.0 - BETA_TWO**STEP)
    new_values = values - VECTOR_RATE * (
        first_hat / (jnp.sqrt(second_hat) + ADAM_EPS) + WEIGHT_DECAY * values
    )
    return (moment_one, second, new_values)


def dot(one, two, dims):
    return lax.dot_general(
        one, two, ((dims[:1], dims[1:]), ((), ())), preferred_element_type=WIDE
    )


def body(
    tokens,
    doc_starts,
    cotangent,
    gains,
    conv_kernel,
    in_proj,
    gate_up,
    out_proj,
    down_proj,
    in_left,
    in_right,
    in_left_root,
    in_right_root,
    gate_left,
    gate_right,
    gate_left_root,
    gate_right_root,
    out_left,
    out_right,
    out_left_root,
    out_right_root,
    down_left,
    down_right,
    down_left_root,
    down_right_root,
    gain_first,
    gain_second,
    kernel_first,
    kernel_second,
):
    chan_in = in_proj.shape[2]
    units = gate_up.shape[2]

    in_kinds = in_proj.transpose(1, 0, 2)
    second_shard = low_shard(gate_up, down_proj, False)
    first_pieces, first_starts = ring_gather(low_shard(in_kinds, out_proj, True), second_shard)
    tokens_halves, tokens_across = spread(tokens, *first_pieces[3:5])
    tokens_full = jnp.concatenate(tokens_halves, axis=1)
    gain_full = jnp.concatenate(spread(gains[:1])[0], axis=1)
    pieces, starts_two = ring_gather(after(second_shard, *first_pieces[-4:-2]))

    cot_halves, cot_across = spread(after(cotangent, tokens_across), pieces[1])
    wide_full = tokens_full.astype(WIDE)
    inv_one = lax.rsqrt(jnp.sum(wide_full * wide_full, axis=1) / D + EPS)
    spread_one = (wide_full * inv_one[:, None] * gain_full).astype(LOW)
    resid_in = tokens.astype(WIDE)
    hat_one = resid_in * inv_one[:, None]
    first_full = placed_rows(first_pieces, first_starts)
    in_full, out_full = first_full[:, : 3 * chan_in], first_full[:, 3 * chan_in :]
    projected = dot(spread_one, in_full, (1, 0))
    in_gate = projected[:, :chan_in]
    out_gate = projected[:, chan_in : 2 * chan_in]
    conv_input = projected[:, 2 * chan_in :]
    bx_low = (in_gate * conv_input).astype(LOW)
    starts = doc_starts.astype(WIDE)
    tail_keep = 1.0 - starts[-1]
    edge_rows = jnp.concatenate([bx_low[-2:-1] * tail_keep.astype(LOW), bx_low[-1:]], axis=0)
    carried = after(from_behind(edge_rows, "seq", 1), cot_across, *pieces[1:3])
    padded = jnp.concatenate([carried, bx_low], axis=0).astype(WIDE)
    keep_one, keep_two = keep_masks(starts)
    filtered = conv_taps(padded, conv_kernel, keep_one, keep_two)
    gated_low = (out_gate * filtered).astype(LOW)
    other, sent, near = branch_parts(gated_low, out_full)
    across = after(swap(sent, "chan", 2), *pieces[3:5])
    residual = resid_in + near_sum(other, near, across)

    squares = all_sum(jnp.sum(residual * residual, axis=1), "chan")
    inv_two = lax.rsqrt(squares / D + EPS)
    hat_two = residual * inv_two[:, None]
    normed_two = (hat_two * gains[1][None, :]).astype(LOW)
    two_halves, _ = spread(normed_two, *pieces[5:7])
    activated, grad_hidden, two_send, two_far, two_near, inner_two, down_full = ffn(
        two_halves, cot_halves, pieces, starts_two
    )
    other = swap(two_send, "chan", 1)
    sent_two = sent = far_sum(other, two_far)
    inner_two = all_sum(inner_two[0], "chan")
    second_part = gradient_parts(two_halves, cot_halves, after(grad_hidden, sent, inner_two), activated)
    across = after(swap(sent, "chan", 2), second_part, inner_two)
    grad_norm_two = near_sum(other, two_near, across)
    resid_norm, gain_two = norm_back(grad_norm_two, hat_two, inv_two, gains[1], inner_two)
    grad_resid = cotangent.astype(WIDE) + resid_norm
    mixed_send, mixed_far, mixed_near = pair_parts(after(activated, grad_resid), down_full)
    resid_halves, resid_across = spread(grad_resid.astype(LOW), mixed_send)
    resid_full = jnp.concatenate(resid_halves, axis=1)
    weights_back = jnp.stack(
        [
            conv_kernel[0] * keep_two[0] * out_gate[0],
            conv_kernel[1] * keep_one[0] * out_gate[0],
            conv_kernel[0] * keep_two[1] * out_gate[1],
        ]
    )
    weights_back = from_behind(after(weights_back, sent_two), "seq", -1)
    top_halves, _ = spread(from_behind(grad_resid[:2].astype(LOW), "seq", -1))
    top_rows = jnp.pad(jnp.concatenate(top_halves, axis=1), ((0, 6), (0, 0)))
    top_gated = dot(top_rows, out_full, (1, 0))
    grad_gated = dot(resid_full, out_full, (1, 0))
    grad_conv = grad_gated * out_gate
    grad_cpart = grad_gated * filtered
    tap_one = keep_one[:, None] * grad_conv
    tap_two = keep_two[:, None] * grad_conv
    grad_padded = (
        jnp.pad(conv_kernel[2][None, :] * grad_conv, ((2, 0), (0, 0)))
        + jnp.pad(conv_kernel[1][None, :] * tap_one, ((1, 1), (0, 0)))
        + jnp.pad(conv_kernel[0][None, :] * tap_two, ((0, 2), (0, 0)))
    )
    out_part = dot(resid_full, gated_low, (0, 0)).astype(LOW)
    returned = jnp.stack(
        [
            weights_back[0] * top_gated[0],
            weights_back[1] * top_gated[0] + weights_back[2] * top_gated[1],
        ]
    )
    edge_back = jnp.concatenate([returned[0:1] * tail_keep, returned[1:2]], axis=0)
    grad_bx = grad_padded[2:] + jnp.pad(edge_back, ((grad_conv.shape[0] - 2, 0), (0, 0)))
    grad_bx = lax.optimization_barrier(grad_bx.astype(LOW)).astype(WIDE)
    kernel_part = jnp.stack(
        [
            jnp.sum(tap_two * padded[:-2], axis=0),
            jnp.sum(tap_one * padded[1:-1], axis=0),
            jnp.sum(grad_conv * padded[2:], axis=0),
        ]
    )
    grad_proj = jnp.concatenate(
        [
            (grad_bx * conv_input).astype(LOW),
            grad_cpart.astype(LOW),
            (grad_bx * in_gate).astype(LOW),
        ],
        axis=1,
    )
    second_terms, arrived, _, _ = ring_total(after(second_part, grad_norm_two))
    other, last_sent, near = branch_parts(grad_proj, in_full)
    grad_norm_one = near_sum(other, near, swap(last_sent, "chan", 2))
    other = swap(after(mixed_send, last_sent), "chan", 1)
    sent = after(far_sum(other, mixed_far), grad_norm_one)
    mixed = (residual + near_sum(other, mixed_near, swap(sent, "chan", 2))).astype(LOW)
    inner_one = all_sum(jnp.sum(grad_proj.astype(WIDE) * projected, axis=1), "chan")
    input_norm, gain_one = norm_back(grad_norm_one, hat_one, inv_one, gains[0], inner_one)
    input_grad = grad_resid + input_norm

    in_part = dot(spread_one, grad_proj, (0, 0)).astype(LOW)
    first_part = after(jnp.concatenate([in_part, out_part], axis=1), last_sent)
    first_terms, _, early, _ = ring_total(first_part)
    second_terms = after_all(second_terms, *early)
    first_terms = after_all(first_terms, mixed)
    vector_grad = all_sum(
        jnp.concatenate([gain_one[None], gain_two[None], kernel_part], axis=0), "seq"
    )
    gain_grad, kernel_grad = vector_grad[:2], vector_grad[2:]

    (gate_grad, gate_new, gate_left_new, gate_right_new), down_outs = both_updates(
        column_tiles(
            gate_up, second_terms, 0, 3, False, gate_left, gate_right, gate_left_root,
            gate_right_root,
        ),
        row_tiles(
            down_proj, second_terms, 2 * units, 3, down_left, down_right, down_left_root,
            down_right_root,
        ),
    )
    down_grad, down_new, down_left_new, down_right_new = down_outs
    (in_grad, in_new, in_left_new, in_right_new), out_outs = both_updates(
        column_tiles(
            in_kinds, first_terms, 0, 1, True, in_left, in_right, in_left_root, in_right_root
        ),
        row_tiles(
            out_proj, first_terms, 3 * chan_in, 1, out_left, out_right, out_left_root,
            out_right_root,
        ),
    )
    out_grad, out_new, out_left_new, out_right_new = out_outs
    in_grad, in_new = in_grad.transpose(1, 0, 2), in_new.transpose(1, 0, 2)
    gain_one_new, gain_two_new, gains_new = adam_step(gains, gain_grad, gain_first, gain_second)
    kernel_one_new, kernel_two_new, kernel_new = adam_step(
        conv_kernel, kernel_grad, kernel_first, kernel_second
    )
    return (
        mixed,
        input_grad,
        in_grad,
        gate_grad,
        out_grad,
        down_grad,
        in_new,
        gate_new,
        out_new,
        down_new,
        in_left_new,
        in_right_new,
        gate_left_new,
        gate_right_new,
        out_left_new,
        out_right_new,
        down_left_new,
        down_right_new,
        gain_one_new,
        gain_two_new,
        gains_new,
        kernel_one_new,
        kernel_two_new,
        kernel_new,
    )


def solution(mesh):
    placed = (
        P("seq", "chan"),
        P("seq"),
        P("seq", "chan"),
        P(None, "chan"),
        P(None, "chan"),
        P("seq", None, "chan"),
        P("seq", None, "chan"),
        P("chan", "seq"),
        P("chan", "seq"),
        P("seq", None, "chan", None, None),
        P("seq", None, "chan", None, None),
        P("seq", None, "chan", None, None),
        P("seq", None, "chan", None, None),
        P("seq", None, "chan", None, None),
        P("seq", None, "chan", None, None),
        P("seq", None, "chan", None, None),
        P("seq", None, "chan", None, None),
        P("chan", "seq", None, None),
        P("chan", "seq", None, None),
        P("chan", "seq", None, None),
        P("chan", "seq", None, None),
        P("chan", "seq", None, None),
        P("chan", "seq", None, None),
        P("chan", "seq", None, None),
        P("chan", "seq", None, None),
        P(None, "chan"),
        P(None, "chan"),
        P(None, "chan"),
        P(None, "chan"),
    )
    return jax.shard_map(
        body,
        mesh=mesh,
        in_specs=placed,
        out_specs=(
            P("seq", "chan"),
            P("seq", "chan"),
            P("seq", None, "chan"),
            P("seq", None, "chan"),
            P("chan", "seq"),
            P("chan", "seq"),
            P("seq", None, "chan"),
            P("seq", None, "chan"),
            P("chan", "seq"),
            P("chan", "seq"),
            P("seq", None, "chan", None, None),
            P("seq", None, "chan", None, None),
            P("seq", None, "chan", None, None),
            P("seq", None, "chan", None, None),
            P("chan", "seq", None, None),
            P("chan", "seq", None, None),
            P("chan", "seq", None, None),
            P("chan", "seq", None, None),
            P(None, "chan"),
            P(None, "chan"),
            P(None, "chan"),
            P(None, "chan"),
            P(None, "chan"),
            P(None, "chan"),
        ),
        check_vma=False,
    )
```

```python
import collections
import math

import jax
import jax.numpy as jnp
from jax import lax
from jax.experimental import pallas as pl
from jax.experimental.pallas import tpu as pltpu
from jax.sharding import PartitionSpec as P

D = 1024
STEP = 10


EPS = 1e-05
DECAY = 0.5
MATRIX_RATE = 0.5
VECTOR_RATE = 1.0
BETA_ONE = 0.9
BETA_TWO = 0.95
ADAM_EPS = 1e-08
WEIGHT_DECAY = 0.01
LOW = jnp.bfloat16
WIDE = jnp.float32
VMEM_BYTES = 56 * 1024 * 1024


def after(value, *earlier):
    return lax.optimization_barrier((value,) + earlier)[0]


def after_all(values, *earlier):
    return lax.optimization_barrier(tuple(values) + earlier)[: len(values)]


def from_behind(block, axis, distance):
    devices = range(lax.axis_size(axis))
    route = [(i - distance, i) for i in devices if i - distance in devices]
    return lax.ppermute(block, axis, route)


def swap(block, axis, bit):
    devices = range(lax.axis_size(axis))
    return lax.ppermute(block, axis, [(i, i ^ bit) for i in devices])


def all_sum(block, axis):
    bit = 1
    while bit < lax.axis_size(axis):
        block = block + swap(block, axis, bit)
        bit *= 2
    return block


def ring_order(count):
    return [2 * p if 2 * p < count else 2 * (count - p) - 1 for p in range(count)]


def ring_index(place, count):
    place = lax.rem(place + 2 * count, count)
    return jnp.where(2 * place < count, 2 * place, 2 * (count - place) - 1)


def ring_place(index, count):
    return jnp.where(lax.rem(index, 2) == 0, index // 2, count - 1 - index // 2)


def ring_send(block, step):
    order = ring_order(lax.axis_size("seq"))
    count = len(order)
    route = [(order[p], order[(p + step) % count]) for p in range(count)]
    return lax.ppermute(block, "seq", route)


def row_start(index, rows):
    quarter_rows = D // 4
    first = index * rows
    relative = (first // quarter_rows) ^ lax.axis_index("chan")
    place = (relative >> 1) | ((relative & 1) << 1)
    return place * quarter_rows + lax.rem(first, quarter_rows)


def copy_pieces(starts, pieces, whole, sems):
    copies = []
    for i, piece in enumerate(pieces):
        rows = pl.ds(pl.multiple_of(starts[i], 16), piece.shape[0])
        copies.append(pltpu.make_async_copy(piece, whole.at[rows], sems.at[i]))
    for copy in copies:
        copy.start()
    for copy in copies:
        copy.wait()


def place_kernel(starts, *refs):
    copy_pieces(starts, refs[:-2], refs[-2], refs[-1])


def placed_rows(pieces, starts):
    width = pieces[0].shape[1]
    count = len(pieces)
    total = sum(p.shape[0] for p in pieces)
    return pl.pallas_call(
        place_kernel,
        grid_spec=pltpu.PrefetchScalarGridSpec(
            num_scalar_prefetch=1,
            grid=(1,),
            in_specs=[pl.BlockSpec(memory_space=pl.ANY)] * count,
            out_specs=pl.BlockSpec((total, width), lambda i, starts: (0, 0)),
            scratch_shapes=[pltpu.SemaphoreType.DMA((count,))],
        ),
        out_shape=jax.ShapeDtypeStruct((total, width), pieces[0].dtype),
        compiler_params=pltpu.CompilerParams(vmem_limit_bytes=VMEM_BYTES),
        cost_estimate=pl.CostEstimate(
            flops=0, bytes_accessed=4 * total * width, transcendentals=0
        ),
    )(starts, *pieces)


def ring_gather(shard, *during):
    count = lax.axis_size("seq")
    place = ring_place(lax.axis_index("seq"), count)
    rows = shard.shape[0]
    pieces, starts = [], []

    def put(block, source, offset=0):
        pieces.append(block)
        starts.append(row_start(ring_index(source, count), rows) + offset)

    put(shard, place)
    ahead = behind = shard
    for step in range(1, count // 2):
        if step == 2:
            ahead, behind = after(ahead, *during), after(behind, *during)
        ahead = ring_send(ahead, 1)
        behind = ring_send(behind, -1)
        put(ahead, place - step)
        put(behind, place + step)
    half = rows // 2
    ahead = ring_send(ahead[:half], 1)
    behind = ring_send(behind[half:], -1)
    put(ahead, place - count // 2)
    put(behind, place - count // 2, half)
    return pieces, jnp.stack(starts).astype(jnp.int32)


def ring_total(partial, *later, middle=()):
    count = lax.axis_size("seq")
    place = ring_place(lax.axis_index("seq"), count)
    rows = partial.shape[0] // count
    half = rows // 2
    far = count // 2

    def own(target, offset=0, extent=rows):
        start = row_start(ring_index(target, count), rows) + offset
        return lax.dynamic_slice(partial, (start, 0), (extent, partial.shape[1]))

    ahead = ring_send(own(place + far, 0, half), 1)
    behind = ring_send(own(place - far, half, half), -1)
    for step in range(far - 1, 0, -1):
        earlier = later if step == 1 else middle if step == 2 else ()
        ahead, behind = lax.optimization_barrier((ahead, behind) + earlier)[:2]
        up, down = own(place + step).astype(WIDE), own(place - step).astype(WIDE)
        if step == far - 1:
            up = up + jnp.pad(ahead.astype(WIDE), ((0, rows - half), (0, 0)))
            down = down + jnp.pad(behind.astype(WIDE), ((half, 0), (0, 0)))
        else:
            up = up + ahead.astype(WIDE)
            down = down + behind.astype(WIDE)
        arrived = ahead, behind
        if step == 2:
            early = ahead, behind
        ahead = ring_send(up.astype(LOW), 1)
        behind = ring_send(down.astype(LOW), -1)
    return (own(place), ahead, behind), arrived, early, (up.astype(LOW), down.astype(LOW))


def spread(quarter, *earlier):
    across = swap(quarter, "chan", 2)
    pair = jnp.concatenate([quarter, after(across, *earlier)], axis=-1)
    return (pair, swap(pair, "chan", 1)), across


def far_sum(other, far):
    return (far + other[:, D // 4 :].astype(WIDE)).astype(LOW)


def near_sum(other, near, across):
    return near + other[:, : D // 4].astype(WIDE) + across.astype(WIDE)


def branch_parts(rows, matrix, *earlier):
    def product(low, high):
        return lax.dot_general(
            rows, matrix[low:high], (((1,), (1,)), ((), ())), preferred_element_type=WIDE
        )

    other = after(swap(product(D // 2, D).astype(LOW), "chan", 1), *earlier)
    sent = far_sum(other, product(D // 4, D // 2))
    return other, sent, product(0, D // 4)


def pair_kernel(rows, matrix, send_out, far_out, near_out):
    def back(low, high):
        return lax.dot_general(
            rows[...], matrix[low:high, :], (((1,), (1,)), ((), ())), preferred_element_type=WIDE
        )

    send_out[...] = back(D // 2, D).astype(LOW)
    keep = back(0, D // 2)
    near_out[...] = keep[:, : D // 4]
    far_out[...] = keep[:, D // 4 :]


def pair_parts(rows, matrix):
    tokens, depth = rows.shape
    block = 512

    def cut(extent):
        return pl.BlockSpec((block, extent), lambda i: (i, 0))

    return pl.pallas_call(
        pair_kernel,
        grid=(tokens // block,),
        in_specs=[cut(depth), pl.BlockSpec(matrix.shape, lambda i: (0, 0))],
        out_specs=[cut(D // 2), cut(D // 4), cut(D // 4)],
        out_shape=[
            jax.ShapeDtypeStruct((tokens, D // 2), LOW),
            jax.ShapeDtypeStruct((tokens, D // 4), WIDE),
            jax.ShapeDtypeStruct((tokens, D // 4), WIDE),
        ],
        compiler_params=pltpu.CompilerParams(vmem_limit_bytes=VMEM_BYTES),
        cost_estimate=pl.CostEstimate(
            flops=2 * tokens * D * depth,
            bytes_accessed=2 * matrix.size + 2 * rows.size + 6 * tokens * D // 2,
            transcendentals=0,
        ),
    )(rows, matrix)


def norm_back(grad_rows, hat_rows, inverse, gain_row, inner):
    scaled = grad_rows * gain_row[None, :]
    return (
        inverse[:, None] * (scaled - hat_rows * (inner / D)[:, None]),
        jnp.sum(grad_rows * hat_rows, axis=0),
    )


def keep_masks(starts):
    keep_one = 1.0 - starts
    before = jnp.concatenate([jnp.zeros((1,), jnp.float32), starts[:-1]])
    return (keep_one, keep_one * (1.0 - before))


def conv_taps(padded, kernel, keep_one, keep_two):
    return (
        kernel[2] * padded[2:]
        + kernel[1] * keep_one[:, None] * padded[1:-1]
        + kernel[0] * keep_two[:, None] * padded[:-2]
    )


def product(one, two, dims):
    return lax.dot_general(
        one.astype(LOW), two.astype(LOW), ((dims[:1], dims[1:]), ((), ())),
        preferred_element_type=WIDE,
    )


def summed(terms, *at):
    return terms[0][at].astype(WIDE) + terms[1][at].astype(WIDE) + terms[2][at].astype(WIDE)


Tiles = collections.namedtuple(
    "Tiles", ("kernel", "steps", "in_specs", "out_specs", "operands", "shapes")
)


def tile_update(g, left_stat, right_stat, left_root, right_root):
    low = g.astype(LOW)
    new_left = DECAY * left_stat + (1.0 - DECAY) * product(low, low, (1, 1))
    new_right = DECAY * right_stat + (1.0 - DECAY) * product(low, low, (0, 0))
    update = product(product(left_root, low, (1, 0)), right_root, (1, 0))
    return update, new_left, new_right


def column_kernel(kinds, tiles, by_kind, *refs):
    parts, rest = refs[: 3 * kinds], refs[3 * kinds :]
    weight, left, right, left_root, right_root = rest[:5]
    grad_out, weight_out, left_out, right_out = rest[5:]
    extent = right.shape[-1]
    for k in range(kinds):
        for i in range(tiles):
            columns = slice(i * extent, (i + 1) * extent)
            at = (k, slice(None), columns) if by_kind else (slice(None), k, columns)
            g = summed(parts[3 * k : 3 * k + 3], slice(None), columns)
            update, new_left, new_right = tile_update(
                g, left[0, k, i], right[0, k, i], left_root[0, k, i], right_root[0, k, i]
            )
            grad_out[at] = g
            weight_out[at] = weight[at] - MATRIX_RATE * update
            left_out[0, k, i] = new_left
            right_out[0, k, i] = new_right


def column_tiles(weight, terms, first_column, step_tiles, by_kind, *stats):
    kinds, width = stats[0].shape[1], weight.shape[2]
    rows, extent = terms[0].shape[0], stats[1].shape[-1]
    steps = width // extent // step_tiles
    step = step_tiles * extent
    begin = first_column // step

    def part(k):
        return [pl.BlockSpec((rows, step), lambda i: (0, begin + k * steps + i))] * 3

    shape = (kinds, rows, step) if by_kind else (rows, kinds, step)
    cut = pl.BlockSpec(shape, lambda i: (0, 0, i))
    stat_cuts = [
        pl.BlockSpec((1, kinds, step_tiles) + s.shape[-2:], lambda i: (0, 0, i, 0, 0))
        for s in stats
    ]
    return Tiles(
        lambda *refs: column_kernel(kinds, step_tiles, by_kind, *refs),
        steps,
        [spec for k in range(kinds) for spec in part(k)] + [cut] + stat_cuts,
        [cut, cut] + stat_cuts[:2],
        list(terms) * kinds + [weight, *stats],
        [weight.shape] * 2 + [s.shape for s in stats[:2]],
    )


def row_kernel(tiles, *refs):
    terms, weight, left, right, left_root, right_root = refs[:3], *refs[3:8]
    grad_out, weight_out, left_out, right_out = refs[8:]
    extent = left.shape[-1]
    for i in range(tiles):
        rows = slice(i * extent, (i + 1) * extent)
        g = summed(terms, slice(None), rows).T
        update, new_left, new_right = tile_update(
            g, left[i, 0], right[i, 0], left_root[i, 0], right_root[i, 0]
        )
        grad_out[rows, :] = g
        weight_out[rows, :] = weight[rows, :] - MATRIX_RATE * update
        left_out[i, 0] = new_left
        right_out[i, 0] = new_right


def row_tiles(weight, terms, first_column, step_tiles, *stats):
    extent = stats[0].shape[-1]
    columns = weight.shape[1]
    step = step_tiles * extent
    begin = first_column // step
    cut = pl.BlockSpec((step, columns), lambda i: (i, 0))
    stat_cuts = [
        pl.BlockSpec((step_tiles, 1) + s.shape[-2:], lambda i: (i, 0, 0, 0)) for s in stats
    ]
    return Tiles(
        lambda *refs: row_kernel(step_tiles, *refs),
        weight.shape[0] // step,
        [pl.BlockSpec((columns, step), lambda i: (0, begin + i))] * len(terms) + [cut] + stat_cuts,
        [cut, cut] + stat_cuts[:2],
        [*terms, weight, *stats],
        [weight.shape] * 2 + [s.shape for s in stats[:2]],
    )


def both_updates(one, two):
    assert one.steps == two.steps
    ins = len(one.operands), len(two.operands)

    def kernel(*refs):
        outs = refs[sum(ins) :]
        one.kernel(*refs[: ins[0]], *outs[:4])
        two.kernel(*refs[ins[0] : sum(ins)], *outs[4:])

    operands = one.operands + two.operands
    shapes = one.shapes + two.shapes
    size = math.prod(one.shapes[0]) + math.prod(two.shapes[0])
    new = pl.pallas_call(
        kernel,
        grid=(one.steps,),
        in_specs=one.in_specs + two.in_specs,
        out_specs=one.out_specs + two.out_specs,
        out_shape=[jax.ShapeDtypeStruct(shape, WIDE) for shape in shapes],
        compiler_params=pltpu.CompilerParams(vmem_limit_bytes=VMEM_BYTES),
        cost_estimate=pl.CostEstimate(
            flops=1024 * size, bytes_accessed=38 * size, transcendentals=0
        ),
    )(*operands)
    return new[:4], new[4:]


def shard_kernel(by_kind, column, row, out):
    kinds, width = column.shape[0 if by_kind else 1], column.shape[2]
    for k in range(kinds):
        block = column[k] if by_kind else column[:, k, :]
        out[:, k * width : (k + 1) * width] = block.astype(LOW)
    out[:, kinds * width :] = row[...].T.astype(LOW)


def low_shard(column, row, by_kind):
    rows, size = row.shape[1], column.size + row.size
    return pl.pallas_call(
        lambda *refs: shard_kernel(by_kind, *refs),
        out_shape=jax.ShapeDtypeStruct((rows, size // rows), LOW),
        compiler_params=pltpu.CompilerParams(vmem_limit_bytes=VMEM_BYTES),
        cost_estimate=pl.CostEstimate(flops=0, bytes_accessed=6 * size, transcendentals=0),
    )(column, row)


def ffn_kernel(units, starts, mine, theirs, cot_mine, cot_theirs, *refs):
    act_out, grad_out, send_out, far_out, near_out, inner_out, down_out = refs[-10:-3]
    matrix, sems, sem = refs[-3:]

    def down_copy():
        return pltpu.make_async_copy(matrix.at[:, pl.ds(2 * units, units)], down_out, sem)

    @pl.when(pl.program_id(0) == 0)
    def _():
        copy_pieces(starts, refs[:-10], matrix, sems)
        down_copy().start()

    normed = jnp.concatenate([mine[...], theirs[...]], axis=1)
    cot = jnp.concatenate([cot_mine[...], cot_theirs[...]], axis=1)
    inner = jnp.zeros((normed.shape[0], 1), WIDE)
    for low in range(0, units, 256):
        high = min(low + 256, units)
        gate = jnp.dot(normed, matrix[:, low:high], preferred_element_type=WIDE)
        up = jnp.dot(normed, matrix[:, units + low : units + high], preferred_element_type=WIDE)
        grad = jnp.dot(
            cot, matrix[:, 2 * units + low : 2 * units + high], preferred_element_type=WIDE
        )
        sigmoid = 0.5 * jnp.tanh(0.5 * gate) + 0.5
        silu = gate * sigmoid
        grad_gate = grad * up * (sigmoid + silu * (1.0 - sigmoid))
        grad_up = grad * silu
        act_out[:, low:high] = (silu * up).astype(LOW)
        grad_out[:, low:high] = grad_gate.astype(LOW)
        grad_out[:, units + low : units + high] = grad_up.astype(LOW)
        inner += jnp.sum(grad_gate * gate + grad_up * up, axis=1, keepdims=True)
    inner_out[...] = jnp.broadcast_to(inner, (inner.shape[0], 128)).T[:8]
    grads = grad_out[...]

    def back(low, high):
        return lax.dot_general(
            grads, matrix[low:high, : 2 * units], (((1,), (1,)), ((), ())),
            preferred_element_type=WIDE,
        )

    send_out[...] = back(D // 2, D).astype(LOW)
    keep = back(0, D // 2)
    near_out[...] = keep[:, : D // 4]
    far_out[...] = keep[:, D // 4 :]

    @pl.when(pl.program_id(0) == pl.num_programs(0) - 1)
    def _():
        down_copy().wait()


def ffn(features, cotangents, pieces, starts):
    tokens, units, count = features[0].shape[0], pieces[0].shape[1] // 3, len(pieces)
    block = 256

    def cut(extent):
        return pl.BlockSpec((block, extent), lambda i, starts: (i, 0))

    whole = pl.BlockSpec(memory_space=pl.ANY)
    return pl.pallas_call(
        lambda *refs: ffn_kernel(units, *refs),
        grid_spec=pltpu.PrefetchScalarGridSpec(
            num_scalar_prefetch=1,
            grid=(tokens // block,),
            in_specs=[cut(D // 2)] * 4 + [whole] * count,
            out_specs=[cut(units), cut(2 * units), cut(D // 2), cut(D // 4), cut(D // 4),
                pl.BlockSpec((8, block), lambda i, starts: (0, i)), whole],
            scratch_shapes=[
                pltpu.VMEM((D, 3 * units), LOW),
                pltpu.SemaphoreType.DMA((count,)),
                pltpu.SemaphoreType.DMA,
            ],
        ),
        out_shape=[
            jax.ShapeDtypeStruct((tokens, units), LOW),
            jax.ShapeDtypeStruct((tokens, 2 * units), LOW),
            jax.ShapeDtypeStruct((tokens, D // 2), LOW),
            jax.ShapeDtypeStruct((tokens, D // 4), WIDE),
            jax.ShapeDtypeStruct((tokens, D // 4), WIDE),
            jax.ShapeDtypeStruct((8, tokens), WIDE),
            jax.ShapeDtypeStruct((D, units), LOW),
        ],
        compiler_params=pltpu.CompilerParams(vmem_limit_bytes=VMEM_BYTES),
        cost_estimate=pl.CostEstimate(
            flops=10 * tokens * D * units,
            bytes_accessed=6 * D * units + 16 * tokens * D,
            transcendentals=tokens * units,
        ),
    )(starts, *features, *cotangents, *pieces)


def parts_kernel(split, mine, theirs, cot_mine, cot_theirs, grads, activated, out):
    j, i = pl.program_id(0), pl.program_id(1)

    def product(left, right):
        out[...] = lax.dot_general(
            left[...], right[...], (((0,), (0,)), ((), ())), preferred_element_type=WIDE
        ).astype(LOW)

    for half, left, right in ((0, mine, grads), (1, theirs, grads)):

        @pl.when((j < split) & (i == half))
        def _():
            product(left, right)

    for half, left, right in ((0, cot_mine, activated), (1, cot_theirs, activated)):

        @pl.when((j == split) & (i == half))
        def _():
            product(left, right)


def gradient_parts(features, cotangents, grads, activated):
    tokens, units = activated.shape
    split = grads.shape[1] // units
    half = pl.BlockSpec((tokens, D // 2), lambda j, i: (0, 0))
    return pl.pallas_call(
        lambda *refs: parts_kernel(split, *refs),
        grid=(split + 1, 2),
        in_specs=[half] * 4
        + [
            pl.BlockSpec((tokens, units), lambda j, i: (0, jnp.minimum(j, split - 1))),
            pl.BlockSpec((tokens, units), lambda j, i: (0, 0)),
        ],
        out_specs=pl.BlockSpec((D // 2, units), lambda j, i: (i, j)),
        out_shape=jax.ShapeDtypeStruct((D, (split + 1) * units), LOW),
        compiler_params=pltpu.CompilerParams(vmem_limit_bytes=VMEM_BYTES),
        cost_estimate=pl.CostEstimate(
            flops=2 * tokens * D * (split + 1) * units,
            bytes_accessed=4 * tokens * D,
            transcendentals=0,
        ),
    )(*features, *cotangents, grads, activated)


def adam_step(values, gradient, moment_one, second):
    moment_one = BETA_ONE * moment_one + (1.0 - BETA_ONE) * gradient
    second = BETA_TWO * second + (1.0 - BETA_TWO) * gradient * gradient
    first_hat = moment_one / (1.0 - BETA_ONE**STEP)
    second_hat = second / (1.0 - BETA_TWO**STEP)
    new_values = values - VECTOR_RATE * (
        first_hat / (jnp.sqrt(second_hat) + ADAM_EPS) + WEIGHT_DECAY * values
    )
    return (moment_one, second, new_values)


def dot(one, two, dims):
    return lax.dot_general(
        one, two, ((dims[:1], dims[1:]), ((), ())), preferred_element_type=WIDE
    )


def body(
    tokens,
    doc_starts,
    cotangent,
    gains,
    conv_kernel,
    in_proj,
    gate_up,
    out_proj,
    down_proj,
    in_left,
    in_right,
    in_left_root,
    in_right_root,
    gate_left,
    gate_right,
    gate_left_root,
    gate_right_root,
    out_left,
    out_right,
    out_left_root,
    out_right_root,
    down_left,
    down_right,
    down_left_root,
    down_right_root,
    gain_first,
    gain_second,
    kernel_first,
    kernel_second,
):
    chan_in = in_proj.shape[2]
    units = gate_up.shape[2]

    in_kinds = in_proj.transpose(1, 0, 2)
    second_shard = low_shard(gate_up, down_proj, False)
    first_pieces, first_starts = ring_gather(low_shard(in_kinds, out_proj, True), second_shard)
    tokens_halves, tokens_across = spread(tokens, *first_pieces[3:5])
    tokens_full = jnp.concatenate(tokens_halves, axis=1)
    gain_full = jnp.concatenate(spread(gains[:1])[0], axis=1)
    pieces, starts_two = ring_gather(after(second_shard, *first_pieces[-4:-2]))

    cot_halves, cot_across = spread(after(cotangent, tokens_across), pieces[1])
    wide_full = tokens_full.astype(WIDE)
    inv_one = lax.rsqrt(jnp.sum(wide_full * wide_full, axis=1) / D + EPS)
    spread_one = (wide_full * inv_one[:, None] * gain_full).astype(LOW)
    resid_in = tokens.astype(WIDE)
    hat_one = resid_in * inv_one[:, None]
    first_full = placed_rows(first_pieces, first_starts)
    in_full, out_full = first_full[:, : 3 * chan_in], first_full[:, 3 * chan_in :]
    projected = dot(spread_one, in_full, (1, 0))
    in_gate = projected[:, :chan_in]
    out_gate = projected[:, chan_in : 2 * chan_in]
    conv_input = projected[:, 2 * chan_in :]
    bx_low = (in_gate * conv_input).astype(LOW)
    starts = doc_starts.astype(WIDE)
    tail_keep = 1.0 - starts[-1]
    edge_rows = jnp.concatenate([bx_low[-2:-1] * tail_keep.astype(LOW), bx_low[-1:]], axis=0)
    carried = after(from_behind(edge_rows, "seq", 1), cot_across, *pieces[1:3])
    padded = jnp.concatenate([carried, bx_low], axis=0).astype(WIDE)
    keep_one, keep_two = keep_masks(starts)
    filtered = conv_taps(padded, conv_kernel, keep_one, keep_two)
    gated_low = (out_gate * filtered).astype(LOW)
    other, sent, near = branch_parts(gated_low, out_full)
    across = after(swap(sent, "chan", 2), *pieces[3:5])
    residual = resid_in + near_sum(other, near, across)

    squares = all_sum(jnp.sum(residual * residual, axis=1), "chan")
    inv_two = lax.rsqrt(squares / D + EPS)
    hat_two = residual * inv_two[:, None]
    normed_two = (hat_two * gains[1][None, :]).astype(LOW)
    two_halves, _ = spread(normed_two, *pieces[5:7])
    activated, grad_hidden, two_send, two_far, two_near, inner_two, down_full = ffn(
        two_halves, cot_halves, pieces, starts_two
    )
    other = swap(two_send, "chan", 1)
    sent_two = sent = far_sum(other, two_far)
    inner_two = all_sum(inner_two[0], "chan")
    weights_back = jnp.stack(
        [
            conv_kernel[0] * keep_two[0] * out_gate[0],
            conv_kernel[1] * keep_one[0] * out_gate[0],
            conv_kernel[0] * keep_two[1] * out_gate[1],
        ]
    )
    weights_back = from_behind(after(weights_back, sent_two), "seq", -1)
    second_part = gradient_parts(two_halves, cot_halves, after(grad_hidden, sent, inner_two), activated)
    across = after(swap(sent, "chan", 2), second_part, inner_two, weights_back)
    grad_norm_two = near_sum(other, two_near, across)
    resid_norm, gain_two = norm_back(grad_norm_two, hat_two, inv_two, gains[1], inner_two)
    grad_resid = cotangent.astype(WIDE) + resid_norm
    mixed_send, mixed_far, mixed_near = pair_parts(after(activated, grad_resid), down_full)
    resid_halves, resid_across = spread(grad_resid.astype(LOW), mixed_send)
    resid_full = jnp.concatenate(resid_halves, axis=1)
    top_halves, _ = spread(from_behind(grad_resid[:2].astype(LOW), "seq", -1))
    top_rows = jnp.pad(jnp.concatenate(top_halves, axis=1), ((0, 6), (0, 0)))
    top_gated = dot(top_rows, out_full, (1, 0))
    grad_gated = dot(resid_full, out_full, (1, 0))
    grad_conv = grad_gated * out_gate
    grad_cpart = grad_gated * filtered
    tap_one = keep_one[:, None] * grad_conv
    tap_two = keep_two[:, None] * grad_conv
    grad_padded = (
        jnp.pad(conv_kernel[2][None, :] * grad_conv, ((2, 0), (0, 0)))
        + jnp.pad(conv_kernel[1][None, :] * tap_one, ((1, 1), (0, 0)))
        + jnp.pad(conv_kernel[0][None, :] * tap_two, ((0, 2), (0, 0)))
    )
    out_part = dot(resid_full, gated_low, (0, 0)).astype(LOW)
    returned = jnp.stack(
        [
            weights_back[0] * top_gated[0],
            weights_back[1] * top_gated[0] + weights_back[2] * top_gated[1],
        ]
    )
    edge_back = jnp.concatenate([returned[0:1] * tail_keep, returned[1:2]], axis=0)
    grad_bx = grad_padded[2:] + jnp.pad(edge_back, ((grad_conv.shape[0] - 2, 0), (0, 0)))
    grad_bx = lax.optimization_barrier(grad_bx.astype(LOW)).astype(WIDE)
    kernel_part = jnp.stack(
        [
            jnp.sum(tap_two * padded[:-2], axis=0),
            jnp.sum(tap_one * padded[1:-1], axis=0),
            jnp.sum(grad_conv * padded[2:], axis=0),
        ]
    )
    grad_proj = jnp.concatenate(
        [
            (grad_bx * conv_input).astype(LOW),
            grad_cpart.astype(LOW),
            (grad_bx * in_gate).astype(LOW),
        ],
        axis=1,
    )
    second_terms, arrived, _, _ = ring_total(after(second_part, grad_norm_two))
    other, last_sent, near = branch_parts(grad_proj, in_full)
    grad_norm_one = near_sum(other, near, swap(last_sent, "chan", 2))
    other = swap(after(mixed_send, last_sent), "chan", 1)
    sent = after(far_sum(other, mixed_far), grad_norm_one)
    mixed = (residual + near_sum(other, mixed_near, swap(sent, "chan", 2))).astype(LOW)
    inner_one = all_sum(jnp.sum(grad_proj.astype(WIDE) * projected, axis=1), "chan")
    input_norm, gain_one = norm_back(grad_norm_one, hat_one, inv_one, gains[0], inner_one)
    input_grad = grad_resid + input_norm

    in_part = dot(spread_one, grad_proj, (0, 0)).astype(LOW)
    first_part = after(jnp.concatenate([in_part, out_part], axis=1), last_sent)
    first_terms, _, early, _ = ring_total(first_part)
    second_terms = after_all(second_terms, *early)
    first_terms = after_all(first_terms, mixed)
    vector_grad = all_sum(
        jnp.concatenate([gain_one[None], gain_two[None], kernel_part], axis=0), "seq"
    )
    gain_grad, kernel_grad = vector_grad[:2], vector_grad[2:]

    (gate_grad, gate_new, gate_left_new, gate_right_new), down_outs = both_updates(
        column_tiles(
            gate_up, second_terms, 0, 3, False, gate_left, gate_right, gate_left_root,
            gate_right_root,
        ),
        row_tiles(
            down_proj, second_terms, 2 * units, 3, down_left, down_right, down_left_root,
            down_right_root,
        ),
    )
    down_grad, down_new, down_left_new, down_right_new = down_outs
    (in_grad, in_new, in_left_new, in_right_new), out_outs = both_updates(
        column_tiles(
            in_kinds, first_terms, 0, 1, True, in_left, in_right, in_left_root, in_right_root
        ),
        row_tiles(
            out_proj, first_terms, 3 * chan_in, 1, out_left, out_right, out_left_root,
            out_right_root,
        ),
    )
    out_grad, out_new, out_left_new, out_right_new = out_outs
    in_grad, in_new = in_grad.transpose(1, 0, 2), in_new.transpose(1, 0, 2)
    gain_one_new, gain_two_new, gains_new = adam_step(gains, gain_grad, gain_first, gain_second)
    kernel_one_new, kernel_two_new, kernel_new = adam_step(
        conv_kernel, kernel_grad, kernel_first, kernel_second
    )
    return (
        mixed,
        input_grad,
        in_grad,
        gate_grad,
        out_grad,
        down_grad,
        in_new,
        gate_new,
        out_new,
        down_new,
        in_left_new,
        in_right_new,
        gate_left_new,
        gate_right_new,
        out_left_new,
        out_right_new,
        down_left_new,
        down_right_new,
        gain_one_new,
        gain_two_new,
        gains_new,
        kernel_one_new,
        kernel_two_new,
        kernel_new,
    )


def solution(mesh):
    placed = (
        P("seq", "chan"),
        P("seq"),
        P("seq", "chan"),
        P(None, "chan"),
        P(None, "chan"),
        P("seq", None, "chan"),
        P("seq", None, "chan"),
        P("chan", "seq"),
        P("chan", "seq"),
        P("seq", None, "chan", None, None),
        P("seq", None, "chan", None, None),
        P("seq", None, "chan", None, None),
        P("seq", None, "chan", None, None),
        P("seq", None, "chan", None, None),
        P("seq", None, "chan", None, None),
        P("seq", None, "chan", None, None),
        P("seq", None, "chan", None, None),
        P("chan", "seq", None, None),
        P("chan", "seq", None, None),
        P("chan", "seq", None, None),
        P("chan", "seq", None, None),
        P("chan", "seq", None, None),
        P("chan", "seq", None, None),
        P("chan", "seq", None, None),
        P("chan", "seq", None, None),
        P(None, "chan"),
        P(None, "chan"),
        P(None, "chan"),
        P(None, "chan"),
    )
    return jax.shard_map(
        body,
        mesh=mesh,
        in_specs=placed,
        out_specs=(
            P("seq", "chan"),
            P("seq", "chan"),
            P("seq", None, "chan"),
            P("seq", None, "chan"),
            P("chan", "seq"),
            P("chan", "seq"),
            P("seq", None, "chan"),
            P("seq", None, "chan"),
            P("chan", "seq"),
            P("chan", "seq"),
            P("seq", None, "chan", None, None),
            P("seq", None, "chan", None, None),
            P("seq", None, "chan", None, None),
            P("seq", None, "chan", None, None),
            P("chan", "seq", None, None),
            P("chan", "seq", None, None),
            P("chan", "seq", None, None),
            P("chan", "seq", None, None),
            P(None, "chan"),
            P(None, "chan"),
            P(None, "chan"),
            P(None, "chan"),
            P(None, "chan"),
            P(None, "chan"),
        ),
        check_vma=False,
    )
```

```python
import collections
import math

import jax
import jax.numpy as jnp
from jax import lax
from jax.experimental import pallas as pl
from jax.experimental.pallas import tpu as pltpu
from jax.sharding import PartitionSpec as P

D = 1024
STEP = 10


EPS = 1e-05
DECAY = 0.5
MATRIX_RATE = 0.5
VECTOR_RATE = 1.0
BETA_ONE = 0.9
BETA_TWO = 0.95
ADAM_EPS = 1e-08
WEIGHT_DECAY = 0.01
LOW = jnp.bfloat16
WIDE = jnp.float32
VMEM_BYTES = 56 * 1024 * 1024


def after(value, *earlier):
    return lax.optimization_barrier((value,) + earlier)[0]


def after_all(values, *earlier):
    return lax.optimization_barrier(tuple(values) + earlier)[: len(values)]


def from_behind(block, axis, distance):
    devices = range(lax.axis_size(axis))
    route = [(i - distance, i) for i in devices if i - distance in devices]
    return lax.ppermute(block, axis, route)


def swap(block, axis, bit):
    devices = range(lax.axis_size(axis))
    return lax.ppermute(block, axis, [(i, i ^ bit) for i in devices])


def all_sum(block, axis):
    bit = 1
    while bit < lax.axis_size(axis):
        block = block + swap(block, axis, bit)
        bit *= 2
    return block


def ring_order(count):
    return [2 * p if 2 * p < count else 2 * (count - p) - 1 for p in range(count)]


def ring_index(place, count):
    place = lax.rem(place + 2 * count, count)
    return jnp.where(2 * place < count, 2 * place, 2 * (count - place) - 1)


def ring_place(index, count):
    return jnp.where(lax.rem(index, 2) == 0, index // 2, count - 1 - index // 2)


def ring_send(block, step):
    order = ring_order(lax.axis_size("seq"))
    count = len(order)
    route = [(order[p], order[(p + step) % count]) for p in range(count)]
    return lax.ppermute(block, "seq", route)


def row_start(index, rows):
    quarter_rows = D // 4
    first = index * rows
    relative = (first // quarter_rows) ^ lax.axis_index("chan")
    place = (relative >> 1) | ((relative & 1) << 1)
    return place * quarter_rows + lax.rem(first, quarter_rows)


def copy_pieces(starts, pieces, whole, sems):
    copies = []
    for i, piece in enumerate(pieces):
        rows = pl.ds(pl.multiple_of(starts[i], 16), piece.shape[0])
        copies.append(pltpu.make_async_copy(piece, whole.at[rows], sems.at[i]))
    for copy in copies:
        copy.start()
    for copy in copies:
        copy.wait()


def place_kernel(starts, *refs):
    copy_pieces(starts, refs[:-2], refs[-2], refs[-1])


def placed_rows(pieces, starts):
    width = pieces[0].shape[1]
    count = len(pieces)
    total = sum(p.shape[0] for p in pieces)
    return pl.pallas_call(
        place_kernel,
        grid_spec=pltpu.PrefetchScalarGridSpec(
            num_scalar_prefetch=1,
            grid=(1,),
            in_specs=[pl.BlockSpec(memory_space=pl.ANY)] * count,
            out_specs=pl.BlockSpec((total, width), lambda i, starts: (0, 0)),
            scratch_shapes=[pltpu.SemaphoreType.DMA((count,))],
        ),
        out_shape=jax.ShapeDtypeStruct((total, width), pieces[0].dtype),
        compiler_params=pltpu.CompilerParams(vmem_limit_bytes=VMEM_BYTES),
        cost_estimate=pl.CostEstimate(
            flops=0, bytes_accessed=4 * total * width, transcendentals=0
        ),
    )(starts, *pieces)


def ring_gather(shard, *during):
    count = lax.axis_size("seq")
    place = ring_place(lax.axis_index("seq"), count)
    rows = shard.shape[0]
    pieces, starts = [], []

    def put(block, source, offset=0):
        pieces.append(block)
        starts.append(row_start(ring_index(source, count), rows) + offset)

    put(shard, place)
    ahead = behind = shard
    for step in range(1, count // 2):
        if step == 2:
            ahead, behind = after(ahead, *during), after(behind, *during)
        ahead = ring_send(ahead, 1)
        behind = ring_send(behind, -1)
        put(ahead, place - step)
        put(behind, place + step)
    half = rows // 2
    ahead = ring_send(ahead[:half], 1)
    behind = ring_send(behind[half:], -1)
    put(ahead, place - count // 2)
    put(behind, place - count // 2, half)
    return pieces, jnp.stack(starts).astype(jnp.int32)


def ring_total(partial, *later, middle=()):
    count = lax.axis_size("seq")
    place = ring_place(lax.axis_index("seq"), count)
    rows = partial.shape[0] // count
    half = rows // 2
    far = count // 2

    def own(target, offset=0, extent=rows):
        start = row_start(ring_index(target, count), rows) + offset
        return lax.dynamic_slice(partial, (start, 0), (extent, partial.shape[1]))

    ahead = ring_send(own(place + far, 0, half), 1)
    behind = ring_send(own(place - far, half, half), -1)
    for step in range(far - 1, 0, -1):
        earlier = later if step == 1 else middle if step == 2 else ()
        ahead, behind = lax.optimization_barrier((ahead, behind) + earlier)[:2]
        up, down = own(place + step).astype(WIDE), own(place - step).astype(WIDE)
        if step == far - 1:
            up = up + jnp.pad(ahead.astype(WIDE), ((0, rows - half), (0, 0)))
            down = down + jnp.pad(behind.astype(WIDE), ((half, 0), (0, 0)))
        else:
            up = up + ahead.astype(WIDE)
            down = down + behind.astype(WIDE)
        arrived = ahead, behind
        if step == 2:
            early = ahead, behind
        ahead = ring_send(up.astype(LOW), 1)
        behind = ring_send(down.astype(LOW), -1)
    return (own(place), ahead, behind), arrived, early, (up.astype(LOW), down.astype(LOW))


def spread(quarter, *earlier):
    across = swap(quarter, "chan", 2)
    pair = jnp.concatenate([quarter, after(across, *earlier)], axis=-1)
    return (pair, swap(pair, "chan", 1)), across


def far_sum(other, far):
    return (far + other[:, D // 4 :].astype(WIDE)).astype(LOW)


def near_sum(other, near, across):
    return near + other[:, : D // 4].astype(WIDE) + across.astype(WIDE)


def branch_parts(rows, matrix, *earlier):
    def product(low, high):
        return lax.dot_general(
            rows, matrix[low:high], (((1,), (1,)), ((), ())), preferred_element_type=WIDE
        )

    other = after(swap(product(D // 2, D).astype(LOW), "chan", 1), *earlier)
    sent = far_sum(other, product(D // 4, D // 2))
    return other, sent, product(0, D // 4)


def pair_kernel(rows, matrix, send_out, far_out, near_out):
    def back(low, high):
        return lax.dot_general(
            rows[...], matrix[low:high, :], (((1,), (1,)), ((), ())), preferred_element_type=WIDE
        )

    send_out[...] = back(D // 2, D).astype(LOW)
    keep = back(0, D // 2)
    near_out[...] = keep[:, : D // 4]
    far_out[...] = keep[:, D // 4 :]


def pair_parts(rows, matrix):
    tokens, depth = rows.shape
    block = 512

    def cut(extent):
        return pl.BlockSpec((block, extent), lambda i: (i, 0))

    return pl.pallas_call(
        pair_kernel,
        grid=(tokens // block,),
        in_specs=[cut(depth), pl.BlockSpec(matrix.shape, lambda i: (0, 0))],
        out_specs=[cut(D // 2), cut(D // 4), cut(D // 4)],
        out_shape=[
            jax.ShapeDtypeStruct((tokens, D // 2), LOW),
            jax.ShapeDtypeStruct((tokens, D // 4), WIDE),
            jax.ShapeDtypeStruct((tokens, D // 4), WIDE),
        ],
        compiler_params=pltpu.CompilerParams(vmem_limit_bytes=VMEM_BYTES),
        cost_estimate=pl.CostEstimate(
            flops=2 * tokens * D * depth,
            bytes_accessed=2 * matrix.size + 2 * rows.size + 6 * tokens * D // 2,
            transcendentals=0,
        ),
    )(rows, matrix)


def norm_back(grad_rows, hat_rows, inverse, gain_row, inner):
    scaled = grad_rows * gain_row[None, :]
    return (
        inverse[:, None] * (scaled - hat_rows * (inner / D)[:, None]),
        jnp.sum(grad_rows * hat_rows, axis=0),
    )


def keep_masks(starts):
    keep_one = 1.0 - starts
    before = jnp.concatenate([jnp.zeros((1,), jnp.float32), starts[:-1]])
    return (keep_one, keep_one * (1.0 - before))


def conv_taps(padded, kernel, keep_one, keep_two):
    return (
        kernel[2] * padded[2:]
        + kernel[1] * keep_one[:, None] * padded[1:-1]
        + kernel[0] * keep_two[:, None] * padded[:-2]
    )


def product(one, two, dims):
    return lax.dot_general(
        one.astype(LOW), two.astype(LOW), ((dims[:1], dims[1:]), ((), ())),
        preferred_element_type=WIDE,
    )


def summed(terms, *at):
    return terms[0][at].astype(WIDE) + terms[1][at].astype(WIDE) + terms[2][at].astype(WIDE)


Tiles = collections.namedtuple(
    "Tiles", ("kernel", "steps", "in_specs", "out_specs", "operands", "shapes")
)


def tile_update(g, left_stat, right_stat, left_root, right_root):
    low = g.astype(LOW)
    new_left = DECAY * left_stat + (1.0 - DECAY) * product(low, low, (1, 1))
    new_right = DECAY * right_stat + (1.0 - DECAY) * product(low, low, (0, 0))
    update = product(product(left_root, low, (1, 0)), right_root, (1, 0))
    return update, new_left, new_right


def column_kernel(kinds, tiles, by_kind, *refs):
    parts, rest = refs[: 3 * kinds], refs[3 * kinds :]
    weight, left, right, left_root, right_root = rest[:5]
    grad_out, weight_out, left_out, right_out = rest[5:]
    extent = right.shape[-1]
    for k in range(kinds):
        for i in range(tiles):
            columns = slice(i * extent, (i + 1) * extent)
            at = (k, slice(None), columns) if by_kind else (slice(None), k, columns)
            g = summed(parts[3 * k : 3 * k + 3], slice(None), columns)
            update, new_left, new_right = tile_update(
                g, left[0, k, i], right[0, k, i], left_root[0, k, i], right_root[0, k, i]
            )
            grad_out[at] = g
            weight_out[at] = weight[at] - MATRIX_RATE * update
            left_out[0, k, i] = new_left
            right_out[0, k, i] = new_right


def column_tiles(weight, terms, first_column, step_tiles, by_kind, *stats):
    kinds, width = stats[0].shape[1], weight.shape[2]
    rows, extent = terms[0].shape[0], stats[1].shape[-1]
    steps = width // extent // step_tiles
    step = step_tiles * extent
    begin = first_column // step

    def part(k):
        return [pl.BlockSpec((rows, step), lambda i: (0, begin + k * steps + i))] * 3

    shape = (kinds, rows, step) if by_kind else (rows, kinds, step)
    cut = pl.BlockSpec(shape, lambda i: (0, 0, i))
    stat_cuts = [
        pl.BlockSpec((1, kinds, step_tiles) + s.shape[-2:], lambda i: (0, 0, i, 0, 0))
        for s in stats
    ]
    return Tiles(
        lambda *refs: column_kernel(kinds, step_tiles, by_kind, *refs),
        steps,
        [spec for k in range(kinds) for spec in part(k)] + [cut] + stat_cuts,
        [cut, cut] + stat_cuts[:2],
        list(terms) * kinds + [weight, *stats],
        [weight.shape] * 2 + [s.shape for s in stats[:2]],
    )


def row_kernel(tiles, *refs):
    terms, weight, left, right, left_root, right_root = refs[:3], *refs[3:8]
    grad_out, weight_out, left_out, right_out = refs[8:]
    extent = left.shape[-1]
    for i in range(tiles):
        rows = slice(i * extent, (i + 1) * extent)
        g = summed(terms, slice(None), rows).T
        update, new_left, new_right = tile_update(
            g, left[i, 0], right[i, 0], left_root[i, 0], right_root[i, 0]
        )
        grad_out[rows, :] = g
        weight_out[rows, :] = weight[rows, :] - MATRIX_RATE * update
        left_out[i, 0] = new_left
        right_out[i, 0] = new_right


def row_tiles(weight, terms, first_column, step_tiles, *stats):
    extent = stats[0].shape[-1]
    columns = weight.shape[1]
    step = step_tiles * extent
    begin = first_column // step
    cut = pl.BlockSpec((step, columns), lambda i: (i, 0))
    stat_cuts = [
        pl.BlockSpec((step_tiles, 1) + s.shape[-2:], lambda i: (i, 0, 0, 0)) for s in stats
    ]
    return Tiles(
        lambda *refs: row_kernel(step_tiles, *refs),
        weight.shape[0] // step,
        [pl.BlockSpec((columns, step), lambda i: (0, begin + i))] * len(terms) + [cut] + stat_cuts,
        [cut, cut] + stat_cuts[:2],
        [*terms, weight, *stats],
        [weight.shape] * 2 + [s.shape for s in stats[:2]],
    )


def both_updates(one, two):
    assert one.steps == two.steps
    ins = len(one.operands), len(two.operands)

    def kernel(*refs):
        outs = refs[sum(ins) :]
        one.kernel(*refs[: ins[0]], *outs[:4])
        two.kernel(*refs[ins[0] : sum(ins)], *outs[4:])

    operands = one.operands + two.operands
    shapes = one.shapes + two.shapes
    size = math.prod(one.shapes[0]) + math.prod(two.shapes[0])
    new = pl.pallas_call(
        kernel,
        grid=(one.steps,),
        in_specs=one.in_specs + two.in_specs,
        out_specs=one.out_specs + two.out_specs,
        out_shape=[jax.ShapeDtypeStruct(shape, WIDE) for shape in shapes],
        compiler_params=pltpu.CompilerParams(vmem_limit_bytes=VMEM_BYTES),
        cost_estimate=pl.CostEstimate(
            flops=1024 * size, bytes_accessed=38 * size, transcendentals=0
        ),
    )(*operands)
    return new[:4], new[4:]


def shard_kernel(by_kind, column, row, out):
    kinds, width = column.shape[0 if by_kind else 1], column.shape[2]
    for k in range(kinds):
        block = column[k] if by_kind else column[:, k, :]
        out[:, k * width : (k + 1) * width] = block.astype(LOW)
    out[:, kinds * width :] = row[...].T.astype(LOW)


def low_shard(column, row, by_kind):
    rows, size = row.shape[1], column.size + row.size
    return pl.pallas_call(
        lambda *refs: shard_kernel(by_kind, *refs),
        out_shape=jax.ShapeDtypeStruct((rows, size // rows), LOW),
        compiler_params=pltpu.CompilerParams(vmem_limit_bytes=VMEM_BYTES),
        cost_estimate=pl.CostEstimate(flops=0, bytes_accessed=6 * size, transcendentals=0),
    )(column, row)


def ffn_kernel(units, starts, mine, theirs, cot_mine, cot_theirs, *refs):
    act_out, grad_out, send_out, far_out, near_out, inner_out, down_out = refs[-10:-3]
    matrix, sems, sem = refs[-3:]

    def down_copy():
        return pltpu.make_async_copy(matrix.at[:, pl.ds(2 * units, units)], down_out, sem)

    @pl.when(pl.program_id(0) == 0)
    def _():
        copy_pieces(starts, refs[:-10], matrix, sems)
        down_copy().start()

    normed = jnp.concatenate([mine[...], theirs[...]], axis=1)
    cot = jnp.concatenate([cot_mine[...], cot_theirs[...]], axis=1)
    inner = jnp.zeros((normed.shape[0], 1), WIDE)
    for low in range(0, units, 256):
        high = min(low + 256, units)
        gate = jnp.dot(normed, matrix[:, low:high], preferred_element_type=WIDE)
        up = jnp.dot(normed, matrix[:, units + low : units + high], preferred_element_type=WIDE)
        grad = jnp.dot(
            cot, matrix[:, 2 * units + low : 2 * units + high], preferred_element_type=WIDE
        )
        sigmoid = 0.5 * jnp.tanh(0.5 * gate) + 0.5
        silu = gate * sigmoid
        grad_gate = grad * up * (sigmoid + silu * (1.0 - sigmoid))
        grad_up = grad * silu
        act_out[:, low:high] = (silu * up).astype(LOW)
        grad_out[:, low:high] = grad_gate.astype(LOW)
        grad_out[:, units + low : units + high] = grad_up.astype(LOW)
        inner += jnp.sum(grad_gate * gate + grad_up * up, axis=1, keepdims=True)
    inner_out[...] = jnp.broadcast_to(inner, (inner.shape[0], 128)).T[:8]
    grads = grad_out[...]

    def back(low, high):
        return lax.dot_general(
            grads, matrix[low:high, : 2 * units], (((1,), (1,)), ((), ())),
            preferred_element_type=WIDE,
        )

    send_out[...] = back(D // 2, D).astype(LOW)
    keep = back(0, D // 2)
    near_out[...] = keep[:, : D // 4]
    far_out[...] = keep[:, D // 4 :]

    @pl.when(pl.program_id(0) == pl.num_programs(0) - 1)
    def _():
        down_copy().wait()


def ffn(features, cotangents, pieces, starts):
    tokens, units, count = features[0].shape[0], pieces[0].shape[1] // 3, len(pieces)
    block = 256

    def cut(extent):
        return pl.BlockSpec((block, extent), lambda i, starts: (i, 0))

    whole = pl.BlockSpec(memory_space=pl.ANY)
    return pl.pallas_call(
        lambda *refs: ffn_kernel(units, *refs),
        grid_spec=pltpu.PrefetchScalarGridSpec(
            num_scalar_prefetch=1,
            grid=(tokens // block,),
            in_specs=[cut(D // 2)] * 4 + [whole] * count,
            out_specs=[cut(units), cut(2 * units), cut(D // 2), cut(D // 4), cut(D // 4),
                pl.BlockSpec((8, block), lambda i, starts: (0, i)), whole],
            scratch_shapes=[
                pltpu.VMEM((D, 3 * units), LOW),
                pltpu.SemaphoreType.DMA((count,)),
                pltpu.SemaphoreType.DMA,
            ],
        ),
        out_shape=[
            jax.ShapeDtypeStruct((tokens, units), LOW),
            jax.ShapeDtypeStruct((tokens, 2 * units), LOW),
            jax.ShapeDtypeStruct((tokens, D // 2), LOW),
            jax.ShapeDtypeStruct((tokens, D // 4), WIDE),
            jax.ShapeDtypeStruct((tokens, D // 4), WIDE),
            jax.ShapeDtypeStruct((8, tokens), WIDE),
            jax.ShapeDtypeStruct((D, units), LOW),
        ],
        compiler_params=pltpu.CompilerParams(vmem_limit_bytes=VMEM_BYTES),
        cost_estimate=pl.CostEstimate(
            flops=10 * tokens * D * units,
            bytes_accessed=6 * D * units + 16 * tokens * D,
            transcendentals=tokens * units,
        ),
    )(starts, *features, *cotangents, *pieces)


def parts_kernel(split, mine, theirs, cot_mine, cot_theirs, grads, activated, out):
    j, i = pl.program_id(0), pl.program_id(1)

    def product(left, right):
        out[...] = lax.dot_general(
            left[...], right[...], (((0,), (0,)), ((), ())), preferred_element_type=WIDE
        ).astype(LOW)

    for half, left, right in ((0, mine, grads), (1, theirs, grads)):

        @pl.when((j < split) & (i == half))
        def _():
            product(left, right)

    for half, left, right in ((0, cot_mine, activated), (1, cot_theirs, activated)):

        @pl.when((j == split) & (i == half))
        def _():
            product(left, right)


def gradient_parts(features, cotangents, grads, activated):
    tokens, units = activated.shape
    split = grads.shape[1] // units
    half = pl.BlockSpec((tokens, D // 2), lambda j, i: (0, 0))
    return pl.pallas_call(
        lambda *refs: parts_kernel(split, *refs),
        grid=(split + 1, 2),
        in_specs=[half] * 4
        + [
            pl.BlockSpec((tokens, units), lambda j, i: (0, jnp.minimum(j, split - 1))),
            pl.BlockSpec((tokens, units), lambda j, i: (0, 0)),
        ],
        out_specs=pl.BlockSpec((D // 2, units), lambda j, i: (i, j)),
        out_shape=jax.ShapeDtypeStruct((D, (split + 1) * units), LOW),
        compiler_params=pltpu.CompilerParams(vmem_limit_bytes=VMEM_BYTES),
        cost_estimate=pl.CostEstimate(
            flops=2 * tokens * D * (split + 1) * units,
            bytes_accessed=4 * tokens * D,
            transcendentals=0,
        ),
    )(*features, *cotangents, grads, activated)


def adam_step(values, gradient, moment_one, second):
    moment_one = BETA_ONE * moment_one + (1.0 - BETA_ONE) * gradient
    second = BETA_TWO * second + (1.0 - BETA_TWO) * gradient * gradient
    first_hat = moment_one / (1.0 - BETA_ONE**STEP)
    second_hat = second / (1.0 - BETA_TWO**STEP)
    new_values = values - VECTOR_RATE * (
        first_hat / (jnp.sqrt(second_hat) + ADAM_EPS) + WEIGHT_DECAY * values
    )
    return (moment_one, second, new_values)


def dot(one, two, dims):
    return lax.dot_general(
        one, two, ((dims[:1], dims[1:]), ((), ())), preferred_element_type=WIDE
    )


def body(
    tokens,
    doc_starts,
    cotangent,
    gains,
    conv_kernel,
    in_proj,
    gate_up,
    out_proj,
    down_proj,
    in_left,
    in_right,
    in_left_root,
    in_right_root,
    gate_left,
    gate_right,
    gate_left_root,
    gate_right_root,
    out_left,
    out_right,
    out_left_root,
    out_right_root,
    down_left,
    down_right,
    down_left_root,
    down_right_root,
    gain_first,
    gain_second,
    kernel_first,
    kernel_second,
):
    chan_in = in_proj.shape[2]
    units = gate_up.shape[2]

    in_kinds = in_proj.transpose(1, 0, 2)
    second_shard = low_shard(gate_up, down_proj, False)
    first_pieces, first_starts = ring_gather(low_shard(in_kinds, out_proj, True), second_shard)
    tokens_halves, tokens_across = spread(tokens, *first_pieces[3:5])
    tokens_full = jnp.concatenate(tokens_halves, axis=1)
    gain_full = jnp.concatenate(spread(gains[:1])[0], axis=1)
    pieces, starts_two = ring_gather(after(second_shard, *first_pieces[-4:-2]))

    cot_halves, cot_across = spread(after(cotangent, tokens_across), pieces[1])
    wide_full = tokens_full.astype(WIDE)
    inv_one = lax.rsqrt(jnp.sum(wide_full * wide_full, axis=1) / D + EPS)
    spread_one = (wide_full * inv_one[:, None] * gain_full).astype(LOW)
    resid_in = tokens.astype(WIDE)
    hat_one = resid_in * inv_one[:, None]
    first_full = placed_rows(first_pieces, first_starts)
    in_full, out_full = first_full[:, : 3 * chan_in], first_full[:, 3 * chan_in :]
    projected = dot(spread_one, in_full, (1, 0))
    in_gate = projected[:, :chan_in]
    out_gate = projected[:, chan_in : 2 * chan_in]
    conv_input = projected[:, 2 * chan_in :]
    bx_low = (in_gate * conv_input).astype(LOW)
    starts = doc_starts.astype(WIDE)
    tail_keep = 1.0 - starts[-1]
    edge_rows = jnp.concatenate([bx_low[-2:-1] * tail_keep.astype(LOW), bx_low[-1:]], axis=0)
    carried = after(from_behind(edge_rows, "seq", 1), cot_across, *pieces[1:3])
    padded = jnp.concatenate([carried, bx_low], axis=0).astype(WIDE)
    keep_one, keep_two = keep_masks(starts)
    filtered = conv_taps(padded, conv_kernel, keep_one, keep_two)
    gated_low = (out_gate * filtered).astype(LOW)
    other, sent, near = branch_parts(gated_low, out_full)
    across = after(swap(sent, "chan", 2), *pieces[3:5])
    residual = resid_in + near_sum(other, near, across)

    squares = all_sum(jnp.sum(residual * residual, axis=1), "chan")
    inv_two = lax.rsqrt(squares / D + EPS)
    hat_two = residual * inv_two[:, None]
    normed_two = (hat_two * gains[1][None, :]).astype(LOW)
    two_halves, _ = spread(normed_two, *pieces[5:7])
    activated, grad_hidden, two_send, two_far, two_near, inner_two, down_full = ffn(
        two_halves, cot_halves, pieces, starts_two
    )
    other = swap(two_send, "chan", 1)
    sent_two = sent = far_sum(other, two_far)
    inner_two = all_sum(inner_two[0], "chan")
    weights_back = jnp.stack(
        [
            conv_kernel[0] * keep_two[0] * out_gate[0],
            conv_kernel[1] * keep_one[0] * out_gate[0],
            conv_kernel[0] * keep_two[1] * out_gate[1],
        ]
    )
    weights_back = from_behind(after(weights_back, sent_two), "seq", -1)
    second_part = gradient_parts(two_halves, cot_halves, after(grad_hidden, sent, inner_two), activated)
    across = after(swap(sent, "chan", 2), second_part, inner_two, weights_back)
    grad_norm_two = near_sum(other, two_near, across)
    resid_norm, gain_two = norm_back(grad_norm_two, hat_two, inv_two, gains[1], inner_two)
    grad_resid = cotangent.astype(WIDE) + resid_norm
    mixed_send, mixed_far, mixed_near = pair_parts(after(activated, grad_resid), down_full)
    resid_halves, resid_across = spread(grad_resid.astype(LOW), mixed_send)
    resid_full = jnp.concatenate(resid_halves, axis=1)
    top_halves, _ = spread(from_behind(grad_resid[:2].astype(LOW), "seq", -1))
    top_rows = jnp.pad(jnp.concatenate(top_halves, axis=1), ((0, 6), (0, 0)))
    top_gated = dot(top_rows, out_full, (1, 0))
    grad_gated = dot(resid_full, out_full, (1, 0))
    grad_conv = grad_gated * out_gate
    grad_cpart = grad_gated * filtered
    tap_one = keep_one[:, None] * grad_conv
    tap_two = keep_two[:, None] * grad_conv
    grad_padded = (
        jnp.pad(conv_kernel[2][None, :] * grad_conv, ((2, 0), (0, 0)))
        + jnp.pad(conv_kernel[1][None, :] * tap_one, ((1, 1), (0, 0)))
        + jnp.pad(conv_kernel[0][None, :] * tap_two, ((0, 2), (0, 0)))
    )
    out_part = dot(resid_full, gated_low, (0, 0)).astype(LOW)
    returned = jnp.stack(
        [
            weights_back[0] * top_gated[0],
            weights_back[1] * top_gated[0] + weights_back[2] * top_gated[1],
        ]
    )
    edge_back = jnp.concatenate([returned[0:1] * tail_keep, returned[1:2]], axis=0)
    grad_bx = grad_padded[2:] + jnp.pad(edge_back, ((grad_conv.shape[0] - 2, 0), (0, 0)))
    grad_bx = lax.optimization_barrier(grad_bx.astype(LOW)).astype(WIDE)
    kernel_part = jnp.stack(
        [
            jnp.sum(tap_two * padded[:-2], axis=0),
            jnp.sum(tap_one * padded[1:-1], axis=0),
            jnp.sum(grad_conv * padded[2:], axis=0),
        ]
    )
    grad_proj = jnp.concatenate(
        [
            (grad_bx * conv_input).astype(LOW),
            grad_cpart.astype(LOW),
            (grad_bx * in_gate).astype(LOW),
        ],
        axis=1,
    )
    second_terms, arrived, _, _ = ring_total(after(second_part, grad_norm_two))
    other, last_sent, near = branch_parts(grad_proj, in_full)
    grad_norm_one = near_sum(other, near, swap(last_sent, "chan", 2))
    other = swap(after(mixed_send, last_sent), "chan", 1)
    sent = after(far_sum(other, mixed_far), grad_norm_one)
    mixed = (residual + near_sum(other, mixed_near, swap(sent, "chan", 2))).astype(LOW)
    inner_one = all_sum(jnp.sum(grad_proj.astype(WIDE) * projected, axis=1), "chan")
    input_norm, gain_one = norm_back(grad_norm_one, hat_one, inv_one, gains[0], inner_one)
    input_grad = grad_resid + input_norm

    in_part = dot(spread_one, grad_proj, (0, 0)).astype(LOW)
    first_part = after(jnp.concatenate([in_part, out_part], axis=1), last_sent)
    first_terms, early, _, _ = ring_total(first_part)
    second_terms = after_all(second_terms, *early)
    first_terms = after_all(first_terms, mixed)
    vector_grad = all_sum(
        jnp.concatenate([gain_one[None], gain_two[None], kernel_part], axis=0), "seq"
    )
    gain_grad, kernel_grad = vector_grad[:2], vector_grad[2:]

    (gate_grad, gate_new, gate_left_new, gate_right_new), down_outs = both_updates(
        column_tiles(
            gate_up, second_terms, 0, 3, False, gate_left, gate_right, gate_left_root,
            gate_right_root,
        ),
        row_tiles(
            down_proj, second_terms, 2 * units, 3, down_left, down_right, down_left_root,
            down_right_root,
        ),
    )
    down_grad, down_new, down_left_new, down_right_new = down_outs
    (in_grad, in_new, in_left_new, in_right_new), out_outs = both_updates(
        column_tiles(
            in_kinds, first_terms, 0, 1, True, in_left, in_right, in_left_root, in_right_root
        ),
        row_tiles(
            out_proj, first_terms, 3 * chan_in, 1, out_left, out_right, out_left_root,
            out_right_root,
        ),
    )
    out_grad, out_new, out_left_new, out_right_new = out_outs
    in_grad, in_new = in_grad.transpose(1, 0, 2), in_new.transpose(1, 0, 2)
    gain_one_new, gain_two_new, gains_new = adam_step(gains, gain_grad, gain_first, gain_second)
    kernel_one_new, kernel_two_new, kernel_new = adam_step(
        conv_kernel, kernel_grad, kernel_first, kernel_second
    )
    return (
        mixed,
        input_grad,
        in_grad,
        gate_grad,
        out_grad,
        down_grad,
        in_new,
        gate_new,
        out_new,
        down_new,
        in_left_new,
        in_right_new,
        gate_left_new,
        gate_right_new,
        out_left_new,
        out_right_new,
        down_left_new,
        down_right_new,
        gain_one_new,
        gain_two_new,
        gains_new,
        kernel_one_new,
        kernel_two_new,
        kernel_new,
    )


def solution(mesh):
    placed = (
        P("seq", "chan"),
        P("seq"),
        P("seq", "chan"),
        P(None, "chan"),
        P(None, "chan"),
        P("seq", None, "chan"),
        P("seq", None, "chan"),
        P("chan", "seq"),
        P("chan", "seq"),
        P("seq", None, "chan", None, None),
        P("seq", None, "chan", None, None),
        P("seq", None, "chan", None, None),
        P("seq", None, "chan", None, None),
        P("seq", None, "chan", None, None),
        P("seq", None, "chan", None, None),
        P("seq", None, "chan", None, None),
        P("seq", None, "chan", None, None),
        P("chan", "seq", None, None),
        P("chan", "seq", None, None),
        P("chan", "seq", None, None),
        P("chan", "seq", None, None),
        P("chan", "seq", None, None),
        P("chan", "seq", None, None),
        P("chan", "seq", None, None),
        P("chan", "seq", None, None),
        P(None, "chan"),
        P(None, "chan"),
        P(None, "chan"),
        P(None, "chan"),
    )
    return jax.shard_map(
        body,
        mesh=mesh,
        in_specs=placed,
        out_specs=(
            P("seq", "chan"),
            P("seq", "chan"),
            P("seq", None, "chan"),
            P("seq", None, "chan"),
            P("chan", "seq"),
            P("chan", "seq"),
            P("seq", None, "chan"),
            P("seq", None, "chan"),
            P("chan", "seq"),
            P("chan", "seq"),
            P("seq", None, "chan", None, None),
            P("seq", None, "chan", None, None),
            P("seq", None, "chan", None, None),
            P("seq", None, "chan", None, None),
            P("chan", "seq", None, None),
            P("chan", "seq", None, None),
            P("chan", "seq", None, None),
            P("chan", "seq", None, None),
            P(None, "chan"),
            P(None, "chan"),
            P(None, "chan"),
            P(None, "chan"),
            P(None, "chan"),
            P(None, "chan"),
        ),
        check_vma=False,
    )
```
